512 devices in a mesh: dp: 64 (over x, z, core), tensor: 8 (over y).
Axes of the slice: x: 4, y: 8, z: 8, core: 2. Of those that a mesh axis runs over, the one named last changes fastest.
Arguments:
- finish: int32 [128], P('dp'), may hold values from 0 to 3, as said below
- source: int32 [128], P('dp'), may hold values from 0 to 255, as said below
- ssm_state: float32 [128, 128, 64, 128], P('dp', 'tensor'), may hold values from -6 to 6
- conv_x: bfloat16 [128, 3, 8192], P('dp', None, 'tensor'), may hold values from -6 to 6
- conv_bc: bfloat16 [128, 3, 2, 1024], P('dp', None, None, 'tensor'), may hold values from -6 to 6
- prompt_ssm: bfloat16 [256, 128, 64, 128], P('dp', 'tensor'), may hold values from -6 to 6
- prompt_conv_x: bfloat16 [256, 3, 8192], P('dp', None, 'tensor'), may hold values from -6 to 6
- prompt_conv_bc: bfloat16 [256, 3, 2, 1024], P('dp', None, None, 'tensor'), may hold values from -6 to 6
- x_in: bfloat16 [3, 128, 8192], P(None, 'dp', 'tensor'), may hold values from -6 to 6
- z_in: bfloat16 [3, 128, 8192], P(None, 'dp', 'tensor'), may hold values from -6 to 6
- bc_in: bfloat16 [3, 128, 2, 1024], P(None, 'dp', None, 'tensor'), may hold values from -6 to 6
- dt_in: float32 [3, 128, 128], P(None, 'dp', 'tensor'), may hold values from -6 to 6
- conv_w: float32 [4, 8192], P(None, 'tensor'), may hold values from -3 to 3
- conv_wbc: float32 [4, 2, 1024], P(None, None, 'tensor'), may hold values from -3 to 3
- dt_bias: float32 [128], P('tensor'), may hold values from -4 to -1
- a_log: float32 [128], P('tensor'), may hold values from -1 to 1.5
- skip_d: float32 [128], P('tensor'), may hold values from 0.5 to 1.5
- norm_gain: float32 [8192], P('tensor'), may hold values from 0.5 to 1.5
Outputs:
- outputs: bfloat16 [3, 128, 8192], P(None, 'dp', 'tensor')
- final_state: float32 [128, 128, 64, 128], P('dp', 'tensor')
The draws below stay inside these ranges and needn't reach their ends.
Inputs may be any that keep to these rules, and one draw needn't show every extreme that they name: `source`: exactly 1 slot of each dp index is refilled (finish below 3); dp indices g that share g // 16 name the same prompt for their refilled slots and others different ones, so each forked prompt refills 16 slots; slots that are not refilled may name any prompt. `finish`: slots that are not refilled have 3.
All inputs are finite; a program needn't handle non-finite values.
Results may differ from the reference program's by a relative error of at most 0.0013.
Values may be sent and summed in bfloat16 or wider, within the bound.
A program may use at most 64 MiB of HBM per device.

```python
import jax
import jax.numpy as jnp
from jax import lax

H = 128
P_SIZE = 64
N = 128
G = 8
K = 4
STEPS = 3
FORK = 16
SLOTS_DEV = 2
REF_DEV = 1
SLOTS = 128
PROMPTS = 256


def fork_plan(key):
    groups = SLOTS // SLOTS_DEV
    span = FORK // REF_DEV
    first, second, third, fourth = jax.random.split(key, 4)
    scores = jax.random.randint(first, (groups, SLOTS_DEV), 0, 2 ** 20) * SLOTS_DEV + jnp.arange(SLOTS_DEV)
    placing = jnp.argsort(scores, axis=1)
    ranking = jnp.argsort(placing, axis=1)
    refilled = ranking < REF_DEV
    chosen = jax.random.permutation(second, PROMPTS)[:groups // span]
    group_prompt = jnp.repeat(chosen, span)
    moments = jax.random.randint(third, (groups, SLOTS_DEV), 0, STEPS)
    others = jax.random.randint(fourth, (groups, SLOTS_DEV), 0, PROMPTS)
    finish = jnp.where(refilled, moments, STEPS).reshape(-1).astype(jnp.int32)
    source = jnp.where(refilled, group_prompt[:, None], others).reshape(-1).astype(jnp.int32)
    return (finish, source)


def draw_finish(key, part):
    return fork_plan(key)[0]


def draw_source(key, part):
    return fork_plan(key)[1]


def level_of(own_key, shape, shards, smallest, largest):
    factor_of, own = 1.0, jax.random.fold_in(own_key, 6)
    for axis_at, parts in shards:
        steps = jnp.exp(jax.random.uniform(jax.random.fold_in(own, axis_at), (parts,), jnp.float32, smallest / len(shards), largest / len(shards)))
        factor_of = factor_of * jnp.repeat(steps, shape[axis_at] // parts).reshape([-1 if axis == axis_at else 1 for axis in range(len(shape))])
    return factor_of


def gaussian(key, extent, deviation, most, cuts=(), kind=jnp.bfloat16):
    entries = jax.random.normal(key, extent, jnp.float32) * deviation
    if len(cuts) > 0:
        entries = level_of(key, extent, cuts, -0.22, 0.18) * entries
    return jnp.clip(entries, min=-most, max=most).astype(kind)


def setup_inputs(seed: int = 0) -> dict:
    arg_keys = jax.random.split(jax.random.key(seed), 19)
    return {
        "finish": draw_finish(jax.random.fold_in(arg_keys[18], 71), 0),
        "source": draw_source(jax.random.fold_in(arg_keys[18], 71), 0),
        "ssm_state": gaussian(arg_keys[2], (SLOTS, H, P_SIZE, N), 1.0, 6.0, ((0, 64), (1, 8)), jnp.float32),
        "conv_x": gaussian(arg_keys[3], (SLOTS, K - 1, H * P_SIZE), 1.0, 6.0, ((0, 64), (2, 8))),
        "conv_bc": gaussian(arg_keys[4], (SLOTS, K - 1, 2, G * N), 1.0, 6.0, ((0, 64), (3, 8))),
        "prompt_ssm": gaussian(arg_keys[5], (PROMPTS, H, P_SIZE, N), 1.0, 6.0, ((0, 64), (1, 8))),
        "prompt_conv_x": gaussian(arg_keys[6], (PROMPTS, K - 1, H * P_SIZE), 1.0, 6.0, ((0, 64), (2, 8))),
        "prompt_conv_bc": gaussian(arg_keys[7], (PROMPTS, K - 1, 2, G * N), 1.0, 6.0, ((0, 64), (3, 8))),
        "x_in": gaussian(arg_keys[8], (STEPS, SLOTS, H * P_SIZE), 1.0, 6.0, ((1, 64), (2, 8))),
        "z_in": gaussian(arg_keys[9], (STEPS, SLOTS, H * P_SIZE), 1.0, 6.0, ((1, 64), (2, 8))),
        "bc_in": gaussian(arg_keys[10], (STEPS, SLOTS, 2, G * N), 1.0, 6.0, ((1, 64), (3, 8))),
        "dt_in": gaussian(arg_keys[11], (STEPS, SLOTS, H), 1.0, 6.0, ((1, 64), (2, 8)), jnp.float32),
        "conv_w": gaussian(arg_keys[12], (K, H * P_SIZE), K ** -0.5, 3.0, ((1, 8),), jnp.float32),
        "conv_wbc": gaussian(arg_keys[13], (K, 2, G * N), K ** -0.5, 3.0, ((2, 8),), jnp.float32),
        "dt_bias": jnp.clip(-4.0 + 3.0 * jax.random.uniform(arg_keys[14], (H,), jnp.float32) ** level_of(arg_keys[14], (H,), ((0, 8),), -0.2, 0.2), -4.0, -1.0),
        "a_log": jnp.clip(-1.0 + 2.5 * jax.random.uniform(arg_keys[15], (H,), jnp.float32) ** level_of(arg_keys[15], (H,), ((0, 8),), -0.2, 0.2), -1.0, 1.5),
        "skip_d": jnp.clip(0.5 + 1.0 * jax.random.uniform(arg_keys[16], (H,), jnp.float32) ** level_of(arg_keys[16], (H,), ((0, 8),), -0.2, 0.2), 0.5, 1.5),
        "norm_gain": jnp.clip(1.0 + 0.1 * jax.random.normal(arg_keys[17], (H * P_SIZE,), jnp.float32), 0.5, 1.5),
    }


def reference(finish, source, ssm_state, conv_x, conv_bc, prompt_ssm, prompt_conv_x, prompt_conv_bc, x_in, z_in, bc_in, dt_in, conv_w, conv_wbc, dt_bias, a_log, skip_d, norm_gain):

    def one_slot(items):
        fin, src, state, win_x_old, win_bc_old, x_rows, z_rows, bc_rows, dt_rows = items
        fork_state = prompt_ssm[src].astype(jnp.float32)
        fork_x = prompt_conv_x[src]
        fork_bc = prompt_conv_bc[src]
        results = []
        for moment in range(STEPS):
            refill = fin == moment
            state = jnp.where(refill, fork_state, state)
            win_x_old = jnp.where(refill, fork_x, win_x_old)
            win_bc_old = jnp.where(refill, fork_bc, win_bc_old)
            window_x = jnp.concatenate([win_x_old, x_rows[moment][None]], axis=0)
            conv_out = jax.nn.silu(lax.optimization_barrier(jnp.sum(conv_w * window_x.astype(jnp.float32), axis=0)))
            win_x_old = window_x[1:]
            window_bc = jnp.concatenate([win_bc_old, bc_rows[moment][None]], axis=0)
            bc_out = jax.nn.silu(lax.optimization_barrier(jnp.sum(conv_wbc * window_bc.astype(jnp.float32), axis=0)))
            win_bc_old = window_bc[1:]
            step_size = jax.nn.softplus(dt_rows[moment] + dt_bias)
            decay = jnp.exp(-jnp.exp(a_log) * step_size)
            heads_x = conv_out.reshape(H, P_SIZE)
            b_heads = jnp.repeat(bc_out[0].reshape(G, N), H // G, axis=0)
            c_heads = jnp.repeat(bc_out[1].reshape(G, N), H // G, axis=0)
            state = decay[:, None, None] * state + (step_size[:, None] * heads_x)[:, :, None] * b_heads[:, None, :]
            y_heads = jnp.einsum('hpn,hn->hp', state, c_heads, precision=lax.Precision.HIGHEST) + skip_d[:, None] * heads_x
            gated = y_heads.reshape(-1) * jax.nn.silu(z_rows[moment].astype(jnp.float32))
            normed = gated * lax.rsqrt(jnp.mean(gated * gated) + 1e-05) * norm_gain
            results.append(normed.astype(jnp.bfloat16))
        return (jnp.stack(results), state)
    outputs, final_state = lax.map(one_slot, (finish, source, ssm_state, conv_x, conv_bc, jnp.swapaxes(x_in, 0, 1), jnp.swapaxes(z_in, 0, 1), jnp.swapaxes(bc_in, 0, 1), jnp.swapaxes(dt_in, 0, 1)))
    return (jnp.swapaxes(outputs, 0, 1), final_state)
```

```python
import functools

import jax
import jax.numpy as jnp
from jax import lax
from jax.experimental import pallas as pl
from jax.experimental.pallas import tpu as pltpu
from jax.sharding import PartitionSpec as P

F32 = jnp.float32
BF16 = jnp.bfloat16
MESH = pl.DeviceIdType.MESH
HIGHEST = lax.Precision.HIGHEST

NZ = 8
HELD = 4
HEADS = 16
HALF = 8
WIDTH = 64
STATES = 128
CH = HEADS * WIDTH
LANES = CH + 2 * STATES
STEPS = 3
TAPS = 4
ROWS = 8
TOTAL = 8192
STAGES = ((4, 5), (3, 6), (2, 7), (1, 0))
NEAR = (1, 7, 2, 6, 3, 5, 4)


def silu(v):
    return v * (1.0 / (1.0 + jnp.exp(-v)))


def softplus(v):
    return jnp.maximum(v, 0.0) + jnp.log1p(jnp.exp(-jnp.abs(v)))


def nt(a, b, precision=None):
    return lax.dot_general(
        a, b, (((1,), (1,)), ((), ())), precision=precision, preferred_element_type=F32
    )


def tn(a, b, precision=None):
    return lax.dot_general(
        a, b, (((0,), (0,)), ((), ())), precision=precision, preferred_element_type=F32
    )


def kernel(
    nx,
    ny,
    fin_ref,
    src_ref,
    ssm_hbm,
    cx_hbm,
    cbc_hbm,
    pssm_hbm,
    pcx_hbm,
    pcbc_hbm,
    x_hbm,
    z_hbm,
    bc_hbm,
    dt_hbm,
    cw_hbm,
    cwbc_hbm,
    bias_hbm,
    alog_hbm,
    skip_hbm,
    gain_hbm,
    out_ref,
    fs_hbm,
    ssm,
    cx,
    cbc,
    pcx,
    pcbc,
    xin,
    zin,
    bcin,
    dtin,
    cw,
    cwbc,
    bias,
    alog,
    skip,
    gain,
    plan_out,
    plan_in,
    pbuf,
    pconv,
    cpack,
    csend,
    cxbuf,
    czsend,
    czbuf,
    sbuf,
    xb0,
    xb1,
    xb2,
    xb3,
    zsend,
    zbuf,
    fbuf,
    ysend,
    ybuf,
    seq,
    fork,
    acc,
    wts,
    st,
    ex,
    dec,
    base,
    bco,
    gub,
    ab,
    in_sem,
    own_sem,
    out_sem,
    plan_s,
    plan_r,
    pair_s,
    pair_r,
    cx_s,
    cx_r,
    cz_s,
    cz_r,
    x_s,
    x_r,
    z_s,
    z_r,
    g_s,
    g_r,
    f_s,
    f_r,
    y_s,
    y_r,
):
    me = lax.axis_index("dp")
    c = lax.rem(me, 2)
    z = lax.rem(me // 2, NZ)
    x = me // (2 * NZ)
    y = lax.axis_index("tensor")
    xbs = (xb0, xb1, xb2, xb3)

    def at(xx, zz, cc):
        return {"dp": (xx * NZ + zz) * 2 + cc}

    def xpeer(d):
        return lax.rem(x + d, nx)

    def zpeer(d):
        return lax.rem(z + d, NZ)

    def ypeer(d):
        return lax.rem(y + d, ny)

    sibling = at(x, z, 1 - c)

    def remote(src, dst, ssem, rsem, dev):
        return pltpu.make_async_remote_copy(
            src_ref=src, dst_ref=dst, send_sem=ssem, recv_sem=rsem, device_id=dev, device_id_type=MESH
        )

    mine = pl.ds(pl.multiple_of(c * HALF, HALF), HALF)
    theirs = pl.ds(pl.multiple_of((1 - c) * HALF, HALF), HALF)
    my_slot = pl.ds(pl.multiple_of(c * HELD, HELD), HELD)
    loads = [
        pltpu.make_async_copy(src, dst, in_sem.at[i])
        for i, (src, dst) in enumerate(
            (
                (pcx_hbm, pcx),
                (pcbc_hbm, pcbc),
                (dt_hbm, dtin),
                (bias_hbm, bias),
                (alog_hbm, alog),
                (skip_hbm, skip),
                (cx_hbm, cx),
                (cbc_hbm, cbc),
                (x_hbm, xin),
                (bc_hbm, bcin),
                (cw_hbm, cw),
                (cwbc_hbm, cwbc),
                (z_hbm, zin),
                (gain_hbm, gain),
                (ssm_hbm, ssm),
            )
        )
    ]
    own = pltpu.make_async_copy(pssm_hbm.at[:, mine], pbuf.at[my_slot], own_sem)

    barrier = pltpu.get_barrier_semaphore()
    pl.semaphore_signal(barrier, inc=1, device_id=sibling, device_id_type=MESH)
    for d in range(1, nx):
        pl.semaphore_signal(barrier, inc=1, device_id=at(xpeer(d), z, c), device_id_type=MESH)
    for d in range(1, NZ):
        pl.semaphore_signal(barrier, inc=1, device_id=at(x, zpeer(d), c), device_id_type=MESH)
    for d in range(1, ny):
        pl.semaphore_signal(barrier, inc=1, device_id={"tensor": ypeer(d)}, device_id_type=MESH)
    own.start()
    for cp in loads:
        cp.start()

    fin0, fin1 = fin_ref[0], fin_ref[1]
    prompt = jnp.where(fin0 < STEPS, src_ref[0], src_ref[1])
    plan_out[...] = jnp.full(plan_out.shape, prompt, jnp.int32)
    wts[...] = jnp.zeros_like(wts)
    st[...] = jnp.zeros_like(st)
    acc[...] = jnp.zeros_like(acc)
    base[...] = jnp.zeros_like(base)
    bco[...] = jnp.zeros_like(bco)
    gub[...] = jnp.zeros_like(gub)
    cpack[...] = jnp.zeros_like(cpack)

    pl.semaphore_wait(barrier, 1 + (nx - 1) + (NZ - 1) + (ny - 1))

    plans = {}
    for d in range(1, nx):
        plans[d] = remote(
            plan_out, plan_in.at[d], plan_s.at[d], plan_r.at[d], at(xpeer(d), z, c)
        )
        plans[d].start()
    pair = remote(pssm_hbm.at[:, theirs], pbuf.at[my_slot], pair_s.at[0], pair_r.at[0], sibling)
    pair.start()

    loads[0].wait()
    loads[1].wait()
    for i in range(3):
        tap = pcx[i].astype(F32)
        for q in range(HELD):
            for k in range(8):
                r = 4 * k + i
                cpack[q, r : r + 1, :] = tap[q : q + 1, 128 * k : 128 * (k + 1)]
    for q in range(HELD):
        for i in range(3):
            for b in range(2):
                r = 4 * (2 * i + b) + 3
                cpack[q, r : r + 1, :] = pcbc[q, i, b : b + 1, :].astype(F32)
    pconv[my_slot] = cpack[...].astype(BF16)
    pair_conv = remote(
        pconv.at[my_slot], pconv.at[my_slot], pair_s.at[1], pair_r.at[1], sibling
    )
    pair_conv.start()

    for i in range(2, 6):
        loads[i].wait()
    for t in range(STEPS):
        st[2 * t : 2 * t + 2, :HEADS] = dtin[t]
    st[6:7, :HEADS] = bias[...]
    st[7:8, :HEADS] = alog[...]
    st[8:9, :HEADS] = skip[...]
    small = st[:, :HEADS]
    spread = (
        lax.broadcasted_iota(jnp.int32, (HEADS, CH), 1) // WIDTH
        == lax.broadcasted_iota(jnp.int32, (HEADS, CH), 0)
    ).astype(F32)
    ex[...] = lax.dot_general(
        small, spread, (((1,), (0,)), ((), ())), precision=HIGHEST, preferred_element_type=F32
    )

    for d in range(1, nx):
        plans[d].wait_recv()
    pair.wait_recv()
    pair_conv.wait_recv()
    own.wait()

    def wanted(d):
        return lax.rem(jnp.max(plan_in[nx - d]), 2 * HELD)

    order = (2, 1, 3) if nx == 4 else tuple(range(1, nx))
    want = {d: wanted(d) for d in order}
    want[0] = lax.rem(prompt, 2 * HELD)
    owner_x = prompt // (2 * HELD * NZ)
    owner_z = lax.rem(prompt // (2 * HELD), NZ)

    conv_sends = []
    for i, d in enumerate(order):
        csend[i] = pconv[want[d]]
        cp = remote(csend.at[i], cxbuf.at[x], cx_s.at[d], cx_r.at[d], at(xpeer(d), z, c))
        cp.start()
        conv_sends.append(cp)
    cxbuf[x] = pconv[want[0]]
    x_sends = []
    for g, offsets in enumerate(STAGES):
        sends = []
        for i, d in enumerate(order):
            for n, o in enumerate(offsets):
                sbuf[i, g, n] = pbuf[want[d], zpeer(o)]
            cp = remote(
                sbuf.at[i, g], xbs[g].at[x], x_s.at[g, d], x_r.at[g, d], at(xpeer(d), z, c)
            )
            cp.start()
            sends.append(cp)
        for n, o in enumerate(offsets):
            xbs[g][x, n] = pbuf[want[0], zpeer(o)]
        x_sends.append(sends)

    for i in range(6, 12):
        loads[i].wait()
    for i in range(3):
        seq[i, :, :CH] = cx[i].astype(F32)
        for s in range(2):
            for b in range(2):
                lo = CH + b * STATES
                seq[i, s : s + 1, lo : lo + STATES] = cbc[s, i, b : b + 1, :].astype(F32)
    for t in range(STEPS):
        seq[3 + t, :, :CH] = xin[t].astype(F32)
        for s in range(2):
            for b in range(2):
                lo = CH + b * STATES
                seq[3 + t, s : s + 1, lo : lo + STATES] = bcin[t, s, b : b + 1, :].astype(F32)
    wts[:TAPS, :CH] = cw[...]
    for k in range(TAPS):
        for b in range(2):
            lo = CH + b * STATES
            wts[k : k + 1, lo : lo + STATES] = cwbc[k, b : b + 1, :]

    for cp in conv_sends:
        cp.wait_recv()
    picked = cxbuf[owner_x]
    czsend[...] = picked
    czbuf[z] = picked
    cz_sends = []
    for d in range(1, NZ):
        cp = remote(czsend, czbuf.at[z], cz_s.at[d], cz_r.at[d], at(x, zpeer(d), c))
        cp.start()
        cz_sends.append(cp)

    for t in range(STEPS):
        total = jnp.zeros((2, STATES), F32)
        for k in range(TAPS):
            total += wts[k : k + 1, CH + STATES :] * seq[t + k, :, CH + STATES :]
        acc[2 * t : 2 * t + 2, CH + STATES :] = total
    c_old = silu(acc[:, CH + STATES :])
    loads[14].wait()
    row = lax.broadcasted_iota(jnp.int32, (ROWS, CH), 0)
    y_old = jnp.where(
        lax.rem(row, 2) == 0,
        nt(c_old, ssm[0].reshape(CH, STATES), HIGHEST),
        nt(c_old, ssm[1].reshape(CH, STATES), HIGHEST),
    )
    base[...] = y_old

    z_sends = {}
    for g, offsets in enumerate(STAGES):
        for cp in x_sends[g]:
            cp.wait_recv()
        for n, o in enumerate(offsets):
            head = xbs[g][owner_x, n]
            if o == 0:
                zbuf[z] = head
            else:
                zsend[o] = head
                z_sends[o] = remote(
                    zsend.at[o], zbuf.at[z], z_s.at[o], z_r.at[o], at(x, zpeer(o), c)
                )
                z_sends[o].start()
        if g == 0:
            for cp in cz_sends:
                cp.wait_recv()
            packed = czbuf[owner_z].astype(F32)
            for k in range(8):
                fork[0:3, 128 * k : 128 * (k + 1)] = packed[4 * k : 4 * k + 3]
            for i in range(3):
                for b in range(2):
                    r = 4 * (2 * i + b) + 3
                    lo = CH + b * STATES
                    fork[i : i + 1, lo : lo + STATES] = packed[r : r + 1]
            first = lax.broadcasted_iota(jnp.int32, (2, LANES), 0) == 0
            fin_rows = jnp.where(first, fin0, fin1)
            for t in range(STEPS):
                total = jnp.zeros((2, LANES), F32)
                for k in range(TAPS):
                    w = seq[t + k]
                    for f in range(t + 1):
                        if t + k - f <= 2:
                            r = t + k - f
                            w = jnp.where(fin_rows == f, fork[r : r + 1, :], w)
                    total += wts[k : k + 1, :] * w
                acc[2 * t : 2 * t + 2, :] = total
            acc[...] = silu(acc[...])
        if g == 1:
            step = softplus(ex[0:ROWS] + ex[6:7])
            dec[...] = jnp.exp(-jnp.exp(ex[7:8]) * step)
            ex[0:6] = step[0:6]
            fin_ch = fin_rows[:, :CH]
            a = jnp.ones((2, CH), F32)
            b = jnp.zeros((2, CH), F32)
            gs = []
            for t in range(STEPS):
                two = slice(2 * t, 2 * t + 2)
                now = fin_ch == t
                d_t = dec[two]
                a = jnp.where(now, 0.0, a) * d_t
                b = jnp.where(now, 1.0, b) * d_t
                u = ex[two] * acc[two, :CH]
                gs = [jnp.where(now, 0.0, v) * d_t for v in gs] + [u]
                c_t = acc[two, CH + STATES :]
                total = a * base[two] + ex[8:9] * acc[two, :CH]
                for k in range(t + 1):
                    b_k = acc[2 * k : 2 * k + 2, CH : CH + STATES]
                    total += gs[k] * jnp.sum(b_k * c_t, axis=1, keepdims=True)
                base[two] = total
                bco[two] = b
            for k in range(STEPS):
                gub[2 * k : 2 * k + 2] = gs[k]
        if g == 2:
            pick = (
                lax.broadcasted_iota(jnp.int32, (16, 9 * STATES), 1) // STATES
                == lax.broadcasted_iota(jnp.int32, (16, 9 * STATES), 0)
            ).astype(F32)
            hb = tn(st[:, :HEADS], pick, HIGHEST)

            def col(r):
                return hb[:, r * STATES : (r + 1) * STATES]

            rate = -jnp.exp(col(7))
            for s, fin in enumerate((fin0, fin1)):
                a = jnp.ones((HEADS, STATES), F32)
                b = jnp.zeros((HEADS, STATES), F32)
                fin_v = jnp.full((HEADS, STATES), fin, jnp.int32)
                for t in range(STEPS):
                    d_t = jnp.exp(rate * softplus(col(2 * t + s) + col(6)))
                    a = jnp.where(fin_v == t, 0.0, a) * d_t
                    b = jnp.where(fin_v == t, 1.0, b) * d_t
                ab[0, s] = a
                ab[1, s] = b
            bm = acc[:, CH : CH + STATES]
            odd = lax.rem(lax.broadcasted_iota(jnp.int32, (ROWS, STATES), 0), 2)
            both = jnp.concatenate(
                [jnp.where(odd == 0, bm, 0.0), jnp.where(odd == 1, bm, 0.0)], axis=1
            )
            for h in range(0, HEADS, 4):
                lo = h * WIDTH
                u = tn(gub[:, lo : lo + 4 * WIDTH], both, HIGHEST)
                for j in range(4):
                    for s in range(2):
                        ssm[s, h + j] = (
                            ab[0, s, h + j : h + j + 1, :] * ssm[s, h + j]
                            + u[j * WIDTH : (j + 1) * WIDTH, s * STATES : (s + 1) * STATES]
                        )

    for i in (12, 13):
        loads[i].wait()
    cs = acc[:, CH + STATES :]
    hi = cs.astype(BF16)
    rest = cs - hi.astype(F32)
    mid = rest.astype(BF16)
    low = (rest - mid.astype(F32)).astype(BF16)
    parts = jnp.concatenate(
        [hi.astype(F32), mid.astype(F32), low.astype(F32), jnp.zeros_like(cs)], axis=0
    ).astype(BF16)

    for o in (4, 3, 5, 2, 6, 1, 7):
        z_sends[o].wait_recv()
    here = c * HALF + z
    fbuf[here] = zbuf[owner_z]
    g_sends, f_sends = {}, {}
    for d in (4, 3, 5, 2, 6, 1, 7):
        g_sends[d] = remote(
            fbuf.at[here], fbuf.at[here], g_s.at[d], g_r.at[d], at(x, zpeer(d), c)
        )
        g_sends[d].start()
    f_sends[0] = remote(fbuf.at[here], fbuf.at[here], f_s.at[0], f_r.at[0], sibling)
    f_sends[0].start()
    for d in NEAR:
        g_sends[d].wait_recv()
        landed = c * HALF + zpeer(NZ - d)
        f_sends[d] = remote(fbuf.at[landed], fbuf.at[landed], f_s.at[d], f_r.at[d], sibling)
        f_sends[d].start()
    for d in (0,) + NEAR:
        f_sends[d].wait_recv()

    y_parts = nt(parts, fbuf[...].reshape(CH, STATES))
    y_fork = y_parts[0:8] + y_parts[8:16] + y_parts[16:24]
    gated = base[...] + bco[...] * y_fork
    for t in range(STEPS):
        two = slice(2 * t, 2 * t + 2)
        bco[two] = silu(zin[t].astype(F32))
    gated = gated * bco[...]
    ysend[...] = jnp.broadcast_to(jnp.sum(gated * gated, axis=1, keepdims=True), ysend.shape)
    ybuf[y] = ysend[...]
    y_sends = []
    for d in range(1, ny):
        cp = remote(ysend, ybuf.at[y], y_s.at[d], y_r.at[d], {"tensor": ypeer(d)})
        cp.start()
        y_sends.append(cp)

    stores = []
    for h in range(HEADS):
        f = fbuf[h].astype(F32)
        for s in range(2):
            ssm[s, h] = ssm[s, h] + ab[1, s, h : h + 1, :] * f
        if h % 4 == 3:
            for s in range(2):
                cp = pltpu.make_async_copy(
                    ssm.at[s, h - 3 : h + 1], fs_hbm.at[s, h - 3 : h + 1], out_sem.at[s, h // 4]
                )
                cp.start()
                stores.append(cp)

    for cp in y_sends:
        cp.wait_recv()
    total = ybuf[0]
    for i in range(1, ny):
        total += ybuf[i]
    scale = lax.rsqrt(total[:, 0:1] / TOTAL + 1e-05)
    normed = gated * scale * gain[...]
    for t in range(STEPS):
        out_ref[t] = normed[2 * t : 2 * t + 2].astype(BF16)

    for cp in list(plans.values()) + [pair, pair_conv] + conv_sends + cz_sends + y_sends:
        cp.wait_send()
    for sends in x_sends:
        for cp in sends:
            cp.wait_send()
    for group in (z_sends, g_sends, f_sends):
        for cp in group.values():
            cp.wait_send()
    for cp in stores:
        cp.wait()


def body(nx, ny, *args):
    args = list(args)
    args[3] = jnp.swapaxes(args[3], 0, 1)
    args[6] = jnp.swapaxes(args[6], 0, 1)
    for i in (14, 15, 16, 17):
        args[i] = args[i].reshape(1, -1)
    dma = pltpu.SemaphoreType.DMA
    vmem = pltpu.VMEM
    in_vmem = [args[i] for i in (2, 3, 4, 6, 7, 8, 9, 10, 11, 12, 13, 14, 15, 16, 17)]
    head = (WIDTH, STATES)
    scratch = [vmem(a.shape, a.dtype) for a in in_vmem]
    scratch += [
        vmem((8, 128), jnp.int32),
        vmem((nx, 8, 128), jnp.int32),
        vmem((2 * HELD, HALF) + head, BF16),
        vmem((2 * HELD, 32, 128), BF16),
        vmem((HELD, 32, 128), F32),
        vmem((nx, 32, 128), BF16),
        vmem((nx, 32, 128), BF16),
        vmem((32, 128), BF16),
        vmem((NZ, 32, 128), BF16),
        vmem((nx, 4, 2) + head, BF16),
    ]
    scratch += [vmem((nx, 2) + head, BF16) for _ in range(4)]
    scratch += [
        vmem((NZ,) + head, BF16),
        vmem((NZ,) + head, BF16),
        vmem((HEADS,) + head, BF16),
        vmem((8, 128), F32),
        vmem((ny, 8, 128), F32),
        vmem((6, 2, LANES), F32),
        vmem((8, LANES), F32),
        vmem((ROWS, LANES), F32),
        vmem((8, LANES), F32),
        vmem((16, 128), F32),
        vmem((16, CH), F32),
        vmem((ROWS, CH), F32),
        vmem((ROWS, CH), F32),
        vmem((ROWS, CH), F32),
        vmem((ROWS, CH), F32),
        vmem((2, 2, HEADS, STATES), F32),
        dma((len(in_vmem),)),
        dma,
        dma((2, 4)),
        dma((nx,)),
        dma((nx,)),
        dma((2,)),
        dma((2,)),
        dma((nx,)),
        dma((nx,)),
        dma((NZ,)),
        dma((NZ,)),
        dma((4, nx)),
        dma((4, nx)),
        dma((NZ,)),
        dma((NZ,)),
        dma((NZ,)),
        dma((NZ,)),
        dma((NZ,)),
        dma((NZ,)),
        dma((ny,)),
        dma((ny,)),
    ]
    anywhere = pl.BlockSpec(memory_space=pl.ANY)
    scalars = pl.BlockSpec(memory_space=pltpu.SMEM)
    slots = args[0].shape[0]
    return pl.pallas_call(
        functools.partial(kernel, nx, ny),
        out_shape=(
            jax.ShapeDtypeStruct((STEPS, slots, CH), BF16),
            jax.ShapeDtypeStruct(args[2].shape, F32),
        ),
        in_specs=[scalars, scalars] + [anywhere] * 16,
        out_specs=(pl.BlockSpec(memory_space=pltpu.VMEM), anywhere),
        scratch_shapes=scratch,
        compiler_params=pltpu.CompilerParams(
            collective_id=0, has_side_effects=True, vmem_limit_bytes=60 * 1024 * 1024
        ),
    )(*args)


def solution(mesh):
    nx = mesh.shape["dp"] // (2 * NZ)
    ny = mesh.shape["tensor"]
    return jax.shard_map(
        functools.partial(body, nx, ny),
        mesh=mesh,
        in_specs=(
            P("dp"),
            P("dp"),
            P("dp", "tensor", None, None),
            P("dp", None, "tensor"),
            P("dp", None, None, "tensor"),
            P("dp", "tensor", None, None),
            P("dp", None, "tensor"),
            P("dp", None, None, "tensor"),
            P(None, "dp", "tensor"),
            P(None, "dp", "tensor"),
            P(None, "dp", None, "tensor"),
            P(None, "dp", "tensor"),
            P(None, "tensor"),
            P(None, None, "tensor"),
            P("tensor"),
            P("tensor"),
            P("tensor"),
            P("tensor"),
        ),
        out_specs=(P(None, "dp", "tensor"), P("dp", "tensor", None, None)),
        check_vma=False,
    )
```

```python
import functools

import jax
import jax.numpy as jnp
from jax import lax
from jax.experimental import pallas as pl
from jax.experimental.pallas import tpu as pltpu
from jax.sharding import PartitionSpec as P

F32 = jnp.float32
BF16 = jnp.bfloat16
MESH = pl.DeviceIdType.MESH

NZ = 8
HELD = 4
HEADS = 16
HALF = 8
WIDTH = 64
STATES = 128
CH = HEADS * WIDTH
LANES = CH + 2 * STATES
STEPS = 3
TAPS = 4
ROWS = 8
TOTAL = 8192
STAGES = ((4, 3, 5), (2, 6, 7), (1, 0))
NEAR = (1, 7, 2, 6, 3, 5, 4)


def silu(v):
    return v * (1.0 / (1.0 + jnp.exp(-v)))


def softplus(v):
    return jnp.maximum(v, 0.0) + jnp.log1p(jnp.exp(-jnp.abs(v)))


def dot(a, b, da, db):
    return lax.dot_general(a, b, (((da,), (db,)), ((), ())), preferred_element_type=F32)


def split(v, n):
    parts = []
    for _ in range(n):
        hi = v.astype(BF16).astype(F32)
        parts.append(hi)
        v = v - hi
    return parts


def stack(parts, axis):
    return jnp.concatenate(parts, axis=axis).astype(BF16)


def sec_pack(R):
    for i in range(3):
        tap = R.pcx[i].astype(F32)
        for q in range(HELD):
            for k in range(8):
                r = 4 * k + i
                R.cpack[q, r : r + 1, :] = tap[q : q + 1, 128 * k : 128 * (k + 1)]
    for q in range(HELD):
        for i in range(3):
            for b in range(2):
                r = 4 * (2 * i + b) + 3
                R.cpack[q, r : r + 1, :] = R.pcbc[q, i, b : b + 1, :].astype(F32)


def sec_dt(R):
    for t in range(STEPS):
        R.st[2 * t : 2 * t + 2, :HEADS] = R.dtin[t]
    R.st[6:7, :HEADS] = R.bias[...]
    R.st[7:8, :HEADS] = R.alog[...]
    R.st[8:9, :HEADS] = R.skip[...]
    parts = split(R.st[:, :HEADS], 3)
    spread = (
        lax.broadcasted_iota(jnp.int32, (HEADS, CH), 1) // WIDTH
        == lax.broadcasted_iota(jnp.int32, (HEADS, CH), 0)
    ).astype(F32)
    full = dot(stack(parts, 1), stack([spread] * 3, 0), 1, 0)
    step = softplus(full[0:ROWS] + full[6:7])
    R.ex[0:ROWS] = step
    R.ex[8:9] = full[8:9]
    R.dec[...] = jnp.exp(-jnp.exp(full[7:8]) * step)


def sec_ab(R):
    pick = (
        lax.broadcasted_iota(jnp.int32, (16, 8 * STATES), 1) // STATES
        == lax.broadcasted_iota(jnp.int32, (16, 8 * STATES), 0)
    ).astype(F32)
    parts = split(R.st[:, :HEADS], 3)
    hb = dot(stack(parts, 0), stack([pick] * 3, 0), 0, 0)

    def col(r):
        return hb[:, r * STATES : (r + 1) * STATES]

    rate = -jnp.exp(col(7))
    for s in range(2):
        a = jnp.ones((HEADS, STATES), F32)
        b = jnp.zeros((HEADS, STATES), F32)
        fin = jnp.full((HEADS, STATES), R.fin[s], jnp.int32)
        for t in range(STEPS):
            d_t = jnp.exp(rate * softplus(col(2 * t + s) + col(6)))
            a = jnp.where(fin == t, 0.0, a) * d_t
            b = jnp.where(fin == t, 1.0, b) * d_t
        R.ab[0, s] = a
        R.ab[1, s] = b


def sec_seq(R):
    for i in range(3):
        R.seq[i, :, :CH] = R.cx[i].astype(F32)
        for s in range(2):
            for b in range(2):
                lo = CH + b * STATES
                R.seq[i, s : s + 1, lo : lo + STATES] = R.cbc[s, i, b : b + 1, :].astype(F32)
    for t in range(STEPS):
        R.seq[3 + t, :, :CH] = R.xin[t].astype(F32)
        for s in range(2):
            for b in range(2):
                lo = CH + b * STATES
                R.seq[3 + t, s : s + 1, lo : lo + STATES] = R.bcin[t, s, b : b + 1, :].astype(F32)
    R.wts[:TAPS, :CH] = R.cw[...]
    for k in range(TAPS):
        for b in range(2):
            lo = CH + b * STATES
            R.wts[k : k + 1, lo : lo + STATES] = R.cwbc[k, b : b + 1, :]


def sec_old(R):
    for t in range(STEPS):
        total = jnp.zeros((2, STATES), F32)
        for k in range(TAPS):
            total += R.wts[k : k + 1, CH + STATES :] * R.seq[t + k, :, CH + STATES :]
        R.acc[2 * t : 2 * t + 2, CH + STATES :] = total
    c_hi, c_lo = split(silu(R.acc[:, CH + STATES :]), 2)
    c_parts = stack([c_hi, c_lo], 0)
    ys = []
    for s in range(2):
        state = R.ssm[s].reshape(CH, STATES)
        hi = state.astype(BF16)
        lo = (state - hi.astype(F32)).astype(BF16)
        both = dot(c_parts, hi, 1, 1)
        ys.append(both[0:ROWS] + both[ROWS:] + dot(c_parts, lo, 1, 1)[0:ROWS])
    row = lax.broadcasted_iota(jnp.int32, (ROWS, CH), 0)
    R.base[...] = jnp.where(lax.rem(row, 2) == 0, ys[0], ys[1])


def sec_unpack(R, packed):
    for k in range(8):
        R.fork[0:3, 128 * k : 128 * (k + 1)] = packed[4 * k : 4 * k + 3]
    for i in range(3):
        for b in range(2):
            r = 4 * (2 * i + b) + 3
            lo = CH + b * STATES
            R.fork[i : i + 1, lo : lo + STATES] = packed[r : r + 1]


def fin_rows(R, lanes):
    first = lax.broadcasted_iota(jnp.int32, (2, lanes), 0) == 0
    return jnp.where(first, R.fin[0], R.fin[1])


def sec_conv(R):
    fin = fin_rows(R, LANES)
    for t in range(STEPS):
        total = jnp.zeros((2, LANES), F32)
        for k in range(TAPS):
            w = R.seq[t + k]
            for f in range(t + 1):
                if t + k - f <= 2:
                    r = t + k - f
                    w = jnp.where(fin == f, R.fork[r : r + 1, :], w)
            total += R.wts[k : k + 1, :] * w
        R.acc[2 * t : 2 * t + 2, :] = total
    R.acc[...] = silu(R.acc[...])


def sec_mix(R):
    fin = fin_rows(R, CH)
    a = jnp.ones((2, CH), F32)
    b = jnp.zeros((2, CH), F32)
    gs = []
    for t in range(STEPS):
        two = slice(2 * t, 2 * t + 2)
        now = fin == t
        d_t = R.dec[two]
        a = jnp.where(now, 0.0, a) * d_t
        b = jnp.where(now, 1.0, b) * d_t
        x_t = R.acc[two, :CH]
        u = R.ex[two] * x_t
        gs = [jnp.where(now, 0.0, v) * d_t for v in gs] + [u]
        c_t = R.acc[two, CH + STATES :]
        total = a * R.base[two] + R.ex[8:9] * x_t
        for k in range(t + 1):
            b_k = R.acc[2 * k : 2 * k + 2, CH : CH + STATES]
            total += gs[k] * jnp.sum(b_k * c_t, axis=1, keepdims=True)
        R.base[two] = total
        R.bco[two] = b
    for k in range(STEPS):
        R.gub[2 * k : 2 * k + 2] = gs[k]
    for t in range(STEPS):
        R.gate[2 * t : 2 * t + 2] = silu(R.zin[t].astype(F32))
    R.cparts[...] = stack(split(R.acc[:, CH + STATES :], 3) + [jnp.zeros((ROWS, STATES), F32)], 0)


def sec_last(R):
    bm = R.acc[:, CH : CH + STATES]
    odd = lax.rem(lax.broadcasted_iota(jnp.int32, (ROWS, STATES), 0), 2)
    both = jnp.concatenate([jnp.where(odd == 0, bm, 0.0), jnp.where(odd == 1, bm, 0.0)], axis=1)
    b_hi, b_lo = split(both, 2)
    g_hi, g_lo = split(R.gub[...], 2)
    rhs = stack([b_hi, b_hi, b_lo, b_lo], 0)
    lhs = stack([g_hi, g_lo, g_hi, g_lo], 0)
    u = dot(lhs, rhs, 0, 0)
    for h in range(HEADS):
        for s in range(2):
            R.ssm[s, h] = (
                R.ab[0, s, h : h + 1, :] * R.ssm[s, h]
                + u[h * WIDTH : (h + 1) * WIDTH, s * STATES : (s + 1) * STATES]
            )


def sec_gate(R):
    y = dot(R.cparts[...], R.fbuf[...].reshape(CH, STATES), 1, 1)
    y = y[0:8] + y[8:16] + y[16:24]
    gated = (R.base[...] + R.bco[...] * y) * R.gate[...]
    R.base[...] = gated
    return jnp.sum(gated * gated, axis=1, keepdims=True)


def sec_state(R, h):
    f = R.fbuf[h].astype(F32)
    for s in range(2):
        R.ssm[s, h] = R.ssm[s, h] + R.ab[1, s, h : h + 1, :] * f


NAMES = (
    "fin_hbm",
    "src_hbm",
    "ssm_hbm",
    "cx_hbm",
    "cbc_hbm",
    "pssm_hbm",
    "pcx_hbm",
    "pcbc_hbm",
    "x_hbm",
    "z_hbm",
    "bc_hbm",
    "dt_hbm",
    "cw_hbm",
    "cwbc_hbm",
    "bias_hbm",
    "alog_hbm",
    "skip_hbm",
    "gain_hbm",
    "out",
    "fs_hbm",
    "ssm",
    "cx",
    "cbc",
    "pcx",
    "pcbc",
    "xin",
    "zin",
    "bcin",
    "dtin",
    "cw",
    "cwbc",
    "bias",
    "alog",
    "skip",
    "gain",
    "fin",
    "src",
    "plan_out",
    "plan_in",
    "pbuf",
    "pconv",
    "cpack",
    "csend",
    "cxbuf",
    "czsend",
    "czbuf",
    "sbuf",
    *(f"xb{g}" for g in range(len(STAGES))),
    "zsend",
    "zbuf",
    "fbuf",
    "ysend",
    "ybuf",
    "seq",
    "fork",
    "acc",
    "wts",
    "st",
    "ex",
    "dec",
    "base",
    "bco",
    "gub",
    "gate",
    "ab",
    "cparts",
    "in_sem",
    "sc_sem",
    "own_sem",
    "out_sem",
    "plan_s",
    "plan_r",
    "pair_s",
    "pair_r",
    "cx_s",
    "cx_r",
    "cz_s",
    "cz_r",
    "x_s",
    "x_r",
    "z_s",
    "z_r",
    "g_s",
    "g_r",
    "f_s",
    "f_r",
    "y_s",
    "y_r",
)


class Refs:
    pass


def kernel(nx, ny, *refs):
    R = Refs()
    for name, ref in zip(NAMES, refs, strict=True):
        setattr(R, name, ref)
    me = lax.axis_index("dp")
    c = lax.rem(me, 2)
    z = lax.rem(me // 2, NZ)
    x = me // (2 * NZ)
    y = lax.axis_index("tensor")
    xbs = [getattr(R, f"xb{g}") for g in range(len(STAGES))]

    def at(xx, zz, cc):
        return {"dp": (xx * NZ + zz) * 2 + cc}

    def xpeer(d):
        return lax.rem(x + d, nx)

    def zpeer(d):
        return lax.rem(z + d, NZ)

    def ypeer(d):
        return lax.rem(y + d, ny)

    sibling = at(x, z, 1 - c)

    def remote(src, dst, ssem, rsem, dev):
        return pltpu.make_async_remote_copy(
            src_ref=src, dst_ref=dst, send_sem=ssem, recv_sem=rsem, device_id=dev, device_id_type=MESH
        )

    barrier = pltpu.get_barrier_semaphore()
    for d in range(1, ny):
        pl.semaphore_signal(barrier, inc=1, device_id={"tensor": ypeer(d)}, device_id_type=MESH)
    for d in range(1, NZ):
        pl.semaphore_signal(barrier, inc=1, device_id=at(x, zpeer(d), c), device_id_type=MESH)
    for d in range(1, nx):
        pl.semaphore_signal(barrier, inc=1, device_id=at(xpeer(d), z, c), device_id_type=MESH)
    pl.semaphore_signal(barrier, inc=1, device_id=sibling, device_id_type=MESH)

    mine = pl.ds(pl.multiple_of(c * HALF, HALF), HALF)
    theirs = pl.ds(pl.multiple_of((1 - c) * HALF, HALF), HALF)
    my_slot = pl.ds(pl.multiple_of(c * HELD, HELD), HELD)
    scalars = [
        pltpu.make_async_copy(R.fin_hbm, R.fin, R.sc_sem.at[0]),
        pltpu.make_async_copy(R.src_hbm, R.src, R.sc_sem.at[1]),
    ]
    loads = [
        pltpu.make_async_copy(src, dst, R.in_sem.at[i])
        for i, (src, dst) in enumerate(
            (
                (R.pcx_hbm, R.pcx),
                (R.pcbc_hbm, R.pcbc),
                (R.dt_hbm, R.dtin),
                (R.bias_hbm, R.bias),
                (R.alog_hbm, R.alog),
                (R.skip_hbm, R.skip),
                (R.cx_hbm, R.cx),
                (R.cbc_hbm, R.cbc),
                (R.x_hbm, R.xin),
                (R.bc_hbm, R.bcin),
                (R.cw_hbm, R.cw),
                (R.cwbc_hbm, R.cwbc),
                (R.z_hbm, R.zin),
                (R.gain_hbm, R.gain),
                (R.ssm_hbm, R.ssm),
            )
        )
    ]
    own = pltpu.make_async_copy(R.pssm_hbm.at[:, mine], R.pbuf.at[my_slot], R.own_sem)
    for cp in scalars + loads[:2] + [own] + loads[2:]:
        cp.start()
    for ref in (R.wts, R.st, R.acc, R.base, R.bco, R.gub, R.gate):
        ref[...] = jnp.zeros_like(ref)
    for cp in scalars:
        cp.wait()
    prompt = jnp.where(R.fin[0] < STEPS, R.src[0], R.src[1])
    R.plan_out[...] = jnp.full(R.plan_out.shape, prompt, jnp.int32)

    pl.semaphore_wait(barrier, 1 + (nx - 1) + (NZ - 1) + (ny - 1))

    order = (2, 1, 3) if nx == 4 else tuple(range(1, nx))
    plans = {}
    for d in order:
        plans[d] = remote(
            R.plan_out, R.plan_in.at[d], R.plan_s.at[d], R.plan_r.at[d], at(xpeer(d), z, c)
        )
        plans[d].start()
    pair = remote(R.pssm_hbm.at[:, theirs], R.pbuf.at[my_slot], R.pair_s.at[0], R.pair_r.at[0], sibling)
    pair.start()
    loads[0].wait()
    loads[1].wait()
    sec_pack(R)
    R.pconv[my_slot] = R.cpack[...].astype(BF16)
    pair_conv = remote(
        R.pconv.at[my_slot], R.pconv.at[my_slot], R.pair_s.at[1], R.pair_r.at[1], sibling
    )
    pair_conv.start()

    for i in range(2, 6):
        loads[i].wait()
    sec_dt(R)
    sec_ab(R)

    pair.wait_recv()
    pair_conv.wait_recv()
    own.wait()
    for d in order:
        plans[d].wait_recv()

    def wanted(d):
        return lax.rem(jnp.max(R.plan_in[nx - d]), 2 * HELD)

    want = {d: wanted(d) for d in order}
    want[0] = lax.rem(prompt, 2 * HELD)
    owner_x = prompt // (2 * HELD * NZ)
    owner_z = lax.rem(prompt // (2 * HELD), NZ)

    conv_sends = []
    for i, d in enumerate(order):
        R.csend[i] = R.pconv[want[d]]
        cp = remote(R.csend.at[i], R.cxbuf.at[x], R.cx_s.at[d], R.cx_r.at[d], at(xpeer(d), z, c))
        cp.start()
        conv_sends.append(cp)
    starts = [sum(len(o) for o in STAGES[:g]) for g in range(len(STAGES))]
    x_sends = []
    for g, offsets in enumerate(STAGES):
        sends = []
        for i, d in enumerate(order):
            for n, o in enumerate(offsets):
                R.sbuf[i, starts[g] + n] = R.pbuf[want[d], zpeer(o)]
            part = R.sbuf.at[i, starts[g] : starts[g] + len(offsets)]
            cp = remote(
                part, xbs[g].at[x], R.x_s.at[g, d], R.x_r.at[g, d], at(xpeer(d), z, c)
            )
            cp.start()
            sends.append(cp)
        x_sends.append(sends)
    R.cxbuf[x] = R.pconv[want[0]]
    for g, offsets in enumerate(STAGES):
        for n, o in enumerate(offsets):
            xbs[g][x, n] = R.pbuf[want[0], zpeer(o)]

    for i in range(6, 12):
        loads[i].wait()
    sec_seq(R)

    for cp in conv_sends:
        cp.wait_recv()
    picked = R.cxbuf[owner_x]
    R.czsend[...] = picked
    R.czbuf[z] = picked
    cz_sends = []
    for d in (4, 3, 5, 2, 6, 1, 7):
        cp = remote(R.czsend, R.czbuf.at[z], R.cz_s.at[d], R.cz_r.at[d], at(x, zpeer(d), c))
        cp.start()
        cz_sends.append(cp)
    loads[14].wait()
    sec_old(R)

    z_sends = {}
    for g, offsets in enumerate(STAGES):
        for cp in x_sends[g]:
            cp.wait_recv()
        for n, o in enumerate(offsets):
            head = xbs[g][owner_x, n]
            if o == 0:
                R.zbuf[z] = head
            else:
                R.zsend[o] = head
                z_sends[o] = remote(
                    R.zsend.at[o], R.zbuf.at[z], R.z_s.at[o], R.z_r.at[o], at(x, zpeer(o), c)
                )
                z_sends[o].start()

    for cp in cz_sends:
        cp.wait_recv()
    sec_unpack(R, R.czbuf[owner_z].astype(F32))
    sec_conv(R)

    for o in (4, 3, 5, 2, 6, 1, 7):
        z_sends[o].wait_recv()
    here = c * HALF + z
    R.fbuf[here] = R.zbuf[owner_z]
    g_sends, f_sends = {}, {}
    for d in (4, 3, 5, 2, 6, 1, 7):
        g_sends[d] = remote(
            R.fbuf.at[here], R.fbuf.at[here], R.g_s.at[d], R.g_r.at[d], at(x, zpeer(d), c)
        )
        g_sends[d].start()
    f_sends[0] = remote(R.fbuf.at[here], R.fbuf.at[here], R.f_s.at[0], R.f_r.at[0], sibling)
    f_sends[0].start()
    for i in (12, 13):
        loads[i].wait()
    sec_mix(R)
    sec_last(R)
    for d in NEAR:
        g_sends[d].wait_recv()
        landed = c * HALF + zpeer(NZ - d)
        f_sends[d] = remote(R.fbuf.at[landed], R.fbuf.at[landed], R.f_s.at[d], R.f_r.at[d], sibling)
        f_sends[d].start()
    for d in (0,) + NEAR:
        f_sends[d].wait_recv()

    squares = sec_gate(R)
    R.ysend[...] = jnp.broadcast_to(squares, R.ysend.shape)
    R.ybuf[y] = R.ysend[...]
    y_sends = []
    for d in (4, 3, 5, 2, 6, 1, 7) if ny == 8 else range(1, ny):
        cp = remote(R.ysend, R.ybuf.at[y], R.y_s.at[d], R.y_r.at[d], {"tensor": ypeer(d)})
        cp.start()
        y_sends.append(cp)

    stores = []
    for h in range(HEADS):
        sec_state(R, h)
        if h % 4 == 3:
            for s in range(2):
                some = slice(h - 3, h + 1)
                cp = pltpu.make_async_copy(
                    R.ssm.at[s, some], R.fs_hbm.at[s, some], R.out_sem.at[s, h // 4]
                )
                cp.start()
                stores.append(cp)
    for cp in list(plans.values()) + [pair, pair_conv] + conv_sends + cz_sends:
        cp.wait_send()
    for sends in x_sends:
        for cp in sends:
            cp.wait_send()
    for group in (z_sends, g_sends, f_sends):
        for cp in group.values():
            cp.wait_send()
    for cp in stores:
        cp.wait()

    for cp in y_sends:
        cp.wait_recv()
    total = R.ybuf[0]
    for i in range(1, ny):
        total += R.ybuf[i]
    scale = lax.rsqrt(total[:, 0:1] / TOTAL + 1e-05)
    normed = R.base[...] * scale * R.gain[...]
    for t in range(STEPS):
        R.out[t] = normed[2 * t : 2 * t + 2].astype(BF16)
    for cp in y_sends:
        cp.wait_send()


def put(out_ref, fs_ref, out_hbm, fs_hbm, sem):
    copies = [
        pltpu.make_async_copy(fs_ref.at[s, h : h + 8], fs_hbm.at[s, h : h + 8], sem.at[2 * s + h // 8])
        for s in range(2)
        for h in (0, 8)
    ]
    copies.append(pltpu.make_async_copy(out_ref, out_hbm, sem.at[4]))
    for cp in copies:
        cp.start()
    for cp in copies:
        cp.wait()


def body(nx, ny, *args):
    args = list(args)
    args[3] = jnp.swapaxes(args[3], 0, 1)
    args[6] = jnp.swapaxes(args[6], 0, 1)
    for i in (14, 15, 16, 17):
        args[i] = args[i].reshape(1, -1)
    dma = pltpu.SemaphoreType.DMA
    vmem = pltpu.VMEM
    in_vmem = [args[i] for i in (2, 3, 4, 6, 7, 8, 9, 10, 11, 12, 13, 14, 15, 16, 17)]
    head = (WIDTH, STATES)
    scratch = [vmem(a.shape, a.dtype) for a in in_vmem]
    scratch += [pltpu.SMEM(a.shape, a.dtype) for a in args[:2]]
    scratch += [
        vmem((8, 128), jnp.int32),
        vmem((nx, 8, 128), jnp.int32),
        vmem((2 * HELD, HALF) + head, BF16),
        vmem((2 * HELD, 32, 128), BF16),
        vmem((HELD, 32, 128), F32),
        vmem((nx, 32, 128), BF16),
        vmem((nx, 32, 128), BF16),
        vmem((32, 128), BF16),
        vmem((NZ, 32, 128), BF16),
        vmem((nx, NZ) + head, BF16),
    ]
    scratch += [vmem((nx, len(o)) + head, BF16) for o in STAGES]
    scratch += [
        vmem((NZ,) + head, BF16),
        vmem((NZ,) + head, BF16),
        vmem((HEADS,) + head, BF16),
        vmem((8, 128), F32),
        vmem((ny, 8, 128), F32),
        vmem((6, 2, LANES), F32),
        vmem((8, LANES), F32),
        vmem((ROWS, LANES), F32),
        vmem((8, LANES), F32),
        vmem((16, 128), F32),
        vmem((16, CH), F32),
        vmem((ROWS, CH), F32),
        vmem((ROWS, CH), F32),
        vmem((ROWS, CH), F32),
        vmem((ROWS, CH), F32),
        vmem((ROWS, CH), F32),
        vmem((2, 2, HEADS, STATES), F32),
        vmem((4 * ROWS, STATES), BF16),
        dma((len(in_vmem),)),
        dma((2,)),
        dma,
        dma((2, 4)),
        dma((nx,)),
        dma((nx,)),
        dma((2,)),
        dma((2,)),
        dma((nx,)),
        dma((nx,)),
        dma((NZ,)),
        dma((NZ,)),
        dma((len(STAGES), nx)),
        dma((len(STAGES), nx)),
        dma((NZ,)),
        dma((NZ,)),
        dma((NZ,)),
        dma((NZ,)),
        dma((NZ,)),
        dma((NZ,)),
        dma((ny,)),
        dma((ny,)),
    ]
    args = [pltpu.with_memory_space_constraint(a, pltpu.HBM) for a in args]
    anywhere = pl.BlockSpec(memory_space=pl.ANY)
    slots = args[0].shape[0]
    out, fs = pl.pallas_call(
        functools.partial(kernel, nx, ny),
        out_shape=(
            pltpu.VMEM((STEPS, slots, CH), BF16),
            pltpu.VMEM(args[2].shape, F32),
        ),
        in_specs=[anywhere] * 18,
        out_specs=(pl.BlockSpec(memory_space=pltpu.VMEM), anywhere),
        scratch_shapes=scratch,
        compiler_params=pltpu.CompilerParams(
            collective_id=0, has_side_effects=True, vmem_limit_bytes=32 * 1024 * 1024
        ),
    )(*args)
    return pl.pallas_call(
        put,
        out_shape=(jax.ShapeDtypeStruct(out.shape, BF16), jax.ShapeDtypeStruct(fs.shape, F32)),
        in_specs=[anywhere] * 2,
        out_specs=(anywhere,anywhere),
        scratch_shapes=[dma((5,))],
        compiler_params=pltpu.CompilerParams(vmem_limit_bytes=16 * 1024 * 1024),
    )(out, fs)


def solution(mesh):
    nx = mesh.shape["dp"] // (2 * NZ)
    ny = mesh.shape["tensor"]
    return jax.shard_map(
        functools.partial(body, nx, ny),
        mesh=mesh,
        in_specs=(
            P("dp"),
            P("dp"),
            P("dp", "tensor", None, None),
            P("dp", None, "tensor"),
            P("dp", None, None, "tensor"),
            P("dp", "tensor", None, None),
            P("dp", None, "tensor"),
            P("dp", None, None, "tensor"),
            P(None, "dp", "tensor"),
            P(None, "dp", "tensor"),
            P(None, "dp", None, "tensor"),
            P(None, "dp", "tensor"),
            P(None, "tensor"),
            P(None, None, "tensor"),
            P("tensor"),
            P("tensor"),
            P("tensor"),
            P("tensor"),
        ),
        out_specs=(P(None, "dp", "tensor"), P("dp", "tensor", None, None)),
        check_vma=False,
    )
```

```python
import functools

import jax
import jax.numpy as jnp
from jax import lax
from jax.experimental import pallas as pl
from jax.experimental.pallas import tpu as pltpu
from jax.sharding import PartitionSpec as P

F32 = jnp.float32
BF16 = jnp.bfloat16
MESH = pl.DeviceIdType.MESH

NZ = 8
HELD = 4
HEADS = 16
HALF = 8
WIDTH = 64
STATES = 128
CH = HEADS * WIDTH
LANES = CH + 2 * STATES
STEPS = 3
TAPS = 4
ROWS = 8
TOTAL = 8192
STAGES = ((4, 3, 5), (2, 6, 7), (1, 0))
NEAR = (1, 7, 2, 6, 3, 5, 4)


def silu(v):
    return v * (1.0 / (1.0 + jnp.exp(-v)))


def softplus(v):
    return jnp.maximum(v, 0.0) + jnp.log1p(jnp.exp(-jnp.abs(v)))


def dot(a, b, da, db):
    return lax.dot_general(a, b, (((da,), (db,)), ((), ())), preferred_element_type=F32)


def split(v, n):
    parts = []
    for _ in range(n):
        hi = v.astype(BF16).astype(F32)
        parts.append(hi)
        v = v - hi
    return parts


def stack(parts, axis):
    return jnp.concatenate(parts, axis=axis).astype(BF16)


def sec_pack(R):
    for i in range(3):
        tap = R.pcx[i].astype(F32)
        for q in range(HELD):
            for k in range(8):
                r = 4 * k + i
                R.cpack[q, r : r + 1, :] = tap[q : q + 1, 128 * k : 128 * (k + 1)]
    for q in range(HELD):
        for i in range(3):
            for b in range(2):
                r = 4 * (2 * i + b) + 3
                R.cpack[q, r : r + 1, :] = R.pcbc[q, i, b : b + 1, :].astype(F32)


def sec_dt(R):
    for t in range(STEPS):
        R.st[2 * t : 2 * t + 2, :HEADS] = R.dtin[t]
    R.st[6:7, :HEADS] = R.bias[...]
    R.st[7:8, :HEADS] = R.alog[...]
    R.st[8:9, :HEADS] = R.skip[...]
    parts = split(R.st[:, :HEADS], 3)
    spread = (
        lax.broadcasted_iota(jnp.int32, (HEADS, CH), 1) // WIDTH
        == lax.broadcasted_iota(jnp.int32, (HEADS, CH), 0)
    ).astype(F32)
    full = dot(stack(parts, 1), stack([spread] * 3, 0), 1, 0)
    step = softplus(full[0:ROWS] + full[6:7])
    R.ex[0:ROWS] = step
    R.ex[8:9] = full[8:9]
    R.dec[...] = jnp.exp(-jnp.exp(full[7:8]) * step)


def sec_ab(R):
    pick = (
        lax.broadcasted_iota(jnp.int32, (16, 8 * STATES), 1) // STATES
        == lax.broadcasted_iota(jnp.int32, (16, 8 * STATES), 0)
    ).astype(F32)
    parts = split(R.st[:, :HEADS], 3)
    hb = dot(stack(parts, 0), stack([pick] * 3, 0), 0, 0)

    def col(r):
        return hb[:, r * STATES : (r + 1) * STATES]

    rate = -jnp.exp(col(7))
    for s in range(2):
        a = jnp.ones((HEADS, STATES), F32)
        b = jnp.zeros((HEADS, STATES), F32)
        fin = jnp.full((HEADS, STATES), R.fin[s], jnp.int32)
        for t in range(STEPS):
            d_t = jnp.exp(rate * softplus(col(2 * t + s) + col(6)))
            a = jnp.where(fin == t, 0.0, a) * d_t
            b = jnp.where(fin == t, 1.0, b) * d_t
        R.ab[0, s] = a
        R.ab[1, s] = b


def sec_seq(R):
    for i in range(3):
        R.seq[i, :, :CH] = R.cx[i].astype(F32)
        for s in range(2):
            for b in range(2):
                lo = CH + b * STATES
                R.seq[i, s : s + 1, lo : lo + STATES] = R.cbc[s, i, b : b + 1, :].astype(F32)
    for t in range(STEPS):
        R.seq[3 + t, :, :CH] = R.xin[t].astype(F32)
        for s in range(2):
            for b in range(2):
                lo = CH + b * STATES
                R.seq[3 + t, s : s + 1, lo : lo + STATES] = R.bcin[t, s, b : b + 1, :].astype(F32)
    R.wts[:TAPS, :CH] = R.cw[...]
    for k in range(TAPS):
        for b in range(2):
            lo = CH + b * STATES
            R.wts[k : k + 1, lo : lo + STATES] = R.cwbc[k, b : b + 1, :]


def sec_old(R):
    for t in range(STEPS):
        total = jnp.zeros((2, STATES), F32)
        for k in range(TAPS):
            total += R.wts[k : k + 1, CH + STATES :] * R.seq[t + k, :, CH + STATES :]
        R.acc[2 * t : 2 * t + 2, CH + STATES :] = total
    c_hi, c_lo = split(silu(R.acc[:, CH + STATES :]), 2)
    c_parts = stack([c_hi, c_lo], 0)
    ys = []
    for s in range(2):
        state = R.ssm[s].reshape(CH, STATES)
        hi = state.astype(BF16)
        lo = (state - hi.astype(F32)).astype(BF16)
        both = dot(c_parts, hi, 1, 1)
        ys.append(both[0:ROWS] + both[ROWS:] + dot(c_parts, lo, 1, 1)[0:ROWS])
    row = lax.broadcasted_iota(jnp.int32, (ROWS, CH), 0)
    R.base[...] = jnp.where(row >= 2 * STEPS, 0.0, jnp.where(lax.rem(row, 2) == 0, ys[0], ys[1]))


def sec_unpack(R, packed):
    for k in range(8):
        R.fork[0:3, 128 * k : 128 * (k + 1)] = packed[4 * k : 4 * k + 3]
    for i in range(3):
        for b in range(2):
            r = 4 * (2 * i + b) + 3
            lo = CH + b * STATES
            R.fork[i : i + 1, lo : lo + STATES] = packed[r : r + 1]


def fin_rows(R, lanes):
    first = lax.broadcasted_iota(jnp.int32, (2, lanes), 0) == 0
    return jnp.where(first, R.fin[0], R.fin[1])


def sec_conv(R):
    fin = fin_rows(R, LANES)
    for t in range(STEPS):
        total = jnp.zeros((2, LANES), F32)
        for k in range(TAPS):
            w = R.seq[t + k]
            for f in range(t + 1):
                if t + k - f <= 2:
                    r = t + k - f
                    w = jnp.where(fin == f, R.fork[r : r + 1, :], w)
            total += R.wts[k : k + 1, :] * w
        R.acc[2 * t : 2 * t + 2, :] = total
    R.acc[...] = silu(R.acc[...])


def sec_mix(R):
    fin = fin_rows(R, CH)
    a = jnp.ones((2, CH), F32)
    b = jnp.zeros((2, CH), F32)
    gs = []
    for t in range(STEPS):
        two = slice(2 * t, 2 * t + 2)
        now = fin == t
        d_t = R.dec[two]
        a = jnp.where(now, 0.0, a) * d_t
        b = jnp.where(now, 1.0, b) * d_t
        x_t = R.acc[two, :CH]
        u = R.ex[two] * x_t
        gs = [jnp.where(now, 0.0, v) * d_t for v in gs] + [u]
        c_t = R.acc[two, CH + STATES :]
        total = a * R.base[two] + R.ex[8:9] * x_t
        for k in range(t + 1):
            b_k = R.acc[2 * k : 2 * k + 2, CH : CH + STATES]
            total += gs[k] * jnp.sum(b_k * c_t, axis=1, keepdims=True)
        R.base[two] = total
        R.bco[two] = b
    for k in range(STEPS):
        R.gub[2 * k : 2 * k + 2] = gs[k]
    for t in range(STEPS):
        R.gate[2 * t : 2 * t + 2] = silu(R.zin[t].astype(F32))


def sec_last(R):
    bm = R.acc[:, CH : CH + STATES]
    odd = lax.rem(lax.broadcasted_iota(jnp.int32, (ROWS, STATES), 0), 2)
    both = jnp.concatenate([jnp.where(odd == 0, bm, 0.0), jnp.where(odd == 1, bm, 0.0)], axis=1)
    b_hi, b_lo = split(both, 2)
    g_hi, g_lo = split(R.gub[...], 2)
    rhs = stack([b_hi, b_hi, b_lo, b_lo], 0)
    lhs = stack([g_hi, g_lo, g_hi, g_lo], 0)
    u = dot(lhs, rhs, 0, 0)
    for h in range(HEADS):
        for s in range(2):
            R.ssm[s, h] = (
                R.ab[0, s, h : h + 1, :] * R.ssm[s, h]
                + u[h * WIDTH : (h + 1) * WIDTH, s * STATES : (s + 1) * STATES]
            )


def sec_own_c(R, f):
    rows = [
        jnp.where(R.fin[0] < STEPS, R.bcin[t, 0, 1:2, :].astype(F32), R.bcin[t, 1, 1:2, :].astype(F32))
        for t in range(STEPS)
    ]
    after = [
        jnp.where(f == 0, rows[0], jnp.where(f == 1, rows[1], rows[2])),
        jnp.where(f == 0, rows[1], rows[2]),
        rows[2],
    ]
    for n in range(STEPS):
        total = jnp.zeros((1, STATES), F32)
        for i in range(n + 1):
            total += R.cwbc[i + 3 - n, 1:2, :] * after[i]
        R.esend[n : n + 1] = total
        R.esend[n + 4 : n + 5] = total


def sec_group_y(R, packed):
    fork_c = [packed[4 * (2 * i + 1) + 3 : 4 * (2 * i + 1) + 4] for i in range(3)]
    zero = jnp.zeros((1, STATES), F32)
    adds = []
    for n in range(STEPS):
        total = zero
        for k in range(3 - n):
            total += R.cwbc[k, 1:2, :] * fork_c[n + k]
        adds.append(total)
    adds = jnp.concatenate((adds + [zero]) * 2, axis=0)
    cs = silu(R.ebuf[...] + adds[None]).reshape(2 * NZ * 8, STATES)
    y = dot(stack(split(cs, 2), 0), R.hbuf[...].reshape(HALF * WIDTH, STATES), 1, 1)
    y = (y[: 2 * NZ * 8] + y[2 * NZ * 8 :]).reshape(2 * NZ, 8, HALF * WIDTH)
    top = lax.broadcasted_iota(jnp.int32, (2 * NZ, 8, 128), 1) < 4
    for i in range(2):
        lo = 256 * i
        R.yrs[:, 8 * i : 8 * i + 8, :] = jnp.where(
            top, y[:, :, lo : lo + 128], y[:, :, lo + 128 : lo + 256]
        )


def sec_gate(R, f, owner_z):
    rows = []
    for n in range(STEPS):
        rows.append(
            jnp.concatenate(
                [
                    R.yrb[cc, owner_z, 8 * i + 4 * j + n : 8 * i + 4 * j + n + 1, :]
                    for cc in range(2)
                    for i in range(2)
                    for j in range(2)
                ],
                axis=1,
            )
        )
    at_step = [
        rows[0],
        jnp.where(f == 0, rows[1], rows[0]),
        jnp.where(f == 0, rows[2], jnp.where(f == 1, rows[1], rows[0])),
    ]
    for t in range(STEPS):
        two = slice(2 * t, 2 * t + 2)
        R.base[two] = (R.base[two] + R.bco[two] * at_step[t]) * R.gate[two]
    gated = R.base[...]
    return jnp.sum(gated * gated, axis=1, keepdims=True)


NAMES = (
    "fin_hbm",
    "src_hbm",
    "ssm_hbm",
    "cx_hbm",
    "cbc_hbm",
    "pssm_hbm",
    "pcx_hbm",
    "pcbc_hbm",
    "x_hbm",
    "z_hbm",
    "bc_hbm",
    "dt_hbm",
    "cw_hbm",
    "cwbc_hbm",
    "bias_hbm",
    "alog_hbm",
    "skip_hbm",
    "gain_hbm",
    "out",
    "pre_out",
    "fork_out",
    "ab_out",
    "ssm",
    "cx",
    "cbc",
    "pcx",
    "pcbc",
    "xin",
    "zin",
    "bcin",
    "dtin",
    "cw",
    "cwbc",
    "bias",
    "alog",
    "skip",
    "gain",
    "fin",
    "src",
    "plan_out",
    "plan_in",
    "pbuf",
    "pconv",
    "cpack",
    "csend",
    "cxbuf",
    "czsend",
    "czbuf",
    "sbuf",
    *(f"xb{g}" for g in range(len(STAGES))),
    "zsend",
    "zbuf",
    "fbuf",
    "ysend",
    "ybuf",
    "seq",
    "fork",
    "acc",
    "wts",
    "st",
    "ex",
    "dec",
    "base",
    "bco",
    "gub",
    "gate",
    "ab",
    "esend",
    "ebuf",
    "hbuf",
    "yrs",
    "yrb",
    "in_sem",
    "sc_sem",
    "own_sem",
    "out_sem",
    "plan_s",
    "plan_r",
    "pair_s",
    "pair_r",
    "cx_s",
    "cx_r",
    "cz_s",
    "cz_r",
    "x_s",
    "x_r",
    "z_s",
    "z_r",
    "g_s",
    "g_r",
    "f_s",
    "f_r",
    "e_s",
    "e_r",
    "r_s",
    "r_r",
    "y_s",
    "y_r",
)


class Refs:
    pass


def kernel(nx, ny, *refs):
    R = Refs()
    for name, ref in zip(NAMES, refs, strict=True):
        setattr(R, name, ref)
    me = lax.axis_index("dp")
    c = lax.rem(me, 2)
    z = lax.rem(me // 2, NZ)
    x = me // (2 * NZ)
    y = lax.axis_index("tensor")
    xbs = [getattr(R, f"xb{g}") for g in range(len(STAGES))]

    def at(xx, zz, cc):
        return {"dp": (xx * NZ + zz) * 2 + cc}

    def xpeer(d):
        return lax.rem(x + d, nx)

    def zpeer(d):
        return lax.rem(z + d, NZ)

    def ypeer(d):
        return lax.rem(y + d, ny)

    sibling = at(x, z, 1 - c)

    def remote(src, dst, ssem, rsem, dev):
        return pltpu.make_async_remote_copy(
            src_ref=src, dst_ref=dst, send_sem=ssem, recv_sem=rsem, device_id=dev, device_id_type=MESH
        )

    barrier = pltpu.get_barrier_semaphore()
    for d in range(1, nx):
        pl.semaphore_signal(barrier, inc=1, device_id=at(xpeer(d), z, c), device_id_type=MESH)
    scalars = [
        pltpu.make_async_copy(R.fin_hbm, R.fin, R.sc_sem.at[0]),
        pltpu.make_async_copy(R.src_hbm, R.src, R.sc_sem.at[1]),
    ]
    for cp in scalars:
        cp.start()
    for d in (4, 3, 5, 2, 6, 1, 7):
        for cc in (c, 1 - c):
            pl.semaphore_signal(barrier, inc=1, device_id=at(x, zpeer(d), cc), device_id_type=MESH)
    for d in range(1, ny):
        pl.semaphore_signal(barrier, inc=1, device_id={"tensor": ypeer(d)}, device_id_type=MESH)
    pl.semaphore_signal(barrier, inc=1, device_id=sibling, device_id_type=MESH)

    mine = pl.ds(pl.multiple_of(c * HALF, HALF), HALF)
    theirs = pl.ds(pl.multiple_of((1 - c) * HALF, HALF), HALF)
    my_slot = pl.ds(pl.multiple_of(c * HELD, HELD), HELD)
    loads = [
        pltpu.make_async_copy(src, dst, R.in_sem.at[i])
        for i, (src, dst) in enumerate(
            (
                (R.pcx_hbm, R.pcx),
                (R.pcbc_hbm, R.pcbc),
                (R.dt_hbm, R.dtin),
                (R.bias_hbm, R.bias),
                (R.alog_hbm, R.alog),
                (R.skip_hbm, R.skip),
                (R.cx_hbm, R.cx),
                (R.cbc_hbm, R.cbc),
                (R.x_hbm, R.xin),
                (R.bc_hbm, R.bcin),
                (R.cw_hbm, R.cw),
                (R.cwbc_hbm, R.cwbc),
                (R.z_hbm, R.zin),
                (R.gain_hbm, R.gain),
                (R.ssm_hbm, R.ssm),
            )
        )
    ]
    own = pltpu.make_async_copy(R.pssm_hbm.at[:, mine], R.pbuf.at[my_slot], R.own_sem)
    for cp in scalars:
        cp.wait()
    prompt = jnp.where(R.fin[0] < STEPS, R.src[0], R.src[1])
    refill = jnp.where(R.fin[0] < STEPS, R.fin[0], R.fin[1])
    R.plan_out[...] = jnp.full(R.plan_out.shape, prompt, jnp.int32)

    pl.semaphore_wait(barrier, 1 + (nx - 1) + 2 * (NZ - 1) + (ny - 1))

    order = (2, 1, 3) if nx == 4 else tuple(range(1, nx))
    plans = {}
    for d in order:
        plans[d] = remote(
            R.plan_out, R.plan_in.at[d], R.plan_s.at[d], R.plan_r.at[d], at(xpeer(d), z, c)
        )
        plans[d].start()
    pair = remote(R.pssm_hbm.at[:, theirs], R.pbuf.at[my_slot], R.pair_s.at[0], R.pair_r.at[0], sibling)
    pair.start()
    for cp in [loads[9], loads[11], loads[0], loads[1], own] + loads[2:9] + [loads[10]] + loads[12:]:
        cp.start()
    for ref in (R.wts, R.st, R.acc, R.base, R.bco, R.gub, R.gate, R.esend):
        ref[...] = jnp.zeros_like(ref)
    loads[9].wait()
    loads[11].wait()
    sec_own_c(R, refill)
    here = c * NZ + z
    R.ebuf[here] = R.esend[...]

    def group(src, dst, ssem, rsem):
        sends = []
        for d in (4, 3, 5, 2, 6, 1, 7, 0):
            for k in (0, 1) if d else (1,):
                cc = c if k == 0 else 1 - c
                to = cc * NZ + zpeer(d)
                cp = remote(src(to), dst, ssem.at[k, d], rsem.at[k, d], at(x, zpeer(d), cc))
                cp.start()
                sends.append(cp)
        return sends

    e_sends = group(lambda to: R.esend, R.ebuf.at[here], R.e_s, R.e_r)
    loads[0].wait()
    loads[1].wait()
    sec_pack(R)
    R.pconv[my_slot] = R.cpack[...].astype(BF16)
    pair_conv = remote(
        R.pconv.at[my_slot], R.pconv.at[my_slot], R.pair_s.at[1], R.pair_r.at[1], sibling
    )
    pair_conv.start()

    for i in range(2, 6):
        loads[i].wait()
    sec_dt(R)
    sec_ab(R)

    pair.wait_recv()
    pair_conv.wait_recv()
    own.wait()
    for d in order:
        plans[d].wait_recv()

    def wanted(d):
        return lax.rem(R.plan_in[nx - d, 0, 0], 2 * HELD)

    want = {d: wanted(d) for d in order}
    want[0] = lax.rem(prompt, 2 * HELD)
    owner_x = prompt // (2 * HELD * NZ)
    owner_z = lax.rem(prompt // (2 * HELD), NZ)

    conv_sends = []
    for i, d in enumerate(order):
        R.csend[i] = R.pconv[want[d]]
        cp = remote(R.csend.at[i], R.cxbuf.at[x], R.cx_s.at[d], R.cx_r.at[d], at(xpeer(d), z, c))
        cp.start()
        conv_sends.append(cp)
    starts = [sum(len(o) for o in STAGES[:g]) for g in range(len(STAGES))]
    x_sends = []
    for g, offsets in enumerate(STAGES):
        sends = []
        for i, d in enumerate(order):
            for n, o in enumerate(offsets):
                R.sbuf[i, starts[g] + n] = R.pbuf[want[d], zpeer(o)]
            part = R.sbuf.at[i, starts[g] : starts[g] + len(offsets)]
            cp = remote(
                part, xbs[g].at[x], R.x_s.at[g, d], R.x_r.at[g, d], at(xpeer(d), z, c)
            )
            cp.start()
            sends.append(cp)
        x_sends.append(sends)
    R.cxbuf[x] = R.pconv[want[0]]
    for g, offsets in enumerate(STAGES):
        for n, o in enumerate(offsets):
            xbs[g][x, n] = R.pbuf[want[0], zpeer(o)]

    for i in (6, 7, 8, 10):
        loads[i].wait()
    sec_seq(R)

    for cp in conv_sends:
        cp.wait_recv()
    picked = R.cxbuf[owner_x]
    R.czsend[...] = picked
    R.czbuf[z] = picked
    cz_sends = []
    for d in (4, 3, 5, 2, 6, 1, 7):
        cp = remote(R.czsend, R.czbuf.at[z], R.cz_s.at[d], R.cz_r.at[d], at(x, zpeer(d), c))
        cp.start()
        cz_sends.append(cp)
    loads[14].wait()
    sec_old(R)

    z_sends = {}
    for g, offsets in enumerate(STAGES):
        for cp in x_sends[g]:
            cp.wait_recv()
        for n, o in enumerate(offsets):
            head = xbs[g][owner_x, n]
            R.hbuf[zpeer(o)] = head
            if o == 0:
                R.zbuf[z] = head
            else:
                R.zsend[o] = head
                z_sends[o] = remote(
                    R.zsend.at[o], R.zbuf.at[z], R.z_s.at[o], R.z_r.at[o], at(x, zpeer(o), c)
                )
                z_sends[o].start()

    for cp in e_sends:
        cp.wait_recv()
    sec_group_y(R, picked.astype(F32))
    r_sends = group(lambda to: R.yrs.at[to], R.yrb.at[c, z], R.r_s, R.r_r)
    R.yrb[c, z] = R.yrs[here]

    for cp in cz_sends:
        cp.wait_recv()
    sec_unpack(R, R.czbuf[owner_z].astype(F32))
    sec_conv(R)

    for o in (4, 3, 5, 2, 6, 1, 7):
        z_sends[o].wait_recv()
    R.fbuf[here] = R.zbuf[owner_z]
    g_sends, f_sends = {}, {}
    for d in (4, 3, 5, 2, 6, 1, 7):
        g_sends[d] = remote(
            R.fbuf.at[here], R.fbuf.at[here], R.g_s.at[d], R.g_r.at[d], at(x, zpeer(d), c)
        )
        g_sends[d].start()
    f_sends[0] = remote(R.fbuf.at[here], R.fbuf.at[here], R.f_s.at[0], R.f_r.at[0], sibling)
    f_sends[0].start()
    for i in (12, 13):
        loads[i].wait()
    sec_mix(R)
    sec_last(R)
    stores = [
        pltpu.make_async_copy(R.ssm, R.pre_out, R.out_sem.at[0]),
        pltpu.make_async_copy(R.ab.at[1], R.ab_out, R.out_sem.at[1]),
    ]
    for cp in stores:
        cp.start()

    for cp in r_sends:
        cp.wait_recv()
    R.ysend[...] = jnp.broadcast_to(sec_gate(R, refill, owner_z), R.ysend.shape)
    R.ybuf[y] = R.ysend[...]
    y_sends = []
    for d in (4, 3, 5, 2, 6, 1, 7) if ny == 8 else range(1, ny):
        cp = remote(R.ysend, R.ybuf.at[y], R.y_s.at[d], R.y_r.at[d], {"tensor": ypeer(d)})
        cp.start()
        y_sends.append(cp)

    for d in NEAR:
        g_sends[d].wait_recv()
        landed = c * HALF + zpeer(NZ - d)
        f_sends[d] = remote(R.fbuf.at[landed], R.fbuf.at[landed], R.f_s.at[d], R.f_r.at[d], sibling)
        f_sends[d].start()
    for d in (0,) + NEAR:
        f_sends[d].wait_recv()

    fork_copy = pltpu.make_async_copy(R.fbuf, R.fork_out, R.out_sem.at[2])
    fork_copy.start()
    for cp in list(plans.values()) + [pair, pair_conv] + conv_sends + cz_sends + e_sends + r_sends:
        cp.wait_send()
    for sends in x_sends:
        for cp in sends:
            cp.wait_send()
    for group in (z_sends, g_sends, f_sends):
        for cp in group.values():
            cp.wait_send()
    for cp in stores + [fork_copy]:
        cp.wait()

    for cp in y_sends:
        cp.wait_recv()
    total = R.ybuf[0]
    for i in range(1, ny):
        total += R.ybuf[i]
    scale = lax.rsqrt(total[:, 0:1] / TOTAL + 1e-05)
    normed = R.base[...] * scale * R.gain[...]
    for t in range(STEPS):
        R.out[t] = normed[2 * t : 2 * t + 2].astype(BF16)
    for cp in y_sends:
        cp.wait_send()


def put(out_ref, pre_ref, fork_ref, ab_ref, out_hbm, fs_hbm, fs, sem):
    copies = [pltpu.make_async_copy(out_ref, out_hbm, sem.at[0])]
    copies[0].start()
    for i in range(4):
        some = slice(4 * i, 4 * i + 4)
        for h in range(4 * i, 4 * i + 4):
            f = fork_ref[h].astype(F32)
            for s in range(2):
                fs[s, h] = pre_ref[s, h] + ab_ref[s, h : h + 1, :] * f
        cp = pltpu.make_async_copy(fs.at[:, some], fs_hbm.at[:, some], sem.at[1 + i])
        cp.start()
        copies.append(cp)
    for cp in copies:
        cp.wait()


def body(nx, ny, *args):
    args = list(args)
    args[3] = jnp.swapaxes(args[3], 0, 1)
    args[6] = jnp.swapaxes(args[6], 0, 1)
    for i in (14, 15, 16, 17):
        args[i] = args[i].reshape(1, -1)
    dma = pltpu.SemaphoreType.DMA
    vmem = pltpu.VMEM
    in_vmem = [args[i] for i in (2, 3, 4, 6, 7, 8, 9, 10, 11, 12, 13, 14, 15, 16, 17)]
    head = (WIDTH, STATES)
    scratch = [vmem(a.shape, a.dtype) for a in in_vmem]
    scratch += [pltpu.SMEM(a.shape, a.dtype) for a in args[:2]]
    scratch += [
        vmem((8, 128), jnp.int32),
        vmem((nx, 8, 128), jnp.int32),
        vmem((2 * HELD, HALF) + head, BF16),
        vmem((2 * HELD, 32, 128), BF16),
        vmem((HELD, 32, 128), F32),
        vmem((nx, 32, 128), BF16),
        vmem((nx, 32, 128), BF16),
        vmem((32, 128), BF16),
        vmem((NZ, 32, 128), BF16),
        vmem((nx, NZ) + head, BF16),
    ]
    scratch += [vmem((nx, len(o)) + head, BF16) for o in STAGES]
    scratch += [
        vmem((NZ,) + head, BF16),
        vmem((NZ,) + head, BF16),
        vmem((HEADS,) + head, BF16),
        vmem((8, 128), F32),
        vmem((ny, 8, 128), F32),
        vmem((6, 2, LANES), F32),
        vmem((8, LANES), F32),
        vmem((ROWS, LANES), F32),
        vmem((8, LANES), F32),
        vmem((16, 128), F32),
        vmem((16, CH), F32),
        vmem((ROWS, CH), F32),
        vmem((ROWS, CH), F32),
        vmem((ROWS, CH), F32),
        vmem((ROWS, CH), F32),
        vmem((ROWS, CH), F32),
        vmem((2, 2, HEADS, STATES), F32),
        vmem((8, STATES), F32),
        vmem((2 * NZ, 8, STATES), F32),
        vmem((HALF,) + head, BF16),
        vmem((2 * NZ, 16, 128), F32),
        vmem((2, NZ, 16, 128), F32),
        dma((len(in_vmem),)),
        dma((2,)),
        dma,
        dma((3,)),
        dma((nx,)),
        dma((nx,)),
        dma((2,)),
        dma((2,)),
        dma((nx,)),
        dma((nx,)),
        dma((NZ,)),
        dma((NZ,)),
        dma((len(STAGES), nx)),
        dma((len(STAGES), nx)),
        dma((NZ,)),
        dma((NZ,)),
        dma((NZ,)),
        dma((NZ,)),
        dma((NZ,)),
        dma((NZ,)),
        dma((2, NZ)),
        dma((2, NZ)),
        dma((2, NZ)),
        dma((2, NZ)),
        dma((ny,)),
        dma((ny,)),
    ]
    args = [pltpu.with_memory_space_constraint(a, pltpu.HBM) for a in args]
    anywhere = pl.BlockSpec(memory_space=pl.ANY)
    slots = args[0].shape[0]
    out, pre, fork, ab = pl.pallas_call(
        functools.partial(kernel, nx, ny),
        out_shape=(
            pltpu.VMEM((STEPS, slots, CH), BF16),
            pltpu.VMEM(args[2].shape, F32),
            pltpu.VMEM((HEADS,) + head, BF16),
            pltpu.VMEM((2, HEADS, STATES), F32),
        ),
        in_specs=[anywhere] * 18,
        out_specs=(pl.BlockSpec(memory_space=pltpu.VMEM), anywhere, anywhere, anywhere),
        scratch_shapes=scratch,
        compiler_params=pltpu.CompilerParams(
            collective_id=0, has_side_effects=True, vmem_limit_bytes=32 * 1024 * 1024
        ),
    )(*args)
    inside = pl.BlockSpec(memory_space=pltpu.VMEM)
    return pl.pallas_call(
        put,
        out_shape=(jax.ShapeDtypeStruct(out.shape, BF16), jax.ShapeDtypeStruct(pre.shape, F32)),
        in_specs=[anywhere, inside, inside, inside],
        out_specs=(anywhere, anywhere),
        scratch_shapes=[vmem(pre.shape, F32), dma((5,))],
        compiler_params=pltpu.CompilerParams(vmem_limit_bytes=16 * 1024 * 1024),
    )(out, pre, fork, ab)


def solution(mesh):
    nx = mesh.shape["dp"] // (2 * NZ)
    ny = mesh.shape["tensor"]
    return jax.shard_map(
        functools.partial(body, nx, ny),
        mesh=mesh,
        in_specs=(
            P("dp"),
            P("dp"),
            P("dp", "tensor", None, None),
            P("dp", None, "tensor"),
            P("dp", None, None, "tensor"),
            P("dp", "tensor", None, None),
            P("dp", None, "tensor"),
            P("dp", None, None, "tensor"),
            P(None, "dp", "tensor"),
            P(None, "dp", "tensor"),
            P(None, "dp", None, "tensor"),
            P(None, "dp", "tensor"),
            P(None, "tensor"),
            P(None, None, "tensor"),
            P("tensor"),
            P("tensor"),
            P("tensor"),
            P("tensor"),
        ),
        out_specs=(P(None, "dp", "tensor"), P("dp", "tensor", None, None)),
        check_vma=False,
    )
```

```python
import functools

import jax
import jax.numpy as jnp
from jax import lax
from jax.experimental import pallas as pl
from jax.experimental.pallas import tpu as pltpu
from jax.sharding import PartitionSpec as P

F32 = jnp.float32
BF16 = jnp.bfloat16
MESH = pl.DeviceIdType.MESH

NZ = 8
HELD = 4
HEADS = 16
HALF = 8
WIDTH = 64
STATES = 128
CH = HEADS * WIDTH
LANES = CH + 2 * STATES
STEPS = 3
TAPS = 4
ROWS = 8
TOTAL = 8192
STAGES = ((4, 3, 5), (2, 6, 7), (1, 0))
NEAR = (1, 7, 2, 6, 3, 5, 4)


def silu(v):
    return v * (1.0 / (1.0 + jnp.exp(-v)))


def softplus(v):
    return jnp.maximum(v, 0.0) + jnp.log1p(jnp.exp(-jnp.abs(v)))


def dot(a, b, da, db):
    return lax.dot_general(a, b, (((da,), (db,)), ((), ())), preferred_element_type=F32)


def split(v, n):
    parts = []
    for _ in range(n):
        hi = v.astype(BF16).astype(F32)
        parts.append(hi)
        v = v - hi
    return parts


def stack(parts, axis):
    return jnp.concatenate(parts, axis=axis).astype(BF16)


def sec_pack(R):
    for i in range(3):
        tap = R.pcx[i].astype(F32)
        for q in range(HELD):
            for k in range(8):
                r = 4 * k + i
                R.cpack[q, r : r + 1, :] = tap[q : q + 1, 128 * k : 128 * (k + 1)]
    for q in range(HELD):
        for i in range(3):
            for b in range(2):
                r = 4 * (2 * i + b) + 3
                R.cpack[q, r : r + 1, :] = R.pcbc[q, i, b : b + 1, :].astype(F32)


def sec_dt(R):
    for t in range(STEPS):
        R.st[2 * t : 2 * t + 2, :HEADS] = R.dtin[t]
    R.st[6:7, :HEADS] = R.bias[...]
    R.st[7:8, :HEADS] = R.alog[...]
    R.st[8:9, :HEADS] = R.skip[...]
    parts = split(R.st[:, :HEADS], 3)
    spread = (
        lax.broadcasted_iota(jnp.int32, (HEADS, CH), 1) // WIDTH
        == lax.broadcasted_iota(jnp.int32, (HEADS, CH), 0)
    ).astype(F32)
    full = dot(stack(parts, 1), stack([spread] * 3, 0), 1, 0)
    step = softplus(full[0:ROWS] + full[6:7])
    R.ex[0:ROWS] = step
    R.ex[8:9] = full[8:9]
    R.dec[...] = jnp.exp(-jnp.exp(full[7:8]) * step)


def sec_ab(R):
    pick = (
        lax.broadcasted_iota(jnp.int32, (16, 8 * STATES), 1) // STATES
        == lax.broadcasted_iota(jnp.int32, (16, 8 * STATES), 0)
    ).astype(F32)
    parts = split(R.st[:, :HEADS], 3)
    hb = dot(stack(parts, 0), stack([pick] * 3, 0), 0, 0)

    def col(r):
        return hb[:, r * STATES : (r + 1) * STATES]

    rate = -jnp.exp(col(7))
    for s in range(2):
        a = jnp.ones((HEADS, STATES), F32)
        b = jnp.zeros((HEADS, STATES), F32)
        fin = jnp.full((HEADS, STATES), R.fin[s], jnp.int32)
        for t in range(STEPS):
            d_t = jnp.exp(rate * softplus(col(2 * t + s) + col(6)))
            a = jnp.where(fin == t, 0.0, a) * d_t
            b = jnp.where(fin == t, 1.0, b) * d_t
        R.ab[0, s] = a
        R.ab[1, s] = b


def sec_seq(R):
    for i in range(3):
        R.seq[i, :, :CH] = R.cx[i].astype(F32)
        for s in range(2):
            for b in range(2):
                lo = CH + b * STATES
                R.seq[i, s : s + 1, lo : lo + STATES] = R.cbc[s, i, b : b + 1, :].astype(F32)
    for t in range(STEPS):
        R.seq[3 + t, :, :CH] = R.xin[t].astype(F32)
        for s in range(2):
            for b in range(2):
                lo = CH + b * STATES
                R.seq[3 + t, s : s + 1, lo : lo + STATES] = R.bcin[t, s, b : b + 1, :].astype(F32)
    R.wts[:TAPS, :CH] = R.cw[...]
    for k in range(TAPS):
        for b in range(2):
            lo = CH + b * STATES
            R.wts[k : k + 1, lo : lo + STATES] = R.cwbc[k, b : b + 1, :]


def sec_old(R):
    for t in range(STEPS):
        total = jnp.zeros((2, STATES), F32)
        for k in range(TAPS):
            total += R.wts[k : k + 1, CH + STATES :] * R.seq[t + k, :, CH + STATES :]
        R.acc[2 * t : 2 * t + 2, CH + STATES :] = total
    c_hi, c_lo = split(silu(R.acc[:, CH + STATES :]), 2)
    c_parts = stack([c_hi, c_lo], 0)
    ys = []
    for s in range(2):
        state = R.ssm[s].reshape(CH, STATES)
        hi = state.astype(BF16)
        lo = (state - hi.astype(F32)).astype(BF16)
        both = dot(c_parts, hi, 1, 1)
        ys.append(both[0:ROWS] + both[ROWS:] + dot(c_parts, lo, 1, 1)[0:ROWS])
    row = lax.broadcasted_iota(jnp.int32, (ROWS, CH), 0)
    R.base[...] = jnp.where(row >= 2 * STEPS, 0.0, jnp.where(lax.rem(row, 2) == 0, ys[0], ys[1]))


def sec_unpack(R, packed):
    for k in range(8):
        R.fork[0:3, 128 * k : 128 * (k + 1)] = packed[4 * k : 4 * k + 3]
    for i in range(3):
        for b in range(2):
            r = 4 * (2 * i + b) + 3
            lo = CH + b * STATES
            R.fork[i : i + 1, lo : lo + STATES] = packed[r : r + 1]


def fin_rows(R, lanes):
    first = lax.broadcasted_iota(jnp.int32, (2, lanes), 0) == 0
    return jnp.where(first, R.fin[0], R.fin[1])


def sec_conv(R):
    fin = fin_rows(R, LANES)
    for t in range(STEPS):
        total = jnp.zeros((2, LANES), F32)
        for k in range(TAPS):
            w = R.seq[t + k]
            for f in range(t + 1):
                if t + k - f <= 2:
                    r = t + k - f
                    w = jnp.where(fin == f, R.fork[r : r + 1, :], w)
            total += R.wts[k : k + 1, :] * w
        R.acc[2 * t : 2 * t + 2, :] = total
    R.acc[...] = silu(R.acc[...])


def sec_mix(R):
    fin = fin_rows(R, CH)
    a = jnp.ones((2, CH), F32)
    b = jnp.zeros((2, CH), F32)
    gs = []
    for t in range(STEPS):
        two = slice(2 * t, 2 * t + 2)
        now = fin == t
        d_t = R.dec[two]
        a = jnp.where(now, 0.0, a) * d_t
        b = jnp.where(now, 1.0, b) * d_t
        x_t = R.acc[two, :CH]
        u = R.ex[two] * x_t
        gs = [jnp.where(now, 0.0, v) * d_t for v in gs] + [u]
        c_t = R.acc[two, CH + STATES :]
        total = a * R.base[two] + R.ex[8:9] * x_t
        for k in range(t + 1):
            b_k = R.acc[2 * k : 2 * k + 2, CH : CH + STATES]
            total += gs[k] * jnp.sum(b_k * c_t, axis=1, keepdims=True)
        R.base[two] = total
        R.bco[two] = b
    for k in range(STEPS):
        R.gub[2 * k : 2 * k + 2] = gs[k]
    for t in range(STEPS):
        R.gate[2 * t : 2 * t + 2] = silu(R.zin[t].astype(F32))


def sec_last(R):
    bm = R.acc[:, CH : CH + STATES]
    odd = lax.rem(lax.broadcasted_iota(jnp.int32, (ROWS, STATES), 0), 2)
    both = jnp.concatenate([jnp.where(odd == 0, bm, 0.0), jnp.where(odd == 1, bm, 0.0)], axis=1)
    b_hi, b_lo = split(both, 2)
    g_hi, g_lo = split(R.gub[...], 2)
    rhs = stack([b_hi, b_hi, b_lo, b_lo], 0)
    lhs = stack([g_hi, g_lo, g_hi, g_lo], 0)
    u = dot(lhs, rhs, 0, 0)
    for h in range(HEADS):
        for s in range(2):
            R.ssm[s, h] = (
                R.ab[0, s, h : h + 1, :] * R.ssm[s, h]
                + u[h * WIDTH : (h + 1) * WIDTH, s * STATES : (s + 1) * STATES]
            )


def sec_own_c(R, f):
    rows = [
        jnp.where(R.fin[0] < STEPS, R.bcin[t, 0, 1:2, :].astype(F32), R.bcin[t, 1, 1:2, :].astype(F32))
        for t in range(STEPS)
    ]
    after = [
        jnp.where(f == 0, rows[0], jnp.where(f == 1, rows[1], rows[2])),
        jnp.where(f == 0, rows[1], rows[2]),
        rows[2],
    ]
    for n in range(STEPS):
        total = jnp.zeros((1, STATES), F32)
        for i in range(n + 1):
            total += R.cwbc[i + 3 - n, 1:2, :] * after[i]
        R.esend[n : n + 1] = total
        R.esend[n + 4 : n + 5] = total


def sec_group_y(R, packed):
    fork_c = [packed[4 * (2 * i + 1) + 3 : 4 * (2 * i + 1) + 4] for i in range(3)]
    zero = jnp.zeros((1, STATES), F32)
    adds = []
    for n in range(STEPS):
        total = zero
        for k in range(3 - n):
            total += R.cwbc[k, 1:2, :] * fork_c[n + k]
        adds.append(total)
    adds = jnp.concatenate((adds + [zero]) * 2, axis=0)
    cs = silu(R.ebuf[...] + adds[None]).reshape(2 * NZ * 8, STATES)
    y = dot(stack(split(cs, 2), 0), R.hbuf[...].reshape(HALF * WIDTH, STATES), 1, 1)
    y = (y[: 2 * NZ * 8] + y[2 * NZ * 8 :]).reshape(2 * NZ, 8, HALF * WIDTH)
    top = lax.broadcasted_iota(jnp.int32, (2 * NZ, 8, 128), 1) < 4
    for i in range(2):
        lo = 256 * i
        R.yrs[:, 8 * i : 8 * i + 8, :] = jnp.where(
            top, y[:, :, lo : lo + 128], y[:, :, lo + 128 : lo + 256]
        )


def sec_gate(R, f, owner_z):
    rows = []
    for n in range(STEPS):
        rows.append(
            jnp.concatenate(
                [
                    R.yrb[cc, owner_z, 8 * i + 4 * j + n : 8 * i + 4 * j + n + 1, :]
                    for cc in range(2)
                    for i in range(2)
                    for j in range(2)
                ],
                axis=1,
            )
        )
    at_step = [
        rows[0],
        jnp.where(f == 0, rows[1], rows[0]),
        jnp.where(f == 0, rows[2], jnp.where(f == 1, rows[1], rows[0])),
    ]
    for t in range(STEPS):
        two = slice(2 * t, 2 * t + 2)
        R.base[two] = (R.base[two] + R.bco[two] * at_step[t]) * R.gate[two]
    gated = R.base[...]
    return jnp.sum(gated * gated, axis=1, keepdims=True)


NAMES = (
    "fin_hbm",
    "src_hbm",
    "ssm_hbm",
    "cx_hbm",
    "cbc_hbm",
    "pssm_hbm",
    "pcx_hbm",
    "pcbc_hbm",
    "x_hbm",
    "z_hbm",
    "bc_hbm",
    "dt_hbm",
    "cw_hbm",
    "cwbc_hbm",
    "bias_hbm",
    "alog_hbm",
    "skip_hbm",
    "gain_hbm",
    "out",
    "pre_out",
    "fork_out",
    "ab_out",
    "ssm",
    "cx",
    "cbc",
    "pcx",
    "pcbc",
    "xin",
    "zin",
    "bcin",
    "dtin",
    "cw",
    "cwbc",
    "bias",
    "alog",
    "skip",
    "gain",
    "fin",
    "src",
    "plan_out",
    "plan_in",
    "pbuf",
    "pconv",
    "cpack",
    "csend",
    "cxbuf",
    "czsend",
    "czbuf",
    "sbuf",
    *(f"xb{g}" for g in range(len(STAGES))),
    "zsend",
    "zbuf",
    "fbuf",
    "ysend",
    "ybuf",
    "seq",
    "fork",
    "acc",
    "wts",
    "st",
    "ex",
    "dec",
    "base",
    "bco",
    "gub",
    "gate",
    "ab",
    "esend",
    "ebuf",
    "hbuf",
    "yrs",
    "yrb",
    "in_sem",
    "sc_sem",
    "own_sem",
    "out_sem",
    "plan_s",
    "plan_r",
    "pair_s",
    "pair_r",
    "cx_s",
    "cx_r",
    "cz_s",
    "cz_r",
    "x_s",
    "x_r",
    "z_s",
    "z_r",
    "g_s",
    "g_r",
    "f_s",
    "f_r",
    "zrel",
    "yrel",
    "e_s",
    "e_r",
    "r_s",
    "r_r",
    "y_s",
    "y_r",
)


class Refs:
    pass


def kernel(nx, ny, *refs):
    R = Refs()
    for name, ref in zip(NAMES, refs, strict=True):
        setattr(R, name, ref)
    me = lax.axis_index("dp")
    c = lax.rem(me, 2)
    z = lax.rem(me // 2, NZ)
    x = me // (2 * NZ)
    y = lax.axis_index("tensor")
    xbs = [getattr(R, f"xb{g}") for g in range(len(STAGES))]

    def at(xx, zz, cc):
        return {"dp": (xx * NZ + zz) * 2 + cc}

    def xpeer(d):
        return lax.rem(x + d, nx)

    def zpeer(d):
        return lax.rem(z + d, NZ)

    def ypeer(d):
        return lax.rem(y + d, ny)

    sibling = at(x, z, 1 - c)

    def remote(src, dst, ssem, rsem, dev):
        return pltpu.make_async_remote_copy(
            src_ref=src, dst_ref=dst, send_sem=ssem, recv_sem=rsem, device_id=dev, device_id_type=MESH
        )

    barrier = pltpu.get_barrier_semaphore()
    for d in range(1, nx):
        pl.semaphore_signal(barrier, inc=1, device_id=at(xpeer(d), z, c), device_id_type=MESH)
    scalars = [
        pltpu.make_async_copy(R.fin_hbm, R.fin, R.sc_sem.at[0]),
        pltpu.make_async_copy(R.src_hbm, R.src, R.sc_sem.at[1]),
    ]
    for cp in scalars:
        cp.start()
    around = [(R.zrel, at(x, zpeer(1), c), at(x, zpeer(NZ - 1), c))]
    if ny > 1:
        around.append((R.yrel, {"tensor": ypeer(1)}, {"tensor": ypeer(ny - 1)}))
    for _, up, down in around:
        pl.semaphore_signal(barrier, inc=1, device_id=up, device_id_type=MESH)
        pl.semaphore_signal(barrier, inc=1, device_id=down, device_id_type=MESH)
    pl.semaphore_signal(barrier, inc=1, device_id=sibling, device_id_type=MESH)

    def tell(n):
        for sem, up, down in around:
            pl.semaphore_signal(sem.at[n, 0], inc=1, device_id=up, device_id_type=MESH)
            pl.semaphore_signal(sem.at[n, 1], inc=1, device_id=down, device_id_type=MESH)

    def hear(n):
        for sem, _, _ in around:
            pl.semaphore_wait(sem.at[n, 0], 1)
            pl.semaphore_wait(sem.at[n, 1], 1)

    mine = pl.ds(pl.multiple_of(c * HALF, HALF), HALF)
    theirs = pl.ds(pl.multiple_of((1 - c) * HALF, HALF), HALF)
    my_slot = pl.ds(pl.multiple_of(c * HELD, HELD), HELD)
    loads = [
        pltpu.make_async_copy(src, dst, R.in_sem.at[i])
        for i, (src, dst) in enumerate(
            (
                (R.pcx_hbm, R.pcx),
                (R.pcbc_hbm, R.pcbc),
                (R.dt_hbm, R.dtin),
                (R.bias_hbm, R.bias),
                (R.alog_hbm, R.alog),
                (R.skip_hbm, R.skip),
                (R.cx_hbm, R.cx),
                (R.cbc_hbm, R.cbc),
                (R.x_hbm, R.xin),
                (R.bc_hbm, R.bcin),
                (R.cw_hbm, R.cw),
                (R.cwbc_hbm, R.cwbc),
                (R.z_hbm, R.zin),
                (R.gain_hbm, R.gain),
                (R.ssm_hbm, R.ssm),
            )
        )
    ]
    own = pltpu.make_async_copy(R.pssm_hbm.at[:, mine], R.pbuf.at[my_slot], R.own_sem)
    for cp in scalars:
        cp.wait()
    prompt = jnp.where(R.fin[0] < STEPS, R.src[0], R.src[1])
    refill = jnp.where(R.fin[0] < STEPS, R.fin[0], R.fin[1])
    R.plan_out[...] = jnp.full(R.plan_out.shape, prompt, jnp.int32)

    pl.semaphore_wait(barrier, 1 + (nx - 1) + 2 * len(around))

    order = (2, 1, 3) if nx == 4 else tuple(range(1, nx))
    plans = {}
    for d in order:
        plans[d] = remote(
            R.plan_out, R.plan_in.at[d], R.plan_s.at[d], R.plan_r.at[d], at(xpeer(d), z, c)
        )
        plans[d].start()
    tell(0)
    pair = remote(R.pssm_hbm.at[:, theirs], R.pbuf.at[my_slot], R.pair_s.at[0], R.pair_r.at[0], sibling)
    pair.start()
    for cp in [loads[9], loads[11], loads[0], loads[1], own] + loads[2:9] + [loads[10]] + loads[12:]:
        cp.start()
    for ref in (R.wts, R.st, R.acc, R.base, R.bco, R.gub, R.gate, R.esend):
        ref[...] = jnp.zeros_like(ref)
    loads[9].wait()
    loads[11].wait()
    sec_own_c(R, refill)
    here = c * NZ + z
    R.ebuf[here] = R.esend[...]

    def group(src, dst, ssem, rsem):
        sends = []
        for d in (4, 3, 5, 2, 6, 1, 7, 0):
            for k in (0, 1) if d else (1,):
                cc = c if k == 0 else 1 - c
                to = cc * NZ + zpeer(d)
                cp = remote(src(to), dst, ssem.at[k, d], rsem.at[k, d], at(x, zpeer(d), cc))
                cp.start()
                sends.append(cp)
        return sends

    loads[0].wait()
    loads[1].wait()
    sec_pack(R)
    R.pconv[my_slot] = R.cpack[...].astype(BF16)
    pair_conv = remote(
        R.pconv.at[my_slot], R.pconv.at[my_slot], R.pair_s.at[1], R.pair_r.at[1], sibling
    )
    pair_conv.start()

    for i in range(2, 6):
        loads[i].wait()
    sec_dt(R)
    sec_ab(R)

    hear(0)
    tell(1)
    pair.wait_recv()
    pair_conv.wait_recv()
    own.wait()
    for d in order:
        plans[d].wait_recv()

    def wanted(d):
        return lax.rem(R.plan_in[nx - d, 0, 0], 2 * HELD)

    want = {d: wanted(d) for d in order}
    want[0] = lax.rem(prompt, 2 * HELD)
    owner_x = prompt // (2 * HELD * NZ)
    owner_z = lax.rem(prompt // (2 * HELD), NZ)

    conv_sends = []
    for i, d in enumerate(order):
        R.csend[i] = R.pconv[want[d]]
        cp = remote(R.csend.at[i], R.cxbuf.at[x], R.cx_s.at[d], R.cx_r.at[d], at(xpeer(d), z, c))
        cp.start()
        conv_sends.append(cp)
    starts = [sum(len(o) for o in STAGES[:g]) for g in range(len(STAGES))]
    x_sends = []
    for g, offsets in enumerate(STAGES):
        sends = []
        for i, d in enumerate(order):
            for n, o in enumerate(offsets):
                R.sbuf[i, starts[g] + n] = R.pbuf[want[d], zpeer(o)]
            part = R.sbuf.at[i, starts[g] : starts[g] + len(offsets)]
            cp = remote(
                part, xbs[g].at[x], R.x_s.at[g, d], R.x_r.at[g, d], at(xpeer(d), z, c)
            )
            cp.start()
            sends.append(cp)
        x_sends.append(sends)
    R.cxbuf[x] = R.pconv[want[0]]
    for g, offsets in enumerate(STAGES):
        for n, o in enumerate(offsets):
            xbs[g][x, n] = R.pbuf[want[0], zpeer(o)]

    for i in (6, 7, 8, 10):
        loads[i].wait()
    sec_seq(R)

    hear(1)
    tell(2)
    hear(2)
    e_sends = []
    for d in (4, 3, 5, 2, 6, 1, 7):
        cp = remote(R.esend, R.ebuf.at[here], R.e_s.at[d], R.e_r.at[d], at(x, zpeer(d), c))
        cp.start()
        e_sends.append(cp)

    for cp in conv_sends:
        cp.wait_recv()
    picked = R.cxbuf[owner_x]
    R.czsend[...] = picked
    R.czbuf[z] = picked
    cz_sends = []
    for d in (4, 3, 5, 2, 6, 1, 7):
        cp = remote(R.czsend, R.czbuf.at[z], R.cz_s.at[d], R.cz_r.at[d], at(x, zpeer(d), c))
        cp.start()
        cz_sends.append(cp)
    loads[14].wait()
    sec_old(R)

    for cp in e_sends:
        cp.wait_recv()
    swap_c = remote(R.ebuf.at[mine], R.ebuf.at[mine], R.e_s.at[0], R.e_r.at[0], sibling)
    swap_c.start()

    z_sends = {}
    for g, offsets in enumerate(STAGES):
        for cp in x_sends[g]:
            cp.wait_recv()
        for n, o in enumerate(offsets):
            head = xbs[g][owner_x, n]
            R.hbuf[zpeer(o)] = head
            if o == 0:
                R.zbuf[z] = head
            else:
                R.zsend[o] = head
                z_sends[o] = remote(
                    R.zsend.at[o], R.zbuf.at[z], R.z_s.at[o], R.z_r.at[o], at(x, zpeer(o), c)
                )
                z_sends[o].start()

    swap_c.wait_recv()
    sec_group_y(R, picked.astype(F32))
    r_sends = group(lambda to: R.yrs.at[to], R.yrb.at[c, z], R.r_s, R.r_r)
    R.yrb[c, z] = R.yrs[here]

    for cp in cz_sends:
        cp.wait_recv()
    sec_unpack(R, R.czbuf[owner_z].astype(F32))
    sec_conv(R)

    for o in (4, 3, 5, 2, 6, 1, 7):
        z_sends[o].wait_recv()
    R.fbuf[here] = R.zbuf[owner_z]
    g_sends = {}
    for d in (4, 3, 5, 2, 6, 1, 7):
        g_sends[d] = remote(
            R.fbuf.at[here], R.fbuf.at[here], R.g_s.at[d], R.g_r.at[d], at(x, zpeer(d), c)
        )
        g_sends[d].start()
    for i in (12, 13):
        loads[i].wait()
    sec_mix(R)
    sec_last(R)
    stores = [
        pltpu.make_async_copy(R.ssm, R.pre_out, R.out_sem.at[0]),
        pltpu.make_async_copy(R.ab.at[1], R.ab_out, R.out_sem.at[1]),
    ]
    for cp in stores:
        cp.start()

    for cp in r_sends:
        cp.wait_recv()
    R.ysend[...] = jnp.broadcast_to(sec_gate(R, refill, owner_z), R.ysend.shape)
    R.ybuf[y] = R.ysend[...]
    y_sends = []
    for d in (4, 3, 5, 2, 6, 1, 7) if ny == 8 else range(1, ny):
        cp = remote(R.ysend, R.ybuf.at[y], R.y_s.at[d], R.y_r.at[d], {"tensor": ypeer(d)})
        cp.start()
        y_sends.append(cp)

    for d in NEAR:
        g_sends[d].wait_recv()
    swap = remote(R.fbuf.at[mine], R.fbuf.at[mine], R.f_s, R.f_r, sibling)
    swap.start()
    stores.append(pltpu.make_async_copy(R.fbuf.at[mine], R.fork_out.at[mine], R.out_sem.at[2]))
    stores[-1].start()
    swap.wait_recv()
    stores.append(pltpu.make_async_copy(R.fbuf.at[theirs], R.fork_out.at[theirs], R.out_sem.at[3]))
    stores[-1].start()
    for cp in list(plans.values()) + [pair, pair_conv] + conv_sends + cz_sends + e_sends + r_sends + [swap_c]:
        cp.wait_send()
    for sends in x_sends:
        for cp in sends:
            cp.wait_send()
    for sends in (z_sends, g_sends):
        for cp in sends.values():
            cp.wait_send()
    swap.wait_send()
    for cp in stores:
        cp.wait()

    for cp in y_sends:
        cp.wait_recv()
    total = R.ybuf[0]
    for i in range(1, ny):
        total += R.ybuf[i]
    scale = lax.rsqrt(total[:, 0:1] / TOTAL + 1e-05)
    normed = R.base[...] * scale * R.gain[...]
    for t in range(STEPS):
        R.out[t] = normed[2 * t : 2 * t + 2].astype(BF16)
    for cp in y_sends:
        cp.wait_send()


def put(out_ref, pre_ref, fork_ref, ab_ref, out_hbm, fs_hbm, fs, sem):
    copies = [pltpu.make_async_copy(out_ref, out_hbm, sem.at[0])]
    copies[0].start()
    for i in range(4):
        some = slice(4 * i, 4 * i + 4)
        for h in range(4 * i, 4 * i + 4):
            f = fork_ref[h].astype(F32)
            for s in range(2):
                fs[s, h] = pre_ref[s, h] + ab_ref[s, h : h + 1, :] * f
        cp = pltpu.make_async_copy(fs.at[:, some], fs_hbm.at[:, some], sem.at[1 + i])
        cp.start()
        copies.append(cp)
    for cp in copies:
        cp.wait()


def body(nx, ny, *args):
    args = list(args)
    args[3] = jnp.swapaxes(args[3], 0, 1)
    args[6] = jnp.swapaxes(args[6], 0, 1)
    for i in (14, 15, 16, 17):
        args[i] = args[i].reshape(1, -1)
    dma = pltpu.SemaphoreType.DMA
    vmem = pltpu.VMEM
    in_vmem = [args[i] for i in (2, 3, 4, 6, 7, 8, 9, 10, 11, 12, 13, 14, 15, 16, 17)]
    head = (WIDTH, STATES)
    scratch = [vmem(a.shape, a.dtype) for a in in_vmem]
    scratch += [pltpu.SMEM(a.shape, a.dtype) for a in args[:2]]
    scratch += [
        vmem((8, 128), jnp.int32),
        vmem((nx, 8, 128), jnp.int32),
        vmem((2 * HELD, HALF) + head, BF16),
        vmem((2 * HELD, 32, 128), BF16),
        vmem((HELD, 32, 128), F32),
        vmem((nx, 32, 128), BF16),
        vmem((nx, 32, 128), BF16),
        vmem((32, 128), BF16),
        vmem((NZ, 32, 128), BF16),
        vmem((nx, NZ) + head, BF16),
    ]
    scratch += [vmem((nx, len(o)) + head, BF16) for o in STAGES]
    scratch += [
        vmem((NZ,) + head, BF16),
        vmem((NZ,) + head, BF16),
        vmem((HEADS,) + head, BF16),
        vmem((8, 128), F32),
        vmem((ny, 8, 128), F32),
        vmem((6, 2, LANES), F32),
        vmem((8, LANES), F32),
        vmem((ROWS, LANES), F32),
        vmem((8, LANES), F32),
        vmem((16, 128), F32),
        vmem((16, CH), F32),
        vmem((ROWS, CH), F32),
        vmem((ROWS, CH), F32),
        vmem((ROWS, CH), F32),
        vmem((ROWS, CH), F32),
        vmem((ROWS, CH), F32),
        vmem((2, 2, HEADS, STATES), F32),
        vmem((8, STATES), F32),
        vmem((2 * NZ, 8, STATES), F32),
        vmem((HALF,) + head, BF16),
        vmem((2 * NZ, 16, 128), F32),
        vmem((2, NZ, 16, 128), F32),
        dma((len(in_vmem),)),
        dma((2,)),
        dma,
        dma((4,)),
        dma((nx,)),
        dma((nx,)),
        dma((2,)),
        dma((2,)),
        dma((nx,)),
        dma((nx,)),
        dma((NZ,)),
        dma((NZ,)),
        dma((len(STAGES), nx)),
        dma((len(STAGES), nx)),
        dma((NZ,)),
        dma((NZ,)),
        dma((NZ,)),
        dma((NZ,)),
        dma,
        dma,
        pltpu.SemaphoreType.REGULAR((3, 2)),
        pltpu.SemaphoreType.REGULAR((3, 2)),
        dma((NZ,)),
        dma((NZ,)),
        dma((2, NZ)),
        dma((2, NZ)),
        dma((ny,)),
        dma((ny,)),
    ]
    args = [pltpu.with_memory_space_constraint(a, pltpu.HBM) for a in args]
    anywhere = pl.BlockSpec(memory_space=pl.ANY)
    slots = args[0].shape[0]
    out, pre, fork, ab = pl.pallas_call(
        functools.partial(kernel, nx, ny),
        out_shape=(
            pltpu.VMEM((STEPS, slots, CH), BF16),
            pltpu.VMEM(args[2].shape, F32),
            pltpu.VMEM((HEADS,) + head, BF16),
            pltpu.VMEM((2, HEADS, STATES), F32),
        ),
        in_specs=[anywhere] * 18,
        out_specs=(pl.BlockSpec(memory_space=pltpu.VMEM), anywhere, anywhere, anywhere),
        scratch_shapes=scratch,
        compiler_params=pltpu.CompilerParams(
            collective_id=0, has_side_effects=True, vmem_limit_bytes=32 * 1024 * 1024
        ),
    )(*args)
    inside = pl.BlockSpec(memory_space=pltpu.VMEM)
    return pl.pallas_call(
        put,
        out_shape=(jax.ShapeDtypeStruct(out.shape, BF16), jax.ShapeDtypeStruct(pre.shape, F32)),
        in_specs=[anywhere, inside, inside, inside],
        out_specs=(anywhere, anywhere),
        scratch_shapes=[vmem(pre.shape, F32), dma((5,))],
        compiler_params=pltpu.CompilerParams(vmem_limit_bytes=16 * 1024 * 1024),
    )(out, pre, fork, ab)


def solution(mesh):
    nx = mesh.shape["dp"] // (2 * NZ)
    ny = mesh.shape["tensor"]
    return jax.shard_map(
        functools.partial(body, nx, ny),
        mesh=mesh,
        in_specs=(
            P("dp"),
            P("dp"),
            P("dp", "tensor", None, None),
            P("dp", None, "tensor"),
            P("dp", None, None, "tensor"),
            P("dp", "tensor", None, None),
            P("dp", None, "tensor"),
            P("dp", None, None, "tensor"),
            P(None, "dp", "tensor"),
            P(None, "dp", "tensor"),
            P(None, "dp", None, "tensor"),
            P(None, "dp", "tensor"),
            P(None, "tensor"),
            P(None, None, "tensor"),
            P("tensor"),
            P("tensor"),
            P("tensor"),
            P("tensor"),
        ),
        out_specs=(P(None, "dp", "tensor"), P("dp", "tensor", None, None)),
        check_vma=False,
    )
```

```python
import functools

import jax
import jax.numpy as jnp
from jax import lax
from jax.experimental import pallas as pl
from jax.experimental.pallas import tpu as pltpu
from jax.sharding import PartitionSpec as P

F32 = jnp.float32
BF16 = jnp.bfloat16
MESH = pl.DeviceIdType.MESH

NZ = 8
HELD = 4
HEADS = 16
HALF = 8
WIDTH = 64
STATES = 128
CH = HEADS * WIDTH
LANES = CH + 2 * STATES
STEPS = 3
TAPS = 4
ROWS = 8
TOTAL = 8192
STAGES = ((4, 3, 5), (2, 6, 7), (1, 0))
NEAR = (1, 7, 2, 6, 3, 5, 4)


def silu(v):
    return v * (1.0 / (1.0 + jnp.exp(-v)))


def softplus(v):
    return jnp.maximum(v, 0.0) + jnp.log1p(jnp.exp(-jnp.abs(v)))


def dot(a, b, da, db):
    return lax.dot_general(a, b, (((da,), (db,)), ((), ())), preferred_element_type=F32)


def split(v, n):
    parts = []
    for _ in range(n):
        hi = v.astype(BF16).astype(F32)
        parts.append(hi)
        v = v - hi
    return parts


def stack(parts, axis):
    return jnp.concatenate(parts, axis=axis).astype(BF16)


def sec_pack(R):
    for i in range(3):
        tap = R.pcx[i].astype(F32)
        for q in range(HELD):
            for k in range(8):
                r = 4 * k + i
                R.cpack[q, r : r + 1, :] = tap[q : q + 1, 128 * k : 128 * (k + 1)]
    for q in range(HELD):
        for i in range(3):
            for b in range(2):
                r = 4 * (2 * i + b) + 3
                R.cpack[q, r : r + 1, :] = R.pcbc[q, i, b : b + 1, :].astype(F32)


def sec_dt(R):
    for t in range(STEPS):
        R.st[2 * t : 2 * t + 2, :HEADS] = R.dtin[t]
    R.st[6:7, :HEADS] = R.bias[...]
    R.st[7:8, :HEADS] = R.alog[...]
    R.st[8:9, :HEADS] = R.skip[...]
    parts = split(R.st[:, :HEADS], 3)
    spread = (
        lax.broadcasted_iota(jnp.int32, (HEADS, CH), 1) // WIDTH
        == lax.broadcasted_iota(jnp.int32, (HEADS, CH), 0)
    ).astype(F32)
    full = dot(stack(parts, 1), stack([spread] * 3, 0), 1, 0)
    step = softplus(full[0:ROWS] + full[6:7])
    R.ex[0:ROWS] = step
    R.ex[8:9] = full[8:9]
    R.dec[...] = jnp.exp(-jnp.exp(full[7:8]) * step)


def sec_ab(R):
    pick = (
        lax.broadcasted_iota(jnp.int32, (16, 8 * STATES), 1) // STATES
        == lax.broadcasted_iota(jnp.int32, (16, 8 * STATES), 0)
    ).astype(F32)
    parts = split(R.st[:, :HEADS], 3)
    hb = dot(stack(parts, 0), stack([pick] * 3, 0), 0, 0)

    def col(r):
        return hb[:, r * STATES : (r + 1) * STATES]

    rate = -jnp.exp(col(7))
    for s in range(2):
        a = jnp.ones((HEADS, STATES), F32)
        b = jnp.zeros((HEADS, STATES), F32)
        fin = jnp.full((HEADS, STATES), R.fin[s], jnp.int32)
        for t in range(STEPS):
            d_t = jnp.exp(rate * softplus(col(2 * t + s) + col(6)))
            a = jnp.where(fin == t, 0.0, a) * d_t
            b = jnp.where(fin == t, 1.0, b) * d_t
        R.ab[0, s] = a
        R.ab[1, s] = b


def sec_seq(R):
    for i in range(3):
        R.seq[i, :, :CH] = R.cx[i].astype(F32)
        for s in range(2):
            for b in range(2):
                lo = CH + b * STATES
                R.seq[i, s : s + 1, lo : lo + STATES] = R.cbc[s, i, b : b + 1, :].astype(F32)
    for t in range(STEPS):
        R.seq[3 + t, :, :CH] = R.xin[t].astype(F32)
        for s in range(2):
            for b in range(2):
                lo = CH + b * STATES
                R.seq[3 + t, s : s + 1, lo : lo + STATES] = R.bcin[t, s, b : b + 1, :].astype(F32)
    R.wts[:TAPS, :CH] = R.cw[...]
    for k in range(TAPS):
        for b in range(2):
            lo = CH + b * STATES
            R.wts[k : k + 1, lo : lo + STATES] = R.cwbc[k, b : b + 1, :]


def sec_old(R):
    for t in range(STEPS):
        total = jnp.zeros((2, STATES), F32)
        for k in range(TAPS):
            total += R.wts[k : k + 1, CH + STATES :] * R.seq[t + k, :, CH + STATES :]
        R.acc[2 * t : 2 * t + 2, CH + STATES :] = total
    c_hi, c_lo = split(silu(R.acc[:, CH + STATES :]), 2)
    c_parts = stack([c_hi, c_lo], 0)
    ys = []
    for s in range(2):
        state = R.ssm[s].reshape(CH, STATES)
        hi = state.astype(BF16)
        lo = (state - hi.astype(F32)).astype(BF16)
        both = dot(c_parts, hi, 1, 1)
        ys.append(both[0:ROWS] + both[ROWS:] + dot(c_parts, lo, 1, 1)[0:ROWS])
    row = lax.broadcasted_iota(jnp.int32, (ROWS, CH), 0)
    R.base[...] = jnp.where(row >= 2 * STEPS, 0.0, jnp.where(lax.rem(row, 2) == 0, ys[0], ys[1]))


def sec_unpack(R, packed):
    for k in range(8):
        R.fork[0:3, 128 * k : 128 * (k + 1)] = packed[4 * k : 4 * k + 3]
    for i in range(3):
        for b in range(2):
            r = 4 * (2 * i + b) + 3
            lo = CH + b * STATES
            R.fork[i : i + 1, lo : lo + STATES] = packed[r : r + 1]


def fin_rows(R, lanes):
    first = lax.broadcasted_iota(jnp.int32, (2, lanes), 0) == 0
    return jnp.where(first, R.fin[0], R.fin[1])


def sec_conv(R):
    fin = fin_rows(R, LANES)
    for t in range(STEPS):
        total = jnp.zeros((2, LANES), F32)
        for k in range(TAPS):
            w = R.seq[t + k]
            for f in range(t + 1):
                if t + k - f <= 2:
                    r = t + k - f
                    w = jnp.where(fin == f, R.fork[r : r + 1, :], w)
            total += R.wts[k : k + 1, :] * w
        R.acc[2 * t : 2 * t + 2, :] = total
    R.acc[...] = silu(R.acc[...])


def sec_mix(R):
    fin = fin_rows(R, CH)
    a = jnp.ones((2, CH), F32)
    b = jnp.zeros((2, CH), F32)
    gs = []
    for t in range(STEPS):
        two = slice(2 * t, 2 * t + 2)
        now = fin == t
        d_t = R.dec[two]
        a = jnp.where(now, 0.0, a) * d_t
        b = jnp.where(now, 1.0, b) * d_t
        x_t = R.acc[two, :CH]
        u = R.ex[two] * x_t
        gs = [jnp.where(now, 0.0, v) * d_t for v in gs] + [u]
        c_t = R.acc[two, CH + STATES :]
        total = a * R.base[two] + R.ex[8:9] * x_t
        for k in range(t + 1):
            b_k = R.acc[2 * k : 2 * k + 2, CH : CH + STATES]
            total += gs[k] * jnp.sum(b_k * c_t, axis=1, keepdims=True)
        R.base[two] = total
        R.bco[two] = b
    for k in range(STEPS):
        R.gub[2 * k : 2 * k + 2] = gs[k]
    for t in range(STEPS):
        R.gate[2 * t : 2 * t + 2] = silu(R.zin[t].astype(F32))


def sec_last(R):
    bm = R.acc[:, CH : CH + STATES]
    odd = lax.rem(lax.broadcasted_iota(jnp.int32, (ROWS, STATES), 0), 2)
    both = jnp.concatenate([jnp.where(odd == 0, bm, 0.0), jnp.where(odd == 1, bm, 0.0)], axis=1)
    b_hi, b_lo = split(both, 2)
    g_hi, g_lo = split(R.gub[...], 2)
    rhs = stack([b_hi, b_hi, b_lo, b_lo], 0)
    lhs = stack([g_hi, g_lo, g_hi, g_lo], 0)
    u = dot(lhs, rhs, 0, 0)
    for h in range(HEADS):
        for s in range(2):
            R.ssm[s, h] = (
                R.ab[0, s, h : h + 1, :] * R.ssm[s, h]
                + u[h * WIDTH : (h + 1) * WIDTH, s * STATES : (s + 1) * STATES]
            )


def sec_own_c(R, f):
    rows = [
        jnp.where(R.fin[0] < STEPS, R.bcin[t, 0, 1:2, :].astype(F32), R.bcin[t, 1, 1:2, :].astype(F32))
        for t in range(STEPS)
    ]
    after = [
        jnp.where(f == 0, rows[0], jnp.where(f == 1, rows[1], rows[2])),
        jnp.where(f == 0, rows[1], rows[2]),
        rows[2],
    ]
    for n in range(STEPS):
        total = jnp.zeros((1, STATES), F32)
        for i in range(n + 1):
            total += R.cwbc[i + 3 - n, 1:2, :] * after[i]
        R.esend[n : n + 1] = total
        R.esend[n + 4 : n + 5] = total


def sec_group_y(R, packed):
    fork_c = [packed[4 * (2 * i + 1) + 3 : 4 * (2 * i + 1) + 4] for i in range(3)]
    zero = jnp.zeros((1, STATES), F32)
    adds = []
    for n in range(STEPS):
        total = zero
        for k in range(3 - n):
            total += R.cwbc[k, 1:2, :] * fork_c[n + k]
        adds.append(total)
    adds = jnp.concatenate((adds + [zero]) * 2, axis=0)
    cs = silu(R.ebuf[...] + adds[None]).reshape(2 * NZ * 8, STATES)
    y = dot(stack(split(cs, 2), 0), R.hbuf[...].reshape(HALF * WIDTH, STATES), 1, 1)
    y = (y[: 2 * NZ * 8] + y[2 * NZ * 8 :]).reshape(2 * NZ, 8, HALF * WIDTH)
    top = lax.broadcasted_iota(jnp.int32, (2 * NZ, 8, 128), 1) < 4
    for i in range(2):
        lo = 256 * i
        R.yrs[:, 8 * i : 8 * i + 8, :] = jnp.where(
            top, y[:, :, lo : lo + 128], y[:, :, lo + 128 : lo + 256]
        )


def sec_gate(R, f, owner_z):
    rows = []
    for n in range(STEPS):
        rows.append(
            jnp.concatenate(
                [
                    R.yrb[cc, owner_z, 8 * i + 4 * j + n : 8 * i + 4 * j + n + 1, :]
                    for cc in range(2)
                    for i in range(2)
                    for j in range(2)
                ],
                axis=1,
            )
        )
    at_step = [
        rows[0],
        jnp.where(f == 0, rows[1], rows[0]),
        jnp.where(f == 0, rows[2], jnp.where(f == 1, rows[1], rows[0])),
    ]
    for t in range(STEPS):
        two = slice(2 * t, 2 * t + 2)
        R.base[two] = (R.base[two] + R.bco[two] * at_step[t]) * R.gate[two]
    gated = R.base[...]
    return jnp.sum(gated * gated, axis=1, keepdims=True)


NAMES = (
    "fin_hbm",
    "src_hbm",
    "ssm_hbm",
    "cx_hbm",
    "cbc_hbm",
    "pssm_hbm",
    "pcx_hbm",
    "pcbc_hbm",
    "x_hbm",
    "z_hbm",
    "bc_hbm",
    "dt_hbm",
    "cw_hbm",
    "cwbc_hbm",
    "bias_hbm",
    "alog_hbm",
    "skip_hbm",
    "gain_hbm",
    "out",
    "pre_out",
    "fork_out",
    "ab_out",
    "ssm",
    "cx",
    "cbc",
    "pcx",
    "pcbc",
    "xin",
    "zin",
    "bcin",
    "dtin",
    "cw",
    "cwbc",
    "bias",
    "alog",
    "skip",
    "gain",
    "fin",
    "src",
    "plan_out",
    "plan_in",
    "pbuf",
    "pconv",
    "cpack",
    "csend",
    "cxbuf",
    "czsend",
    "czbuf",
    "sbuf",
    *(f"xb{g}" for g in range(len(STAGES))),
    "zsend",
    "zbuf",
    "fbuf",
    "ysend",
    "ybuf",
    "seq",
    "fork",
    "acc",
    "wts",
    "st",
    "ex",
    "dec",
    "base",
    "bco",
    "gub",
    "gate",
    "ab",
    "esend",
    "ebuf",
    "hbuf",
    "yrs",
    "yrb",
    "in_sem",
    "sc_sem",
    "own_sem",
    "out_sem",
    "plan_s",
    "plan_r",
    "pair_s",
    "pair_r",
    "cx_s",
    "cx_r",
    "cz_s",
    "cz_r",
    "x_s",
    "x_r",
    "z_s",
    "z_r",
    "g_s",
    "g_r",
    "f_s",
    "f_r",
    "zrel",
    "yrel",
    "e_s",
    "e_r",
    "r_s",
    "r_r",
    "y_s",
    "y_r",
)


class Refs:
    pass


def kernel(nx, ny, *refs):
    R = Refs()
    for name, ref in zip(NAMES, refs, strict=True):
        setattr(R, name, ref)
    me = lax.axis_index("dp")
    c = lax.rem(me, 2)
    z = lax.rem(me // 2, NZ)
    x = me // (2 * NZ)
    y = lax.axis_index("tensor")
    xbs = [getattr(R, f"xb{g}") for g in range(len(STAGES))]

    def at(xx, zz, cc):
        return {"dp": (xx * NZ + zz) * 2 + cc}

    def xpeer(d):
        return lax.rem(x + d, nx)

    def zpeer(d):
        return lax.rem(z + d, NZ)

    def ypeer(d):
        return lax.rem(y + d, ny)

    sibling = at(x, z, 1 - c)

    def remote(src, dst, ssem, rsem, dev):
        return pltpu.make_async_remote_copy(
            src_ref=src, dst_ref=dst, send_sem=ssem, recv_sem=rsem, device_id=dev, device_id_type=MESH
        )

    barrier = pltpu.get_barrier_semaphore()
    for d in range(1, nx):
        pl.semaphore_signal(barrier, inc=1, device_id=at(xpeer(d), z, c), device_id_type=MESH)
    scalars = [
        pltpu.make_async_copy(R.fin_hbm, R.fin, R.sc_sem.at[0]),
        pltpu.make_async_copy(R.src_hbm, R.src, R.sc_sem.at[1]),
    ]
    for cp in scalars:
        cp.start()
    for d in (1, 2, NZ - 2, NZ - 1):
        pl.semaphore_signal(barrier, inc=1, device_id=at(x, zpeer(d), c), device_id_type=MESH)
    for d in (1, ny - 1) if ny > 1 else ():
        pl.semaphore_signal(barrier, inc=1, device_id={"tensor": ypeer(d)}, device_id_type=MESH)
    pl.semaphore_signal(barrier, inc=1, device_id=sibling, device_id_type=MESH)

    def tell_z():
        for i, d in enumerate((2, NZ - 2)):
            pl.semaphore_signal(R.zrel.at[i], inc=1, device_id=at(x, zpeer(d), c), device_id_type=MESH)

    def hear_z():
        for i in range(2):
            pl.semaphore_wait(R.zrel.at[i], 1)

    def tell_y(n):
        for i, d in enumerate((1, ny - 1) if ny > 1 else ()):
            pl.semaphore_signal(
                R.yrel.at[n, i], inc=1, device_id={"tensor": ypeer(d)}, device_id_type=MESH
            )

    def hear_y(n):
        for i in range(2 if ny > 1 else 0):
            pl.semaphore_wait(R.yrel.at[n, i], 1)

    mine = pl.ds(pl.multiple_of(c * HALF, HALF), HALF)
    theirs = pl.ds(pl.multiple_of((1 - c) * HALF, HALF), HALF)
    my_slot = pl.ds(pl.multiple_of(c * HELD, HELD), HELD)
    loads = [
        pltpu.make_async_copy(src, dst, R.in_sem.at[i])
        for i, (src, dst) in enumerate(
            (
                (R.pcx_hbm, R.pcx),
                (R.pcbc_hbm, R.pcbc),
                (R.dt_hbm, R.dtin),
                (R.bias_hbm, R.bias),
                (R.alog_hbm, R.alog),
                (R.skip_hbm, R.skip),
                (R.cx_hbm, R.cx),
                (R.cbc_hbm, R.cbc),
                (R.x_hbm, R.xin),
                (R.bc_hbm, R.bcin),
                (R.cw_hbm, R.cw),
                (R.cwbc_hbm, R.cwbc),
                (R.z_hbm, R.zin),
                (R.gain_hbm, R.gain),
                (R.ssm_hbm, R.ssm),
            )
        )
    ]
    own = pltpu.make_async_copy(R.pssm_hbm.at[:, mine], R.pbuf.at[my_slot], R.own_sem)
    for cp in scalars:
        cp.wait()
    prompt = jnp.where(R.fin[0] < STEPS, R.src[0], R.src[1])
    refill = jnp.where(R.fin[0] < STEPS, R.fin[0], R.fin[1])
    R.plan_out[...] = jnp.full(R.plan_out.shape, prompt, jnp.int32)

    pl.semaphore_wait(barrier, 1 + (nx - 1) + 4 + (2 if ny > 1 else 0))

    order = (2, 1, 3) if nx == 4 else tuple(range(1, nx))
    plans = {}
    for d in order:
        plans[d] = remote(
            R.plan_out, R.plan_in.at[d], R.plan_s.at[d], R.plan_r.at[d], at(xpeer(d), z, c)
        )
        plans[d].start()
    tell_z()
    tell_y(0)
    pair = remote(R.pssm_hbm.at[:, theirs], R.pbuf.at[my_slot], R.pair_s.at[0], R.pair_r.at[0], sibling)
    pair.start()
    for cp in [loads[9], loads[11], loads[0], loads[1], own] + loads[2:9] + [loads[10]] + loads[12:]:
        cp.start()
    for ref in (R.wts, R.st, R.acc, R.base, R.bco, R.gub, R.gate, R.esend):
        ref[...] = jnp.zeros_like(ref)
    loads[9].wait()
    loads[11].wait()
    sec_own_c(R, refill)
    here = c * NZ + z
    R.ebuf[here] = R.esend[...]

    def group(src, dst, ssem, rsem):
        sends = []
        for d in (4, 3, 5, 2, 6, 1, 7, 0):
            for k in (0, 1) if d else (1,):
                cc = c if k == 0 else 1 - c
                to = cc * NZ + zpeer(d)
                cp = remote(src(to), dst, ssem.at[k, d], rsem.at[k, d], at(x, zpeer(d), cc))
                cp.start()
                sends.append(cp)
        return sends

    loads[0].wait()
    loads[1].wait()
    sec_pack(R)
    R.pconv[my_slot] = R.cpack[...].astype(BF16)
    pair_conv = remote(
        R.pconv.at[my_slot], R.pconv.at[my_slot], R.pair_s.at[1], R.pair_r.at[1], sibling
    )
    pair_conv.start()

    hear_z()
    e_sends = []
    for d in (4, 3, 5, 2, 6, 1, 7):
        cp = remote(R.esend, R.ebuf.at[here], R.e_s.at[d], R.e_r.at[d], at(x, zpeer(d), c))
        cp.start()
        e_sends.append(cp)

    hear_y(0)
    tell_y(1)
    pair.wait_recv()
    pair_conv.wait_recv()
    own.wait()
    for d in order:
        plans[d].wait_recv()

    def wanted(d):
        return lax.rem(R.plan_in[nx - d, 0, 0], 2 * HELD)

    want = {d: wanted(d) for d in order}
    want[0] = lax.rem(prompt, 2 * HELD)
    owner_x = prompt // (2 * HELD * NZ)
    owner_z = lax.rem(prompt // (2 * HELD), NZ)

    conv_sends = []
    for i, d in enumerate(order):
        R.csend[i] = R.pconv[want[d]]
        cp = remote(R.csend.at[i], R.cxbuf.at[x], R.cx_s.at[d], R.cx_r.at[d], at(xpeer(d), z, c))
        cp.start()
        conv_sends.append(cp)
    starts = [sum(len(o) for o in STAGES[:g]) for g in range(len(STAGES))]
    x_sends = []
    for g, offsets in enumerate(STAGES):
        sends = []
        for i, d in enumerate(order):
            for n, o in enumerate(offsets):
                R.sbuf[i, starts[g] + n] = R.pbuf[want[d], zpeer(o)]
            part = R.sbuf.at[i, starts[g] : starts[g] + len(offsets)]
            cp = remote(
                part, xbs[g].at[x], R.x_s.at[g, d], R.x_r.at[g, d], at(xpeer(d), z, c)
            )
            cp.start()
            sends.append(cp)
        x_sends.append(sends)
    R.cxbuf[x] = R.pconv[want[0]]
    for g, offsets in enumerate(STAGES):
        for n, o in enumerate(offsets):
            xbs[g][x, n] = R.pbuf[want[0], zpeer(o)]

    for i in (6, 7, 8, 10):
        loads[i].wait()
    sec_seq(R)
    for i in range(2, 6):
        loads[i].wait()
    sec_dt(R)
    sec_ab(R)

    hear_y(1)
    tell_y(2)
    for cp in conv_sends:
        cp.wait_recv()
    picked = R.cxbuf[owner_x]
    R.czsend[...] = picked
    R.czbuf[z] = picked
    cz_sends = []
    for d in (4, 3, 5, 2, 6, 1, 7):
        cp = remote(R.czsend, R.czbuf.at[z], R.cz_s.at[d], R.cz_r.at[d], at(x, zpeer(d), c))
        cp.start()
        cz_sends.append(cp)
    for cp in e_sends:
        cp.wait_recv()
    swap_c = remote(R.ebuf.at[mine], R.ebuf.at[mine], R.e_s.at[0], R.e_r.at[0], sibling)
    swap_c.start()


    z_sends = {}
    for g, offsets in enumerate(STAGES):
        for cp in x_sends[g]:
            cp.wait_recv()
        for n, o in enumerate(offsets):
            head = xbs[g][owner_x, n]
            R.hbuf[zpeer(o)] = head
            if o == 0:
                R.zbuf[z] = head
            else:
                R.zsend[o] = head
                z_sends[o] = remote(
                    R.zsend.at[o], R.zbuf.at[z], R.z_s.at[o], R.z_r.at[o], at(x, zpeer(o), c)
                )
                z_sends[o].start()

    swap_c.wait_recv()
    sec_group_y(R, picked.astype(F32))
    r_sends = group(lambda to: R.yrs.at[to], R.yrb.at[c, z], R.r_s, R.r_r)
    R.yrb[c, z] = R.yrs[here]
    loads[14].wait()
    sec_old(R)

    for cp in cz_sends:
        cp.wait_recv()
    sec_unpack(R, R.czbuf[owner_z].astype(F32))
    sec_conv(R)

    for o in (4, 3, 5, 2, 6, 1, 7):
        z_sends[o].wait_recv()
    R.fbuf[here] = R.zbuf[owner_z]
    g_sends = {}
    for d in (1, 7, 2, 6, 3, 5, 4):
        g_sends[d] = remote(
            R.fbuf.at[here], R.fbuf.at[here], R.g_s.at[d], R.g_r.at[d], at(x, zpeer(d), c)
        )
        g_sends[d].start()
    for i in (12, 13):
        loads[i].wait()
    sec_mix(R)
    sec_last(R)
    stores = [
        pltpu.make_async_copy(R.ssm, R.pre_out, R.out_sem.at[0]),
        pltpu.make_async_copy(R.ab.at[1], R.ab_out, R.out_sem.at[1]),
    ]
    for cp in stores:
        cp.start()

    for cp in r_sends:
        cp.wait_recv()
    R.ysend[...] = jnp.broadcast_to(sec_gate(R, refill, owner_z), R.ysend.shape)
    hear_y(2)
    R.ybuf[y] = R.ysend[...]
    y_sends = []
    for d in (4, 3, 5, 2, 6, 1, 7) if ny == 8 else range(1, ny):
        cp = remote(R.ysend, R.ybuf.at[y], R.y_s.at[d], R.y_r.at[d], {"tensor": ypeer(d)})
        cp.start()
        y_sends.append(cp)

    for d in NEAR:
        g_sends[d].wait_recv()
    swap = remote(R.fbuf.at[mine], R.fbuf.at[mine], R.f_s, R.f_r, sibling)
    swap.start()
    stores.append(pltpu.make_async_copy(R.fbuf.at[mine], R.fork_out.at[mine], R.out_sem.at[2]))
    stores[-1].start()
    swap.wait_recv()
    stores.append(pltpu.make_async_copy(R.fbuf.at[theirs], R.fork_out.at[theirs], R.out_sem.at[3]))
    stores[-1].start()
    for cp in list(plans.values()) + [pair, pair_conv] + conv_sends + cz_sends + e_sends + r_sends + [swap_c]:
        cp.wait_send()
    for sends in x_sends:
        for cp in sends:
            cp.wait_send()
    for sends in (z_sends, g_sends):
        for cp in sends.values():
            cp.wait_send()
    swap.wait_send()
    for cp in stores:
        cp.wait()

    for cp in y_sends:
        cp.wait_recv()
    total = R.ybuf[0]
    for i in range(1, ny):
        total += R.ybuf[i]
    scale = lax.rsqrt(total[:, 0:1] / TOTAL + 1e-05)
    normed = R.base[...] * scale * R.gain[...]
    for t in range(STEPS):
        R.out[t] = normed[2 * t : 2 * t + 2].astype(BF16)
    for cp in y_sends:
        cp.wait_send()


def put(out_ref, pre_ref, fork_ref, ab_ref, out_hbm, fs_hbm, fs, sem):
    copies = [pltpu.make_async_copy(out_ref, out_hbm, sem.at[0])]
    copies[0].start()
    for i in range(4):
        some = slice(4 * i, 4 * i + 4)
        for h in range(4 * i, 4 * i + 4):
            f = fork_ref[h].astype(F32)
            for s in range(2):
                fs[s, h] = pre_ref[s, h] + ab_ref[s, h : h + 1, :] * f
        cp = pltpu.make_async_copy(fs.at[:, some], fs_hbm.at[:, some], sem.at[1 + i])
        cp.start()
        copies.append(cp)
    for cp in copies:
        cp.wait()


def body(nx, ny, *args):
    args = list(args)
    args[3] = jnp.swapaxes(args[3], 0, 1)
    args[6] = jnp.swapaxes(args[6], 0, 1)
    for i in (14, 15, 16, 17):
        args[i] = args[i].reshape(1, -1)
    dma = pltpu.SemaphoreType.DMA
    vmem = pltpu.VMEM
    in_vmem = [args[i] for i in (2, 3, 4, 6, 7, 8, 9, 10, 11, 12, 13, 14, 15, 16, 17)]
    head = (WIDTH, STATES)
    scratch = [vmem(a.shape, a.dtype) for a in in_vmem]
    scratch += [pltpu.SMEM(a.shape, a.dtype) for a in args[:2]]
    scratch += [
        vmem((8, 128), jnp.int32),
        vmem((nx, 8, 128), jnp.int32),
        vmem((2 * HELD, HALF) + head, BF16),
        vmem((2 * HELD, 32, 128), BF16),
        vmem((HELD, 32, 128), F32),
        vmem((nx, 32, 128), BF16),
        vmem((nx, 32, 128), BF16),
        vmem((32, 128), BF16),
        vmem((NZ, 32, 128), BF16),
        vmem((nx, NZ) + head, BF16),
    ]
    scratch += [vmem((nx, len(o)) + head, BF16) for o in STAGES]
    scratch += [
        vmem((NZ,) + head, BF16),
        vmem((NZ,) + head, BF16),
        vmem((HEADS,) + head, BF16),
        vmem((8, 128), F32),
        vmem((ny, 8, 128), F32),
        vmem((6, 2, LANES), F32),
        vmem((8, LANES), F32),
        vmem((ROWS, LANES), F32),
        vmem((8, LANES), F32),
        vmem((16, 128), F32),
        vmem((16, CH), F32),
        vmem((ROWS, CH), F32),
        vmem((ROWS, CH), F32),
        vmem((ROWS, CH), F32),
        vmem((ROWS, CH), F32),
        vmem((ROWS, CH), F32),
        vmem((2, 2, HEADS, STATES), F32),
        vmem((8, STATES), F32),
        vmem((2 * NZ, 8, STATES), F32),
        vmem((HALF,) + head, BF16),
        vmem((2 * NZ, 16, 128), F32),
        vmem((2, NZ, 16, 128), F32),
        dma((len(in_vmem),)),
        dma((2,)),
        dma,
        dma((4,)),
        dma((nx,)),
        dma((nx,)),
        dma((2,)),
        dma((2,)),
        dma((nx,)),
        dma((nx,)),
        dma((NZ,)),
        dma((NZ,)),
        dma((len(STAGES), nx)),
        dma((len(STAGES), nx)),
        dma((NZ,)),
        dma((NZ,)),
        dma((NZ,)),
        dma((NZ,)),
        dma,
        dma,
        pltpu.SemaphoreType.REGULAR((2,)),
        pltpu.SemaphoreType.REGULAR((3, 2)),
        dma((NZ,)),
        dma((NZ,)),
        dma((2, NZ)),
        dma((2, NZ)),
        dma((ny,)),
        dma((ny,)),
    ]
    args = [pltpu.with_memory_space_constraint(a, pltpu.HBM) for a in args]
    anywhere = pl.BlockSpec(memory_space=pl.ANY)
    slots = args[0].shape[0]
    out, pre, fork, ab = pl.pallas_call(
        functools.partial(kernel, nx, ny),
        out_shape=(
            pltpu.VMEM((STEPS, slots, CH), BF16),
            pltpu.VMEM(args[2].shape, F32),
            pltpu.VMEM((HEADS,) + head, BF16),
            pltpu.VMEM((2, HEADS, STATES), F32),
        ),
        in_specs=[anywhere] * 18,
        out_specs=(pl.BlockSpec(memory_space=pltpu.VMEM), anywhere, anywhere, anywhere),
        scratch_shapes=scratch,
        compiler_params=pltpu.CompilerParams(
            collective_id=0, has_side_effects=True, vmem_limit_bytes=32 * 1024 * 1024
        ),
    )(*args)
    inside = pl.BlockSpec(memory_space=pltpu.VMEM)
    return pl.pallas_call(
        put,
        out_shape=(jax.ShapeDtypeStruct(out.shape, BF16), jax.ShapeDtypeStruct(pre.shape, F32)),
        in_specs=[anywhere, inside, inside, inside],
        out_specs=(anywhere, anywhere),
        scratch_shapes=[vmem(pre.shape, F32), dma((5,))],
        compiler_params=pltpu.CompilerParams(vmem_limit_bytes=16 * 1024 * 1024),
    )(out, pre, fork, ab)


def solution(mesh):
    nx = mesh.shape["dp"] // (2 * NZ)
    ny = mesh.shape["tensor"]
    return jax.shard_map(
        functools.partial(body, nx, ny),
        mesh=mesh,
        in_specs=(
            P("dp"),
            P("dp"),
            P("dp", "tensor", None, None),
            P("dp", None, "tensor"),
            P("dp", None, None, "tensor"),
            P("dp", "tensor", None, None),
            P("dp", None, "tensor"),
            P("dp", None, None, "tensor"),
            P(None, "dp", "tensor"),
            P(None, "dp", "tensor"),
            P(None, "dp", None, "tensor"),
            P(None, "dp", "tensor"),
            P(None, "tensor"),
            P(None, None, "tensor"),
            P("tensor"),
            P("tensor"),
            P("tensor"),
            P("tensor"),
        ),
        out_specs=(P(None, "dp", "tensor"), P("dp", "tensor", None, None)),
        check_vma=False,
    )
```

```python
import functools

import jax
import jax.numpy as jnp
from jax import lax
from jax.experimental import pallas as pl
from jax.experimental.pallas import tpu as pltpu
from jax.sharding import PartitionSpec as P

F32 = jnp.float32
BF16 = jnp.bfloat16
MESH = pl.DeviceIdType.MESH

NZ = 8
HELD = 4
HEADS = 16
HALF = 8
WIDTH = 64
STATES = 128
CH = HEADS * WIDTH
LANES = CH + 2 * STATES
STEPS = 3
TAPS = 4
ROWS = 8
TOTAL = 8192
STAGES = ((4, 3, 5), (2, 6, 7), (1, 0))
NEAR = (1, 7, 2, 6, 3, 5, 4)


def silu(v):
    return v * (1.0 / (1.0 + jnp.exp(-v)))


def softplus(v):
    return jnp.maximum(v, 0.0) + jnp.log1p(jnp.exp(-jnp.abs(v)))


def dot(a, b, da, db):
    return lax.dot_general(a, b, (((da,), (db,)), ((), ())), preferred_element_type=F32)


def split(v, n):
    parts = []
    for _ in range(n):
        hi = v.astype(BF16).astype(F32)
        parts.append(hi)
        v = v - hi
    return parts


def stack(parts, axis):
    return jnp.concatenate(parts, axis=axis).astype(BF16)


def sec_pack(R):
    for i in range(3):
        tap = R.pcx[i].astype(F32)
        for q in range(HELD):
            for k in range(8):
                r = 4 * k + i
                R.cpack[q, r : r + 1, :] = tap[q : q + 1, 128 * k : 128 * (k + 1)]
    for q in range(HELD):
        for i in range(3):
            for b in range(2):
                r = 4 * (2 * i + b) + 3
                R.cpack[q, r : r + 1, :] = R.pcbc[q, i, b : b + 1, :].astype(F32)


def sec_dt(R):
    for t in range(STEPS):
        R.st[2 * t : 2 * t + 2, :HEADS] = R.dtin[t]
    R.st[6:7, :HEADS] = R.bias[...]
    R.st[7:8, :HEADS] = R.alog[...]
    R.st[8:9, :HEADS] = R.skip[...]
    parts = split(R.st[:, :HEADS], 3)
    spread = (
        lax.broadcasted_iota(jnp.int32, (HEADS, CH), 1) // WIDTH
        == lax.broadcasted_iota(jnp.int32, (HEADS, CH), 0)
    ).astype(F32)
    full = dot(stack(parts, 1), stack([spread] * 3, 0), 1, 0)
    step = softplus(full[0:ROWS] + full[6:7])
    R.ex[0:ROWS] = step
    R.ex[8:9] = full[8:9]
    R.dec[...] = jnp.exp(-jnp.exp(full[7:8]) * step)


def sec_ab(R):
    pick = (
        lax.broadcasted_iota(jnp.int32, (16, 8 * STATES), 1) // STATES
        == lax.broadcasted_iota(jnp.int32, (16, 8 * STATES), 0)
    ).astype(F32)
    parts = split(R.st[:, :HEADS], 3)
    hb = dot(stack(parts, 0), stack([pick] * 3, 0), 0, 0)

    def col(r):
        return hb[:, r * STATES : (r + 1) * STATES]

    rate = -jnp.exp(col(7))
    for s in range(2):
        a = jnp.ones((HEADS, STATES), F32)
        b = jnp.zeros((HEADS, STATES), F32)
        fin = jnp.full((HEADS, STATES), R.fin[s], jnp.int32)
        for t in range(STEPS):
            d_t = jnp.exp(rate * softplus(col(2 * t + s) + col(6)))
            a = jnp.where(fin == t, 0.0, a) * d_t
            b = jnp.where(fin == t, 1.0, b) * d_t
        R.ab[0, s] = a
        R.ab[1, s] = b


def sec_seq(R):
    for i in range(3):
        R.seq[i, :, :CH] = R.cx[i].astype(F32)
        for s in range(2):
            for b in range(2):
                lo = CH + b * STATES
                R.seq[i, s : s + 1, lo : lo + STATES] = R.cbc[s, i, b : b + 1, :].astype(F32)
    for t in range(STEPS):
        R.seq[3 + t, :, :CH] = R.xin[t].astype(F32)
        for s in range(2):
            for b in range(2):
                lo = CH + b * STATES
                R.seq[3 + t, s : s + 1, lo : lo + STATES] = R.bcin[t, s, b : b + 1, :].astype(F32)
    R.wts[:TAPS, :CH] = R.cw[...]
    for k in range(TAPS):
        for b in range(2):
            lo = CH + b * STATES
            R.wts[k : k + 1, lo : lo + STATES] = R.cwbc[k, b : b + 1, :]


def sec_old(R):
    for t in range(STEPS):
        total = jnp.zeros((2, STATES), F32)
        for k in range(TAPS):
            total += R.wts[k : k + 1, CH + STATES :] * R.seq[t + k, :, CH + STATES :]
        R.acc[2 * t : 2 * t + 2, CH + STATES :] = total
    c_hi, c_lo = split(silu(R.acc[:, CH + STATES :]), 2)
    c_parts = stack([c_hi, c_lo], 0)
    ys = []
    for s in range(2):
        state = R.ssm[s].reshape(CH, STATES)
        hi = state.astype(BF16)
        lo = (state - hi.astype(F32)).astype(BF16)
        both = dot(c_parts, hi, 1, 1)
        ys.append(both[0:ROWS] + both[ROWS:] + dot(c_parts, lo, 1, 1)[0:ROWS])
    row = lax.broadcasted_iota(jnp.int32, (ROWS, CH), 0)
    R.base[...] = jnp.where(row >= 2 * STEPS, 0.0, jnp.where(lax.rem(row, 2) == 0, ys[0], ys[1]))


def sec_unpack(R, packed):
    for k in range(8):
        R.fork[0:3, 128 * k : 128 * (k + 1)] = packed[4 * k : 4 * k + 3]
    for i in range(3):
        for b in range(2):
            r = 4 * (2 * i + b) + 3
            lo = CH + b * STATES
            R.fork[i : i + 1, lo : lo + STATES] = packed[r : r + 1]


def fin_rows(R, lanes):
    first = lax.broadcasted_iota(jnp.int32, (2, lanes), 0) == 0
    return jnp.where(first, R.fin[0], R.fin[1])


def sec_conv(R):
    fin = fin_rows(R, LANES)
    for t in range(STEPS):
        total = jnp.zeros((2, LANES), F32)
        for k in range(TAPS):
            w = R.seq[t + k]
            for f in range(t + 1):
                if t + k - f <= 2:
                    r = t + k - f
                    w = jnp.where(fin == f, R.fork[r : r + 1, :], w)
            total += R.wts[k : k + 1, :] * w
        R.acc[2 * t : 2 * t + 2, :] = total
    R.acc[...] = silu(R.acc[...])


def sec_mix(R):
    fin = fin_rows(R, CH)
    a = jnp.ones((2, CH), F32)
    b = jnp.zeros((2, CH), F32)
    gs = []
    for t in range(STEPS):
        two = slice(2 * t, 2 * t + 2)
        now = fin == t
        d_t = R.dec[two]
        a = jnp.where(now, 0.0, a) * d_t
        b = jnp.where(now, 1.0, b) * d_t
        x_t = R.acc[two, :CH]
        u = R.ex[two] * x_t
        gs = [jnp.where(now, 0.0, v) * d_t for v in gs] + [u]
        c_t = R.acc[two, CH + STATES :]
        total = a * R.base[two] + R.ex[8:9] * x_t
        for k in range(t + 1):
            b_k = R.acc[2 * k : 2 * k + 2, CH : CH + STATES]
            total += gs[k] * jnp.sum(b_k * c_t, axis=1, keepdims=True)
        R.base[two] = total
        R.bco[two] = b
    for k in range(STEPS):
        R.gub[2 * k : 2 * k + 2] = gs[k]
    for t in range(STEPS):
        R.gate[2 * t : 2 * t + 2] = silu(R.zin[t].astype(F32))


def sec_last(R):
    bm = R.acc[:, CH : CH + STATES]
    odd = lax.rem(lax.broadcasted_iota(jnp.int32, (ROWS, STATES), 0), 2)
    both = jnp.concatenate([jnp.where(odd == 0, bm, 0.0), jnp.where(odd == 1, bm, 0.0)], axis=1)
    b_hi, b_lo = split(both, 2)
    g_hi, g_lo = split(R.gub[...], 2)
    rhs = stack([b_hi, b_hi, b_lo, b_lo], 0)
    lhs = stack([g_hi, g_lo, g_hi, g_lo], 0)
    u = dot(lhs, rhs, 0, 0)
    for h in range(HEADS):
        for s in range(2):
            R.ssm[s, h] = (
                R.ab[0, s, h : h + 1, :] * R.ssm[s, h]
                + u[h * WIDTH : (h + 1) * WIDTH, s * STATES : (s + 1) * STATES]
            )


def sec_own_c(R, f):
    rows = [
        jnp.where(R.fin[0] < STEPS, R.bcin[t, 0, 1:2, :].astype(F32), R.bcin[t, 1, 1:2, :].astype(F32))
        for t in range(STEPS)
    ]
    after = [
        jnp.where(f == 0, rows[0], jnp.where(f == 1, rows[1], rows[2])),
        jnp.where(f == 0, rows[1], rows[2]),
        rows[2],
    ]
    for n in range(STEPS):
        total = jnp.zeros((1, STATES), F32)
        for i in range(n + 1):
            total += R.cwbc[i + 3 - n, 1:2, :] * after[i]
        R.esend[n : n + 1] = total


def sec_group_y(R, packed):
    fork_c = [packed[4 * (2 * i + 1) + 3 : 4 * (2 * i + 1) + 4] for i in range(3)]
    zero = jnp.zeros((1, STATES), F32)
    adds = []
    for n in range(STEPS):
        total = zero
        for k in range(3 - n):
            total += R.cwbc[k, 1:2, :] * fork_c[n + k]
        adds.append(total)
    adds = jnp.concatenate(adds + [zero] * 5, axis=0)
    cs = silu(R.ebuf[...] + adds[None]).reshape(2 * NZ * 8, STATES)
    y = dot(stack(split(cs, 2), 0), R.hbuf[...].reshape(HALF * WIDTH, STATES), 1, 1)
    y = (y[: 2 * NZ * 8] + y[2 * NZ * 8 :]).reshape(2 * NZ, 8, HALF * WIDTH)
    for n in range(STEPS):
        for q in range(4):
            R.yrs[:, n, q, :] = y[:, n, 128 * q : 128 * (q + 1)]


def sec_gate(R, f, owner_z):
    rows = []
    for n in range(STEPS):
        rows.append(
            jnp.concatenate(
                [
                    R.yrb[cc, owner_z, n, q : q + 1, :]
                    for cc in range(2)
                    for q in range(4)
                ],
                axis=1,
            )
        )
    at_step = [
        rows[0],
        jnp.where(f == 0, rows[1], rows[0]),
        jnp.where(f == 0, rows[2], jnp.where(f == 1, rows[1], rows[0])),
    ]
    for t in range(STEPS):
        two = slice(2 * t, 2 * t + 2)
        R.base[two] = (R.base[two] + R.bco[two] * at_step[t]) * R.gate[two]
    gated = R.base[...]
    return jnp.sum(gated * gated, axis=1, keepdims=True)


NAMES = (
    "fin_hbm",
    "src_hbm",
    "ssm_hbm",
    "cx_hbm",
    "cbc_hbm",
    "pssm_hbm",
    "pcx_hbm",
    "pcbc_hbm",
    "x_hbm",
    "z_hbm",
    "bc_hbm",
    "dt_hbm",
    "cw_hbm",
    "cwbc_hbm",
    "bias_hbm",
    "alog_hbm",
    "skip_hbm",
    "gain_hbm",
    "out",
    "pre_out",
    "fork_out",
    "ab_out",
    "ssm",
    "cx",
    "cbc",
    "pcx",
    "pcbc",
    "xin",
    "zin",
    "bcin",
    "dtin",
    "cw",
    "cwbc",
    "bias",
    "alog",
    "skip",
    "gain",
    "fin",
    "src",
    "plan_out",
    "plan_in",
    "pbuf",
    "pconv",
    "cpack",
    "csend",
    "cxbuf",
    "czsend",
    "czbuf",
    "sbuf",
    *(f"xb{g}" for g in range(len(STAGES))),
    "zsend",
    "zbuf",
    "fbuf",
    "ysend",
    "ybuf",
    "seq",
    "fork",
    "acc",
    "wts",
    "st",
    "ex",
    "dec",
    "base",
    "bco",
    "gub",
    "gate",
    "ab",
    "esend",
    "ebuf",
    "hbuf",
    "yrs",
    "yrb",
    "in_sem",
    "sc_sem",
    "own_sem",
    "out_sem",
    "plan_s",
    "plan_r",
    "pair_s",
    "pair_r",
    "cx_s",
    "cx_r",
    "cz_s",
    "cz_r",
    "x_s",
    "x_r",
    "z_s",
    "z_r",
    "g_s",
    "g_r",
    "f_s",
    "f_r",
    "zrel",
    "yrel",
    "e_s",
    "e_r",
    "r_s",
    "r_r",
    "y_s",
    "y_r",
)


class Refs:
    pass


def kernel(nx, ny, *refs):
    R = Refs()
    for name, ref in zip(NAMES, refs, strict=True):
        setattr(R, name, ref)
    me = lax.axis_index("dp")
    c = lax.rem(me, 2)
    z = lax.rem(me // 2, NZ)
    x = me // (2 * NZ)
    y = lax.axis_index("tensor")
    xbs = [getattr(R, f"xb{g}") for g in range(len(STAGES))]

    def at(xx, zz, cc):
        return {"dp": (xx * NZ + zz) * 2 + cc}

    def xpeer(d):
        return lax.rem(x + d, nx)

    def zpeer(d):
        return lax.rem(z + d, NZ)

    def ypeer(d):
        return lax.rem(y + d, ny)

    sibling = at(x, z, 1 - c)

    def remote(src, dst, ssem, rsem, dev):
        return pltpu.make_async_remote_copy(
            src_ref=src, dst_ref=dst, send_sem=ssem, recv_sem=rsem, device_id=dev, device_id_type=MESH
        )

    barrier = pltpu.get_barrier_semaphore()
    for d in range(1, nx):
        pl.semaphore_signal(barrier, inc=1, device_id=at(xpeer(d), z, c), device_id_type=MESH)
    scalars = [
        pltpu.make_async_copy(R.fin_hbm, R.fin, R.sc_sem.at[0]),
        pltpu.make_async_copy(R.src_hbm, R.src, R.sc_sem.at[1]),
    ]
    for cp in scalars:
        cp.start()
    for d in (1, 2, NZ - 2, NZ - 1):
        pl.semaphore_signal(barrier, inc=1, device_id=at(x, zpeer(d), c), device_id_type=MESH)
    for d in (1, ny - 1) if ny > 1 else ():
        pl.semaphore_signal(barrier, inc=1, device_id={"tensor": ypeer(d)}, device_id_type=MESH)
    pl.semaphore_signal(barrier, inc=1, device_id=sibling, device_id_type=MESH)

    def tell_z():
        for i, d in enumerate((2, NZ - 2)):
            pl.semaphore_signal(R.zrel.at[i], inc=1, device_id=at(x, zpeer(d), c), device_id_type=MESH)

    def hear_z():
        for i in range(2):
            pl.semaphore_wait(R.zrel.at[i], 1)

    def tell_y(n):
        for i, d in enumerate((1, ny - 1) if ny > 1 else ()):
            pl.semaphore_signal(
                R.yrel.at[n, i], inc=1, device_id={"tensor": ypeer(d)}, device_id_type=MESH
            )

    def hear_y(n):
        for i in range(2 if ny > 1 else 0):
            pl.semaphore_wait(R.yrel.at[n, i], 1)

    mine = pl.ds(pl.multiple_of(c * HALF, HALF), HALF)
    theirs = pl.ds(pl.multiple_of((1 - c) * HALF, HALF), HALF)
    my_slot = pl.ds(pl.multiple_of(c * HELD, HELD), HELD)
    loads = [
        pltpu.make_async_copy(src, dst, R.in_sem.at[i])
        for i, (src, dst) in enumerate(
            (
                (R.pcx_hbm, R.pcx),
                (R.pcbc_hbm, R.pcbc),
                (R.dt_hbm, R.dtin),
                (R.bias_hbm, R.bias),
                (R.alog_hbm, R.alog),
                (R.skip_hbm, R.skip),
                (R.cx_hbm, R.cx),
                (R.cbc_hbm, R.cbc),
                (R.x_hbm, R.xin),
                (R.bc_hbm, R.bcin),
                (R.cw_hbm, R.cw),
                (R.cwbc_hbm, R.cwbc),
                (R.z_hbm, R.zin),
                (R.gain_hbm, R.gain),
                (R.ssm_hbm, R.ssm),
            )
        )
    ]
    own = pltpu.make_async_copy(R.pssm_hbm.at[:, mine], R.pbuf.at[my_slot], R.own_sem)
    for cp in scalars:
        cp.wait()
    prompt = jnp.where(R.fin[0] < STEPS, R.src[0], R.src[1])
    refill = jnp.where(R.fin[0] < STEPS, R.fin[0], R.fin[1])
    R.plan_out[...] = jnp.full(R.plan_out.shape, prompt, jnp.int32)

    pl.semaphore_wait(barrier, 1 + (nx - 1) + 4 + (2 if ny > 1 else 0))

    order = (2, 1, 3) if nx == 4 else tuple(range(1, nx))
    plans = {}
    for d in order:
        plans[d] = remote(
            R.plan_out, R.plan_in.at[d], R.plan_s.at[d], R.plan_r.at[d], at(xpeer(d), z, c)
        )
        plans[d].start()
    tell_z()
    tell_y(0)
    pair = remote(R.pssm_hbm.at[:, theirs], R.pbuf.at[my_slot], R.pair_s.at[0], R.pair_r.at[0], sibling)
    pair.start()
    for cp in [loads[9], loads[11], loads[0], loads[1], own] + loads[2:9] + [loads[10]] + loads[12:]:
        cp.start()
    for ref in (R.wts, R.st, R.acc, R.base, R.bco, R.gub, R.gate, R.esend):
        ref[...] = jnp.zeros_like(ref)
    loads[9].wait()
    loads[11].wait()
    sec_own_c(R, refill)
    here = c * NZ + z
    R.ebuf[here] = R.esend[...]

    def group(src, dst, ssem, rsem):
        sends = []
        for d in (4, 3, 5, 2, 6, 1, 7, 0):
            for k in (0, 1) if d else (1,):
                cc = c if k == 0 else 1 - c
                to = cc * NZ + zpeer(d)
                cp = remote(src(to), dst, ssem.at[k, d], rsem.at[k, d], at(x, zpeer(d), cc))
                cp.start()
                sends.append(cp)
        return sends

    loads[0].wait()
    loads[1].wait()
    sec_pack(R)
    R.pconv[my_slot] = R.cpack[...].astype(BF16)
    pair_conv = remote(
        R.pconv.at[my_slot], R.pconv.at[my_slot], R.pair_s.at[1], R.pair_r.at[1], sibling
    )
    pair_conv.start()

    hear_z()
    e_sends = []
    for d in (4, 3, 5, 2, 6, 1, 7):
        cp = remote(R.esend, R.ebuf.at[here], R.e_s.at[d], R.e_r.at[d], at(x, zpeer(d), c))
        cp.start()
        e_sends.append(cp)

    hear_y(0)
    tell_y(1)
    pair.wait_recv()
    pair_conv.wait_recv()
    own.wait()
    for d in order:
        plans[d].wait_recv()

    def wanted(d):
        return lax.rem(R.plan_in[nx - d, 0, 0], 2 * HELD)

    want = {d: wanted(d) for d in order}
    want[0] = lax.rem(prompt, 2 * HELD)
    owner_x = prompt // (2 * HELD * NZ)
    owner_z = lax.rem(prompt // (2 * HELD), NZ)

    conv_sends = []
    for i, d in enumerate(order):
        R.csend[i] = R.pconv[want[d]]
        cp = remote(R.csend.at[i], R.cxbuf.at[x], R.cx_s.at[d], R.cx_r.at[d], at(xpeer(d), z, c))
        cp.start()
        conv_sends.append(cp)
    starts = [sum(len(o) for o in STAGES[:g]) for g in range(len(STAGES))]
    x_sends = []
    for g, offsets in enumerate(STAGES):
        sends = []
        for i, d in enumerate(order):
            for n, o in enumerate(offsets):
                R.sbuf[i, starts[g] + n] = R.pbuf[want[d], zpeer(o)]
            part = R.sbuf.at[i, starts[g] : starts[g] + len(offsets)]
            cp = remote(
                part, xbs[g].at[x], R.x_s.at[g, d], R.x_r.at[g, d], at(xpeer(d), z, c)
            )
            cp.start()
            sends.append(cp)
        x_sends.append(sends)
    R.cxbuf[x] = R.pconv[want[0]]
    for g, offsets in enumerate(STAGES):
        for n, o in enumerate(offsets):
            xbs[g][x, n] = R.pbuf[want[0], zpeer(o)]

    for i in (6, 7, 8, 10):
        loads[i].wait()
    sec_seq(R)
    for i in range(2, 6):
        loads[i].wait()
    sec_dt(R)
    sec_ab(R)

    hear_y(1)
    tell_y(2)
    for cp in conv_sends:
        cp.wait_recv()
    picked = R.cxbuf[owner_x]
    R.czsend[...] = picked
    R.czbuf[z] = picked
    cz_sends = []
    for d in (4, 3, 5, 2, 6, 1, 7):
        cp = remote(R.czsend, R.czbuf.at[z], R.cz_s.at[d], R.cz_r.at[d], at(x, zpeer(d), c))
        cp.start()
        cz_sends.append(cp)
    for cp in e_sends:
        cp.wait_recv()
    swap_c = remote(R.ebuf.at[mine], R.ebuf.at[mine], R.e_s.at[0], R.e_r.at[0], sibling)
    swap_c.start()


    z_sends = {}
    for g, offsets in enumerate(STAGES):
        for cp in x_sends[g]:
            cp.wait_recv()
        for n, o in enumerate(offsets):
            head = xbs[g][owner_x, n]
            R.hbuf[zpeer(o)] = head
            if o == 0:
                R.zbuf[z] = head
            else:
                R.zsend[o] = head
                z_sends[o] = remote(
                    R.zsend.at[o], R.zbuf.at[z], R.z_s.at[o], R.z_r.at[o], at(x, zpeer(o), c)
                )
                z_sends[o].start()

    swap_c.wait_recv()
    sec_group_y(R, picked.astype(F32))
    r_sends = group(lambda to: R.yrs.at[to], R.yrb.at[c, z], R.r_s, R.r_r)
    R.yrb[c, z] = R.yrs[here]
    loads[14].wait()
    sec_old(R)

    for cp in cz_sends:
        cp.wait_recv()
    sec_unpack(R, R.czbuf[owner_z].astype(F32))
    sec_conv(R)

    for o in (4, 3, 5, 2, 6, 1, 7):
        z_sends[o].wait_recv()
    R.fbuf[here] = R.zbuf[owner_z]
    g_sends = {}
    for d in (1, 7, 2, 6, 3, 5, 4):
        g_sends[d] = remote(
            R.fbuf.at[here], R.fbuf.at[here], R.g_s.at[d], R.g_r.at[d], at(x, zpeer(d), c)
        )
        g_sends[d].start()
    for i in (12, 13):
        loads[i].wait()
    sec_mix(R)
    sec_last(R)
    stores = [
        pltpu.make_async_copy(R.ssm, R.pre_out, R.out_sem.at[0]),
        pltpu.make_async_copy(R.ab.at[1], R.ab_out, R.out_sem.at[1]),
    ]
    for cp in stores:
        cp.start()

    for cp in r_sends:
        cp.wait_recv()
    R.ysend[...] = jnp.broadcast_to(sec_gate(R, refill, owner_z), R.ysend.shape)
    hear_y(2)
    R.ybuf[y] = R.ysend[...]
    y_sends = []
    for d in (4, 3, 5, 2, 6, 1, 7) if ny == 8 else range(1, ny):
        cp = remote(R.ysend, R.ybuf.at[y], R.y_s.at[d], R.y_r.at[d], {"tensor": ypeer(d)})
        cp.start()
        y_sends.append(cp)

    for d in NEAR:
        g_sends[d].wait_recv()
    swap = remote(R.fbuf.at[mine], R.fbuf.at[mine], R.f_s, R.f_r, sibling)
    swap.start()
    stores.append(pltpu.make_async_copy(R.fbuf.at[mine], R.fork_out.at[mine], R.out_sem.at[2]))
    stores[-1].start()
    swap.wait_recv()
    stores.append(pltpu.make_async_copy(R.fbuf.at[theirs], R.fork_out.at[theirs], R.out_sem.at[3]))
    stores[-1].start()
    for cp in list(plans.values()) + [pair, pair_conv] + conv_sends + cz_sends + e_sends + r_sends + [swap_c]:
        cp.wait_send()
    for sends in x_sends:
        for cp in sends:
            cp.wait_send()
    for sends in (z_sends, g_sends):
        for cp in sends.values():
            cp.wait_send()
    swap.wait_send()
    for cp in stores:
        cp.wait()

    for cp in y_sends:
        cp.wait_recv()
    total = R.ybuf[0]
    for i in range(1, ny):
        total += R.ybuf[i]
    scale = lax.rsqrt(total[:, 0:1] / TOTAL + 1e-05)
    normed = R.base[...] * scale * R.gain[...]
    for t in range(STEPS):
        R.out[t] = normed[2 * t : 2 * t + 2].astype(BF16)
    for cp in y_sends:
        cp.wait_send()


def put(out_ref, pre_ref, fork_ref, ab_ref, out_hbm, fs_hbm, fs, sem):
    copies = [pltpu.make_async_copy(out_ref, out_hbm, sem.at[0])]
    copies[0].start()
    for i in range(4):
        some = slice(4 * i, 4 * i + 4)
        for h in range(4 * i, 4 * i + 4):
            f = fork_ref[h].astype(F32)
            for s in range(2):
                fs[s, h] = pre_ref[s, h] + ab_ref[s, h : h + 1, :] * f
        cp = pltpu.make_async_copy(fs.at[:, some], fs_hbm.at[:, some], sem.at[1 + i])
        cp.start()
        copies.append(cp)
    for cp in copies:
        cp.wait()


def body(nx, ny, *args):
    args = list(args)
    args[3] = jnp.swapaxes(args[3], 0, 1)
    args[6] = jnp.swapaxes(args[6], 0, 1)
    for i in (14, 15, 16, 17):
        args[i] = args[i].reshape(1, -1)
    dma = pltpu.SemaphoreType.DMA
    vmem = pltpu.VMEM
    in_vmem = [args[i] for i in (2, 3, 4, 6, 7, 8, 9, 10, 11, 12, 13, 14, 15, 16, 17)]
    head = (WIDTH, STATES)
    scratch = [vmem(a.shape, a.dtype) for a in in_vmem]
    scratch += [pltpu.SMEM(a.shape, a.dtype) for a in args[:2]]
    scratch += [
        vmem((8, 128), jnp.int32),
        vmem((nx, 8, 128), jnp.int32),
        vmem((2 * HELD, HALF) + head, BF16),
        vmem((2 * HELD, 32, 128), BF16),
        vmem((HELD, 32, 128), F32),
        vmem((nx, 32, 128), BF16),
        vmem((nx, 32, 128), BF16),
        vmem((32, 128), BF16),
        vmem((NZ, 32, 128), BF16),
        vmem((nx, NZ) + head, BF16),
    ]
    scratch += [vmem((nx, len(o)) + head, BF16) for o in STAGES]
    scratch += [
        vmem((NZ,) + head, BF16),
        vmem((NZ,) + head, BF16),
        vmem((HEADS,) + head, BF16),
        vmem((8, 128), F32),
        vmem((ny, 8, 128), F32),
        vmem((6, 2, LANES), F32),
        vmem((8, LANES), F32),
        vmem((ROWS, LANES), F32),
        vmem((8, LANES), F32),
        vmem((16, 128), F32),
        vmem((16, CH), F32),
        vmem((ROWS, CH), F32),
        vmem((ROWS, CH), F32),
        vmem((ROWS, CH), F32),
        vmem((ROWS, CH), F32),
        vmem((ROWS, CH), F32),
        vmem((2, 2, HEADS, STATES), F32),
        vmem((8, STATES), F32),
        vmem((2 * NZ, 8, STATES), F32),
        vmem((HALF,) + head, BF16),
        vmem((2 * NZ, STEPS, 4, 128), F32),
        vmem((2, NZ, STEPS, 4, 128), F32),
        dma((len(in_vmem),)),
        dma((2,)),
        dma,
        dma((4,)),
        dma((nx,)),
        dma((nx,)),
        dma((2,)),
        dma((2,)),
        dma((nx,)),
        dma((nx,)),
        dma((NZ,)),
        dma((NZ,)),
        dma((len(STAGES), nx)),
        dma((len(STAGES), nx)),
        dma((NZ,)),
        dma((NZ,)),
        dma((NZ,)),
        dma((NZ,)),
        dma,
        dma,
        pltpu.SemaphoreType.REGULAR((2,)),
        pltpu.SemaphoreType.REGULAR((3, 2)),
        dma((NZ,)),
        dma((NZ,)),
        dma((2, NZ)),
        dma((2, NZ)),
        dma((ny,)),
        dma((ny,)),
    ]
    args = [pltpu.with_memory_space_constraint(a, pltpu.HBM) for a in args]
    anywhere = pl.BlockSpec(memory_space=pl.ANY)
    slots = args[0].shape[0]
    out, pre, fork, ab = pl.pallas_call(
        functools.partial(kernel, nx, ny),
        out_shape=(
            pltpu.VMEM((STEPS, slots, CH), BF16),
            pltpu.VMEM(args[2].shape, F32),
            pltpu.VMEM((HEADS,) + head, BF16),
            pltpu.VMEM((2, HEADS, STATES), F32),
        ),
        in_specs=[anywhere] * 18,
        out_specs=(pl.BlockSpec(memory_space=pltpu.VMEM), anywhere, anywhere, anywhere),
        scratch_shapes=scratch,
        compiler_params=pltpu.CompilerParams(
            collective_id=0, has_side_effects=True, vmem_limit_bytes=32 * 1024 * 1024
        ),
    )(*args)
    inside = pl.BlockSpec(memory_space=pltpu.VMEM)
    return pl.pallas_call(
        put,
        out_shape=(jax.ShapeDtypeStruct(out.shape, BF16), jax.ShapeDtypeStruct(pre.shape, F32)),
        in_specs=[anywhere, inside, inside, inside],
        out_specs=(anywhere, anywhere),
        scratch_shapes=[vmem(pre.shape, F32), dma((5,))],
        compiler_params=pltpu.CompilerParams(vmem_limit_bytes=16 * 1024 * 1024),
    )(out, pre, fork, ab)


def solution(mesh):
    nx = mesh.shape["dp"] // (2 * NZ)
    ny = mesh.shape["tensor"]
    return jax.shard_map(
        functools.partial(body, nx, ny),
        mesh=mesh,
        in_specs=(
            P("dp"),
            P("dp"),
            P("dp", "tensor", None, None),
            P("dp", None, "tensor"),
            P("dp", None, None, "tensor"),
            P("dp", "tensor", None, None),
            P("dp", None, "tensor"),
            P("dp", None, None, "tensor"),
            P(None, "dp", "tensor"),
            P(None, "dp", "tensor"),
            P(None, "dp", None, "tensor"),
            P(None, "dp", "tensor"),
            P(None, "tensor"),
            P(None, None, "tensor"),
            P("tensor"),
            P("tensor"),
            P("tensor"),
            P("tensor"),
        ),
        out_specs=(P(None, "dp", "tensor"), P("dp", "tensor", None, None)),
        check_vma=False,
    )
```

```python
import functools

import jax
import jax.numpy as jnp
from jax import lax
from jax.experimental import pallas as pl
from jax.experimental.pallas import tpu as pltpu
from jax.sharding import PartitionSpec as P

F32 = jnp.float32
BF16 = jnp.bfloat16
MESH = pl.DeviceIdType.MESH

NZ = 8
HELD = 4
HEADS = 16
HALF = 8
WIDTH = 64
STATES = 128
CH = HEADS * WIDTH
LANES = CH + 2 * STATES
STEPS = 3
TAPS = 4
ROWS = 8
TOTAL = 8192
STAGES = ((4, 3, 5), (2, 6, 7), (1, 0))
NEAR = (1, 7, 2, 6, 3, 5, 4)


def silu(v):
    return v * (1.0 / (1.0 + jnp.exp(-v)))


def softplus(v):
    return jnp.maximum(v, 0.0) + jnp.log1p(jnp.exp(-jnp.abs(v)))


def dot(a, b, da, db):
    return lax.dot_general(a, b, (((da,), (db,)), ((), ())), preferred_element_type=F32)


def split(v, n):
    parts = []
    for _ in range(n):
        hi = v.astype(BF16).astype(F32)
        parts.append(hi)
        v = v - hi
    return parts


def stack(parts, axis):
    return jnp.concatenate(parts, axis=axis).astype(BF16)


def sec_pack(R):
    for i in range(3):
        tap = R.pcx[i].astype(F32)
        for q in range(HELD):
            for k in range(8):
                r = 4 * k + i
                R.cpack[q, r : r + 1, :] = tap[q : q + 1, 128 * k : 128 * (k + 1)]
    for q in range(HELD):
        for i in range(3):
            for b in range(2):
                r = 4 * (2 * i + b) + 3
                R.cpack[q, r : r + 1, :] = R.pcbc[q, i, b : b + 1, :].astype(F32)


def sec_dt(R):
    for t in range(STEPS):
        R.st[2 * t : 2 * t + 2, :HEADS] = R.dtin[t]
    R.st[6:7, :HEADS] = R.bias[...]
    R.st[7:8, :HEADS] = R.alog[...]
    R.st[8:9, :HEADS] = R.skip[...]
    parts = split(R.st[:, :HEADS], 3)
    spread = (
        lax.broadcasted_iota(jnp.int32, (HEADS, CH), 1) // WIDTH
        == lax.broadcasted_iota(jnp.int32, (HEADS, CH), 0)
    ).astype(F32)
    full = dot(stack(parts, 1), stack([spread] * 3, 0), 1, 0)
    step = softplus(full[0:ROWS] + full[6:7])
    R.ex[0:ROWS] = step
    R.ex[8:9] = full[8:9]
    R.dec[...] = jnp.exp(-jnp.exp(full[7:8]) * step)


def sec_ab(R):
    pick = (
        lax.broadcasted_iota(jnp.int32, (16, 8 * STATES), 1) // STATES
        == lax.broadcasted_iota(jnp.int32, (16, 8 * STATES), 0)
    ).astype(F32)
    parts = split(R.st[:, :HEADS], 3)
    hb = dot(stack(parts, 0), stack([pick] * 3, 0), 0, 0)

    def col(r):
        return hb[:, r * STATES : (r + 1) * STATES]

    rate = -jnp.exp(col(7))
    for s in range(2):
        a = jnp.ones((HEADS, STATES), F32)
        b = jnp.zeros((HEADS, STATES), F32)
        fin = jnp.full((HEADS, STATES), R.fin[s], jnp.int32)
        for t in range(STEPS):
            d_t = jnp.exp(rate * softplus(col(2 * t + s) + col(6)))
            a = jnp.where(fin == t, 0.0, a) * d_t
            b = jnp.where(fin == t, 1.0, b) * d_t
        R.ab[0, s] = a
        R.ab[1, s] = b


def sec_seq(R):
    for i in range(3):
        R.seq[i, :, :CH] = R.cx[i].astype(F32)
        for s in range(2):
            for b in range(2):
                lo = CH + b * STATES
                R.seq[i, s : s + 1, lo : lo + STATES] = R.cbc[s, i, b : b + 1, :].astype(F32)
    for t in range(STEPS):
        R.seq[3 + t, :, :CH] = R.xin[t].astype(F32)
        for s in range(2):
            for b in range(2):
                lo = CH + b * STATES
                R.seq[3 + t, s : s + 1, lo : lo + STATES] = R.bcin[t, s, b : b + 1, :].astype(F32)
    R.wts[:TAPS, :CH] = R.cw[...]
    for k in range(TAPS):
        for b in range(2):
            lo = CH + b * STATES
            R.wts[k : k + 1, lo : lo + STATES] = R.cwbc[k, b : b + 1, :]


def sec_old(R):
    for t in range(STEPS):
        total = jnp.zeros((2, STATES), F32)
        for k in range(TAPS):
            total += R.wts[k : k + 1, CH + STATES :] * R.seq[t + k, :, CH + STATES :]
        R.acc[2 * t : 2 * t + 2, CH + STATES :] = total
    c_hi, c_lo = split(silu(R.acc[:, CH + STATES :]), 2)
    c_parts = stack([c_hi, c_lo], 0)
    ys = []
    for s in range(2):
        state = R.ssm[s].reshape(CH, STATES)
        hi = state.astype(BF16)
        lo = (state - hi.astype(F32)).astype(BF16)
        both = dot(c_parts, hi, 1, 1)
        ys.append(both[0:ROWS] + both[ROWS:] + dot(c_parts, lo, 1, 1)[0:ROWS])
    row = lax.broadcasted_iota(jnp.int32, (ROWS, CH), 0)
    R.base[...] = jnp.where(row >= 2 * STEPS, 0.0, jnp.where(lax.rem(row, 2) == 0, ys[0], ys[1]))


def sec_unpack(R, packed):
    for k in range(8):
        R.fork[0:3, 128 * k : 128 * (k + 1)] = packed[4 * k : 4 * k + 3]
    for i in range(3):
        for b in range(2):
            r = 4 * (2 * i + b) + 3
            lo = CH + b * STATES
            R.fork[i : i + 1, lo : lo + STATES] = packed[r : r + 1]


def fin_rows(R, lanes):
    first = lax.broadcasted_iota(jnp.int32, (2, lanes), 0) == 0
    return jnp.where(first, R.fin[0], R.fin[1])


def sec_conv(R):
    fin = fin_rows(R, LANES)
    for t in range(STEPS):
        total = jnp.zeros((2, LANES), F32)
        for k in range(TAPS):
            w = R.seq[t + k]
            for f in range(t + 1):
                if t + k - f <= 2:
                    r = t + k - f
                    w = jnp.where(fin == f, R.fork[r : r + 1, :], w)
            total += R.wts[k : k + 1, :] * w
        R.acc[2 * t : 2 * t + 2, :] = total
    R.acc[...] = silu(R.acc[...])


def sec_mix(R):
    fin = fin_rows(R, CH)
    a = jnp.ones((2, CH), F32)
    b = jnp.zeros((2, CH), F32)
    gs = []
    for t in range(STEPS):
        two = slice(2 * t, 2 * t + 2)
        now = fin == t
        d_t = R.dec[two]
        a = jnp.where(now, 0.0, a) * d_t
        b = jnp.where(now, 1.0, b) * d_t
        x_t = R.acc[two, :CH]
        u = R.ex[two] * x_t
        gs = [jnp.where(now, 0.0, v) * d_t for v in gs] + [u]
        c_t = R.acc[two, CH + STATES :]
        total = a * R.base[two] + R.ex[8:9] * x_t
        for k in range(t + 1):
            b_k = R.acc[2 * k : 2 * k + 2, CH : CH + STATES]
            total += gs[k] * jnp.sum(b_k * c_t, axis=1, keepdims=True)
        R.base[two] = total
        R.bco[two] = b
    for k in range(STEPS):
        R.gub[2 * k : 2 * k + 2] = gs[k]
    for t in range(STEPS):
        R.gate[2 * t : 2 * t + 2] = silu(R.zin[t].astype(F32))


def sec_last(R):
    bm = R.acc[:, CH : CH + STATES]
    odd = lax.rem(lax.broadcasted_iota(jnp.int32, (ROWS, STATES), 0), 2)
    both = jnp.concatenate([jnp.where(odd == 0, bm, 0.0), jnp.where(odd == 1, bm, 0.0)], axis=1)
    b_hi, b_lo = split(both, 2)
    g_hi, g_lo = split(R.gub[...], 2)
    rhs = stack([b_hi, b_hi, b_lo, b_lo], 0)
    lhs = stack([g_hi, g_lo, g_hi, g_lo], 0)
    u = dot(lhs, rhs, 0, 0)
    for h in range(HEADS):
        for s in range(2):
            R.ssm[s, h] = (
                R.ab[0, s, h : h + 1, :] * R.ssm[s, h]
                + u[h * WIDTH : (h + 1) * WIDTH, s * STATES : (s + 1) * STATES]
            )


def sec_own_c(R, f):
    rows = [
        jnp.where(R.fin[0] < STEPS, R.bcin[t, 0, 1:2, :].astype(F32), R.bcin[t, 1, 1:2, :].astype(F32))
        for t in range(STEPS)
    ]
    after = [
        jnp.where(f == 0, rows[0], jnp.where(f == 1, rows[1], rows[2])),
        jnp.where(f == 0, rows[1], rows[2]),
        rows[2],
    ]
    for n in range(STEPS):
        total = jnp.zeros((1, STATES), F32)
        for i in range(n + 1):
            total += R.cwbc[i + 3 - n, 1:2, :] * after[i]
        R.esend[n : n + 1] = total


def sec_group_y(R, packed):
    fork_c = [packed[4 * (2 * i + 1) + 3 : 4 * (2 * i + 1) + 4] for i in range(3)]
    zero = jnp.zeros((1, STATES), F32)
    adds = []
    for n in range(STEPS):
        total = zero
        for k in range(3 - n):
            total += R.cwbc[k, 1:2, :] * fork_c[n + k]
        adds.append(total)
    adds = jnp.concatenate(adds + [zero] * 5, axis=0)
    R.epad[:, 0:4, :] = R.ebuf[...]
    cs = silu(R.epad[...] + adds[None]).reshape(2 * NZ * 8, STATES)
    y = dot(stack(split(cs, 2), 0), R.hbuf[...].reshape(HALF * WIDTH, STATES), 1, 1)
    y = (y[: 2 * NZ * 8] + y[2 * NZ * 8 :]).reshape(2 * NZ, 8, HALF * WIDTH)
    for n in range(STEPS):
        for q in range(4):
            R.yrs[:, n, q, :] = y[:, n, 128 * q : 128 * (q + 1)]


def sec_gate(R, f, owner_z):
    rows = []
    for n in range(STEPS):
        rows.append(
            jnp.concatenate(
                [
                    R.yrb[cc, owner_z, n, q : q + 1, :]
                    for cc in range(2)
                    for q in range(4)
                ],
                axis=1,
            )
        )
    at_step = [
        rows[0],
        jnp.where(f == 0, rows[1], rows[0]),
        jnp.where(f == 0, rows[2], jnp.where(f == 1, rows[1], rows[0])),
    ]
    for t in range(STEPS):
        two = slice(2 * t, 2 * t + 2)
        R.base[two] = (R.base[two] + R.bco[two] * at_step[t]) * R.gate[two]
    gated = R.base[...]
    return jnp.sum(gated * gated, axis=1, keepdims=True)


NAMES = (
    "fin_hbm",
    "src_hbm",
    "ssm_hbm",
    "cx_hbm",
    "cbc_hbm",
    "pssm_hbm",
    "pcx_hbm",
    "pcbc_hbm",
    "x_hbm",
    "z_hbm",
    "bc_hbm",
    "dt_hbm",
    "cw_hbm",
    "cwbc_hbm",
    "bias_hbm",
    "alog_hbm",
    "skip_hbm",
    "gain_hbm",
    "out",
    "pre_out",
    "fork_out",
    "ab_out",
    "ssm",
    "cx",
    "cbc",
    "pcx",
    "pcbc",
    "xin",
    "zin",
    "bcin",
    "dtin",
    "cw",
    "cwbc",
    "bias",
    "alog",
    "skip",
    "gain",
    "fin",
    "src",
    "plan_out",
    "plan_in",
    "pbuf",
    "pconv",
    "cpack",
    "csend",
    "cxbuf",
    "czsend",
    "czbuf",
    "sbuf",
    *(f"xb{g}" for g in range(len(STAGES))),
    "zsend",
    "zbuf",
    "fbuf",
    "ysend",
    "ybuf",
    "seq",
    "fork",
    "acc",
    "wts",
    "st",
    "ex",
    "dec",
    "base",
    "bco",
    "gub",
    "gate",
    "ab",
    "esend",
    "ebuf",
    "epad",
    "hbuf",
    "yrs",
    "yrb",
    "in_sem",
    "sc_sem",
    "own_sem",
    "out_sem",
    "plan_s",
    "plan_r",
    "pair_s",
    "pair_r",
    "cx_s",
    "cx_r",
    "cz_s",
    "cz_r",
    "x_s",
    "x_r",
    "z_s",
    "z_r",
    "g_s",
    "g_r",
    "f_s",
    "f_r",
    "zrel",
    "yrel",
    "e_s",
    "e_r",
    "r_s",
    "r_r",
    "y_s",
    "y_r",
)


class Refs:
    pass


def kernel(nx, ny, *refs):
    R = Refs()
    for name, ref in zip(NAMES, refs, strict=True):
        setattr(R, name, ref)
    me = lax.axis_index("dp")
    c = lax.rem(me, 2)
    z = lax.rem(me // 2, NZ)
    x = me // (2 * NZ)
    y = lax.axis_index("tensor")
    xbs = [getattr(R, f"xb{g}") for g in range(len(STAGES))]

    def at(xx, zz, cc):
        return {"dp": (xx * NZ + zz) * 2 + cc}

    def xpeer(d):
        return lax.rem(x + d, nx)

    def zpeer(d):
        return lax.rem(z + d, NZ)

    def ypeer(d):
        return lax.rem(y + d, ny)

    sibling = at(x, z, 1 - c)

    def remote(src, dst, ssem, rsem, dev):
        return pltpu.make_async_remote_copy(
            src_ref=src, dst_ref=dst, send_sem=ssem, recv_sem=rsem, device_id=dev, device_id_type=MESH
        )

    barrier = pltpu.get_barrier_semaphore()
    for d in range(1, nx):
        pl.semaphore_signal(barrier, inc=1, device_id=at(xpeer(d), z, c), device_id_type=MESH)
    scalars = [
        pltpu.make_async_copy(R.fin_hbm, R.fin, R.sc_sem.at[0]),
        pltpu.make_async_copy(R.src_hbm, R.src, R.sc_sem.at[1]),
    ]
    for cp in scalars:
        cp.start()
    for d in (1, 2, NZ - 2, NZ - 1):
        pl.semaphore_signal(barrier, inc=1, device_id=at(x, zpeer(d), c), device_id_type=MESH)
    for d in (1, ny - 1) if ny > 1 else ():
        pl.semaphore_signal(barrier, inc=1, device_id={"tensor": ypeer(d)}, device_id_type=MESH)
    pl.semaphore_signal(barrier, inc=1, device_id=sibling, device_id_type=MESH)

    def tell_z():
        for i, d in enumerate((2, NZ - 2)):
            pl.semaphore_signal(R.zrel.at[i], inc=1, device_id=at(x, zpeer(d), c), device_id_type=MESH)

    def hear_z():
        for i in range(2):
            pl.semaphore_wait(R.zrel.at[i], 1)

    def tell_y(n):
        for i, d in enumerate((1, ny - 1) if ny > 1 else ()):
            pl.semaphore_signal(
                R.yrel.at[n, i], inc=1, device_id={"tensor": ypeer(d)}, device_id_type=MESH
            )

    def hear_y(n):
        for i in range(2 if ny > 1 else 0):
            pl.semaphore_wait(R.yrel.at[n, i], 1)

    mine = pl.ds(pl.multiple_of(c * HALF, HALF), HALF)
    theirs = pl.ds(pl.multiple_of((1 - c) * HALF, HALF), HALF)
    my_slot = pl.ds(pl.multiple_of(c * HELD, HELD), HELD)
    loads = [
        pltpu.make_async_copy(src, dst, R.in_sem.at[i])
        for i, (src, dst) in enumerate(
            (
                (R.pcx_hbm, R.pcx),
                (R.pcbc_hbm, R.pcbc),
                (R.dt_hbm, R.dtin),
                (R.bias_hbm, R.bias),
                (R.alog_hbm, R.alog),
                (R.skip_hbm, R.skip),
                (R.cx_hbm, R.cx),
                (R.cbc_hbm, R.cbc),
                (R.x_hbm, R.xin),
                (R.bc_hbm, R.bcin),
                (R.cw_hbm, R.cw),
                (R.cwbc_hbm, R.cwbc),
                (R.z_hbm, R.zin),
                (R.gain_hbm, R.gain),
                (R.ssm_hbm, R.ssm),
            )
        )
    ]
    own = pltpu.make_async_copy(R.pssm_hbm.at[:, mine], R.pbuf.at[my_slot], R.own_sem)
    for cp in scalars:
        cp.wait()
    prompt = jnp.where(R.fin[0] < STEPS, R.src[0], R.src[1])
    refill = jnp.where(R.fin[0] < STEPS, R.fin[0], R.fin[1])
    R.plan_out[...] = jnp.full(R.plan_out.shape, prompt, jnp.int32)

    pl.semaphore_wait(barrier, 1 + (nx - 1) + 4 + (2 if ny > 1 else 0))

    order = (2, 1, 3) if nx == 4 else tuple(range(1, nx))
    plans = {}
    for d in order:
        plans[d] = remote(
            R.plan_out, R.plan_in.at[d], R.plan_s.at[d], R.plan_r.at[d], at(xpeer(d), z, c)
        )
        plans[d].start()
    tell_z()
    tell_y(0)
    pair = remote(R.pssm_hbm.at[:, theirs], R.pbuf.at[my_slot], R.pair_s.at[0], R.pair_r.at[0], sibling)
    pair.start()
    for cp in [loads[9], loads[11], loads[0], loads[1], own] + loads[2:9] + [loads[10]] + loads[12:]:
        cp.start()
    for ref in (R.wts, R.st, R.acc, R.base, R.bco, R.gub, R.gate, R.esend, R.epad):
        ref[...] = jnp.zeros_like(ref)
    loads[9].wait()
    loads[11].wait()
    sec_own_c(R, refill)
    here = c * NZ + z
    R.ebuf[here] = R.esend[...]

    def group(src, dst, ssem, rsem):
        sends = []
        for d in (4, 3, 5, 2, 6, 1, 7, 0):
            for k in (0, 1) if d else (1,):
                cc = c if k == 0 else 1 - c
                to = cc * NZ + zpeer(d)
                cp = remote(src(to), dst, ssem.at[k, d], rsem.at[k, d], at(x, zpeer(d), cc))
                cp.start()
                sends.append(cp)
        return sends

    loads[0].wait()
    loads[1].wait()
    sec_pack(R)
    R.pconv[my_slot] = R.cpack[...].astype(BF16)
    pair_conv = remote(
        R.pconv.at[my_slot], R.pconv.at[my_slot], R.pair_s.at[1], R.pair_r.at[1], sibling
    )
    pair_conv.start()

    hear_z()
    e_sends = []
    for d in (4, 3, 5, 2, 6, 1, 7):
        cp = remote(R.esend, R.ebuf.at[here], R.e_s.at[d], R.e_r.at[d], at(x, zpeer(d), c))
        cp.start()
        e_sends.append(cp)

    hear_y(0)
    tell_y(1)
    pair.wait_recv()
    pair_conv.wait_recv()
    own.wait()
    for d in order:
        plans[d].wait_recv()

    def wanted(d):
        return lax.rem(R.plan_in[nx - d, 0, 0], 2 * HELD)

    want = {d: wanted(d) for d in order}
    want[0] = lax.rem(prompt, 2 * HELD)
    owner_x = prompt // (2 * HELD * NZ)
    owner_z = lax.rem(prompt // (2 * HELD), NZ)

    conv_sends = []
    for i, d in enumerate(order):
        R.csend[i] = R.pconv[want[d]]
        cp = remote(R.csend.at[i], R.cxbuf.at[x], R.cx_s.at[d], R.cx_r.at[d], at(xpeer(d), z, c))
        cp.start()
        conv_sends.append(cp)
    starts = [sum(len(o) for o in STAGES[:g]) for g in range(len(STAGES))]
    x_sends = []
    for g, offsets in enumerate(STAGES):
        sends = []
        for i, d in enumerate(order):
            for n, o in enumerate(offsets):
                R.sbuf[i, starts[g] + n] = R.pbuf[want[d], zpeer(o)]
            part = R.sbuf.at[i, starts[g] : starts[g] + len(offsets)]
            cp = remote(
                part, xbs[g].at[x], R.x_s.at[g, d], R.x_r.at[g, d], at(xpeer(d), z, c)
            )
            cp.start()
            sends.append(cp)
        x_sends.append(sends)
    R.cxbuf[x] = R.pconv[want[0]]
    for g, offsets in enumerate(STAGES):
        for n, o in enumerate(offsets):
            xbs[g][x, n] = R.pbuf[want[0], zpeer(o)]

    for i in (6, 7, 8, 10):
        loads[i].wait()
    sec_seq(R)
    for i in range(2, 6):
        loads[i].wait()
    sec_dt(R)
    sec_ab(R)

    hear_y(1)
    tell_y(2)
    for cp in conv_sends:
        cp.wait_recv()
    picked = R.cxbuf[owner_x]
    R.czsend[...] = picked
    R.czbuf[z] = picked
    cz_sends = []
    for d in (4, 3, 5, 2, 6, 1, 7):
        cp = remote(R.czsend, R.czbuf.at[z], R.cz_s.at[d], R.cz_r.at[d], at(x, zpeer(d), c))
        cp.start()
        cz_sends.append(cp)
    for cp in e_sends:
        cp.wait_recv()
    swap_c = remote(R.ebuf.at[mine], R.ebuf.at[mine], R.e_s.at[0], R.e_r.at[0], sibling)
    swap_c.start()


    z_sends = {}
    for g, offsets in enumerate(STAGES):
        for cp in x_sends[g]:
            cp.wait_recv()
        for n, o in enumerate(offsets):
            head = xbs[g][owner_x, n]
            R.hbuf[zpeer(o)] = head
            if o == 0:
                R.zbuf[z] = head
            else:
                R.zsend[o] = head
                z_sends[o] = remote(
                    R.zsend.at[o], R.zbuf.at[z], R.z_s.at[o], R.z_r.at[o], at(x, zpeer(o), c)
                )
                z_sends[o].start()

    swap_c.wait_recv()
    sec_group_y(R, picked.astype(F32))
    r_sends = group(lambda to: R.yrs.at[to], R.yrb.at[c, z], R.r_s, R.r_r)
    R.yrb[c, z] = R.yrs[here]
    loads[14].wait()
    sec_old(R)

    for cp in cz_sends:
        cp.wait_recv()
    sec_unpack(R, R.czbuf[owner_z].astype(F32))
    sec_conv(R)

    for o in (4, 3, 5, 2, 6, 1, 7):
        z_sends[o].wait_recv()
    R.fbuf[here] = R.zbuf[owner_z]
    g_sends = {}
    for d in (1, 7, 2, 6, 3, 5, 4):
        g_sends[d] = remote(
            R.fbuf.at[here], R.fbuf.at[here], R.g_s.at[d], R.g_r.at[d], at(x, zpeer(d), c)
        )
        g_sends[d].start()
    for i in (12, 13):
        loads[i].wait()
    sec_mix(R)
    sec_last(R)
    stores = [
        pltpu.make_async_copy(R.ssm, R.pre_out, R.out_sem.at[0]),
        pltpu.make_async_copy(R.ab.at[1], R.ab_out, R.out_sem.at[1]),
    ]
    for cp in stores:
        cp.start()

    for cp in r_sends:
        cp.wait_recv()
    R.ysend[...] = jnp.broadcast_to(sec_gate(R, refill, owner_z), R.ysend.shape)
    hear_y(2)
    R.ybuf[y] = R.ysend[...]
    y_sends = []
    for d in (4, 3, 5, 2, 6, 1, 7) if ny == 8 else range(1, ny):
        cp = remote(R.ysend, R.ybuf.at[y], R.y_s.at[d], R.y_r.at[d], {"tensor": ypeer(d)})
        cp.start()
        y_sends.append(cp)

    for d in NEAR:
        g_sends[d].wait_recv()
    swap = remote(R.fbuf.at[mine], R.fbuf.at[mine], R.f_s, R.f_r, sibling)
    swap.start()
    stores.append(pltpu.make_async_copy(R.fbuf.at[mine], R.fork_out.at[mine], R.out_sem.at[2]))
    stores[-1].start()
    swap.wait_recv()
    stores.append(pltpu.make_async_copy(R.fbuf.at[theirs], R.fork_out.at[theirs], R.out_sem.at[3]))
    stores[-1].start()
    for cp in list(plans.values()) + [pair, pair_conv] + conv_sends + cz_sends + e_sends + r_sends + [swap_c]:
        cp.wait_send()
    for sends in x_sends:
        for cp in sends:
            cp.wait_send()
    for sends in (z_sends, g_sends):
        for cp in sends.values():
            cp.wait_send()
    swap.wait_send()
    for cp in stores:
        cp.wait()

    for cp in y_sends:
        cp.wait_recv()
    total = R.ybuf[0]
    for i in range(1, ny):
        total += R.ybuf[i]
    scale = lax.rsqrt(total[:, 0:1] / TOTAL + 1e-05)
    normed = R.base[...] * scale * R.gain[...]
    for t in range(STEPS):
        R.out[t] = normed[2 * t : 2 * t + 2].astype(BF16)
    for cp in y_sends:
        cp.wait_send()


def put(out_ref, pre_ref, fork_ref, ab_ref, out_hbm, fs_hbm, fs, sem):
    copies = [pltpu.make_async_copy(out_ref, out_hbm, sem.at[0])]
    copies[0].start()
    for i in range(4):
        some = slice(4 * i, 4 * i + 4)
        for h in range(4 * i, 4 * i + 4):
            f = fork_ref[h].astype(F32)
            for s in range(2):
                fs[s, h] = pre_ref[s, h] + ab_ref[s, h : h + 1, :] * f
        cp = pltpu.make_async_copy(fs.at[:, some], fs_hbm.at[:, some], sem.at[1 + i])
        cp.start()
        copies.append(cp)
    for cp in copies:
        cp.wait()


def body(nx, ny, *args):
    args = list(args)
    args[3] = jnp.swapaxes(args[3], 0, 1)
    args[6] = jnp.swapaxes(args[6], 0, 1)
    for i in (14, 15, 16, 17):
        args[i] = args[i].reshape(1, -1)
    dma = pltpu.SemaphoreType.DMA
    vmem = pltpu.VMEM
    in_vmem = [args[i] for i in (2, 3, 4, 6, 7, 8, 9, 10, 11, 12, 13, 14, 15, 16, 17)]
    head = (WIDTH, STATES)
    scratch = [vmem(a.shape, a.dtype) for a in in_vmem]
    scratch += [pltpu.SMEM(a.shape, a.dtype) for a in args[:2]]
    scratch += [
        vmem((8, 128), jnp.int32),
        vmem((nx, 8, 128), jnp.int32),
        vmem((2 * HELD, HALF) + head, BF16),
        vmem((2 * HELD, 32, 128), BF16),
        vmem((HELD, 32, 128), F32),
        vmem((nx, 32, 128), BF16),
        vmem((nx, 32, 128), BF16),
        vmem((32, 128), BF16),
        vmem((NZ, 32, 128), BF16),
        vmem((nx, NZ) + head, BF16),
    ]
    scratch += [vmem((nx, len(o)) + head, BF16) for o in STAGES]
    scratch += [
        vmem((NZ,) + head, BF16),
        vmem((NZ,) + head, BF16),
        vmem((HEADS,) + head, BF16),
        vmem((8, 128), F32),
        vmem((ny, 8, 128), F32),
        vmem((6, 2, LANES), F32),
        vmem((8, LANES), F32),
        vmem((ROWS, LANES), F32),
        vmem((8, LANES), F32),
        vmem((16, 128), F32),
        vmem((16, CH), F32),
        vmem((ROWS, CH), F32),
        vmem((ROWS, CH), F32),
        vmem((ROWS, CH), F32),
        vmem((ROWS, CH), F32),
        vmem((ROWS, CH), F32),
        vmem((2, 2, HEADS, STATES), F32),
        vmem((4, STATES), F32),
        vmem((2 * NZ, 4, STATES), F32),
        vmem((2 * NZ, 8, STATES), F32),
        vmem((HALF,) + head, BF16),
        vmem((2 * NZ, STEPS, 4, 128), F32),
        vmem((2, NZ, STEPS, 4, 128), F32),
        dma((len(in_vmem),)),
        dma((2,)),
        dma,
        dma((4,)),
        dma((nx,)),
        dma((nx,)),
        dma((2,)),
        dma((2,)),
        dma((nx,)),
        dma((nx,)),
        dma((NZ,)),
        dma((NZ,)),
        dma((len(STAGES), nx)),
        dma((len(STAGES), nx)),
        dma((NZ,)),
        dma((NZ,)),
        dma((NZ,)),
        dma((NZ,)),
        dma,
        dma,
        pltpu.SemaphoreType.REGULAR((2,)),
        pltpu.SemaphoreType.REGULAR((3, 2)),
        dma((NZ,)),
        dma((NZ,)),
        dma((2, NZ)),
        dma((2, NZ)),
        dma((ny,)),
        dma((ny,)),
    ]
    args = [pltpu.with_memory_space_constraint(a, pltpu.HBM) for a in args]
    anywhere = pl.BlockSpec(memory_space=pl.ANY)
    slots = args[0].shape[0]
    out, pre, fork, ab = pl.pallas_call(
        functools.partial(kernel, nx, ny),
        out_shape=(
            pltpu.VMEM((STEPS, slots, CH), BF16),
            pltpu.VMEM(args[2].shape, F32),
            pltpu.VMEM((HEADS,) + head, BF16),
            pltpu.VMEM((2, HEADS, STATES), F32),
        ),
        in_specs=[anywhere] * 18,
        out_specs=(pl.BlockSpec(memory_space=pltpu.VMEM), anywhere, anywhere, anywhere),
        scratch_shapes=scratch,
        compiler_params=pltpu.CompilerParams(
            collective_id=0, has_side_effects=True, vmem_limit_bytes=32 * 1024 * 1024
        ),
    )(*args)
    inside = pl.BlockSpec(memory_space=pltpu.VMEM)
    return pl.pallas_call(
        put,
        out_shape=(jax.ShapeDtypeStruct(out.shape, BF16), jax.ShapeDtypeStruct(pre.shape, F32)),
        in_specs=[anywhere, inside, inside, inside],
        out_specs=(anywhere, anywhere),
        scratch_shapes=[vmem(pre.shape, F32), dma((5,))],
        compiler_params=pltpu.CompilerParams(vmem_limit_bytes=16 * 1024 * 1024),
    )(out, pre, fork, ab)


def solution(mesh):
    nx = mesh.shape["dp"] // (2 * NZ)
    ny = mesh.shape["tensor"]
    return jax.shard_map(
        functools.partial(body, nx, ny),
        mesh=mesh,
        in_specs=(
            P("dp"),
            P("dp"),
            P("dp", "tensor", None, None),
            P("dp", None, "tensor"),
            P("dp", None, None, "tensor"),
            P("dp", "tensor", None, None),
            P("dp", None, "tensor"),
            P("dp", None, None, "tensor"),
            P(None, "dp", "tensor"),
            P(None, "dp", "tensor"),
            P(None, "dp", None, "tensor"),
            P(None, "dp", "tensor"),
            P(None, "tensor"),
            P(None, None, "tensor"),
            P("tensor"),
            P("tensor"),
            P("tensor"),
            P("tensor"),
        ),
        out_specs=(P(None, "dp", "tensor"), P("dp", "tensor", None, None)),
        check_vma=False,
    )
```
